128 devices in a mesh: clip: 16 (over y, z_lo, core), tile: 8 (over x, z_hi).
Axes of the slice: x: 4, y: 4, z: 4 (z_hi: 2, z_lo: 2; z = z_hi * 2 + z_lo), core: 2. Of those that a mesh axis runs over, the one named last changes fastest.
Arguments:
- features: bfloat16 [16, 3, 8, 128, 512], P('clip', None, 'tile'), may hold values from -80 to 80
- target: bfloat16 [16, 3, 8, 128, 256], P('clip', None, 'tile'), may hold values from -6 to 6
- gn_gain: float32 [512], replicated, may hold values from 0.5 to 1.5
- attn_query: bfloat16 [512, 512], replicated
- attn_key: bfloat16 [512, 512], replicated
- attn_value: bfloat16 [512, 512], replicated, may hold values from -0.25 to 0.25
- attn_out: bfloat16 [512, 512], replicated, may hold values from -0.25 to 0.25
- conv_weight: bfloat16 [3, 3, 3, 512, 256], replicated, may hold values from -0.0546875 to 0.0546875
- conv_bias: float32 [256], replicated, may hold values from -3 to 3
- percept: bfloat16 [256, 256], replicated, may hold values from -0.375 to 0.375
- lpips_weight: float32 [256], replicated, may hold values from 0.2 to 2
- crop_owner: int32 [16, 64, 1], P('clip'), may hold values from 0 to 7; in each aligned block of 8 rows (0 to 7, 8 to 15, ..., all dimensions but the last counted through in order) at most 2 rows name the same one
- crop_frame: int32 [16, 64], P('clip'), may hold values from 0 to 2
- crop_col: int32 [16, 64], P('clip'), may hold values from 0 to 64
Outputs:
- decoded: bfloat16 [16, 3, 8, 128, 256], P('clip', None, 'tile')
- conv_grad: float32 [3, 3, 3, 512, 256], replicated
- distances: float32 [16, 64], P('clip', 'tile')
The draws below stay inside these ranges and needn't reach their ends.
Inputs may be any that keep to these rules, and one draw needn't show every extreme that they name: `crop_owner`: in each clip the crops form aligned blocks of 8, block b being scored by tile b; in each block no tile owns more than 2 crops, and in some block a tile owns exactly 2.
All inputs are finite; a program needn't handle non-finite values.
Results may differ from the reference program's by a relative error of at most 0.013.
Values may be sent and summed in bfloat16 or wider, within the bound.
A program may use at most 128 MiB of HBM per device.

```python
import math
import jax
import jax.numpy as jnp
import numpy as np
from jax import lax

C = 512
CO = 256
GROUPS = 32
F = 3
ROWS_DEV = 1
WCOL = 128
CROPW = 64
CROP_DEV = 8
CAP = 2
H = 8
CLIPS = 16
NCROP = 64
N_TILE = 8


def shared_direction(key):
    sign_key = jax.random.fold_in(key, 901)
    return jnp.where(jax.random.bernoulli(sign_key, 0.5, (C,)), 1.0, -1.0).astype(jnp.float32)


def projection_weight(key, direction):
    noise = jnp.clip(jax.random.normal(key, (C, C), jnp.float32), -4.0, 4.0) / math.sqrt(C)
    return (noise + 2.0 * direction[:, None] * direction[None, :] / C).astype(jnp.bfloat16)


def draw_attn_query(key, part):
    direction = shared_direction(key)
    key = jax.random.fold_in(key, 23)
    return projection_weight(key, direction)


def draw_attn_key(key, part):
    direction = shared_direction(key)
    key = jax.random.fold_in(key, 29)
    return projection_weight(key, direction)


def draw_features(key, part):
    key = jax.random.fold_in(key, 17)
    base_key, channel_key = jax.random.split(key, 2)
    shape = (CLIPS, F, H, WCOL, C)
    levels = jnp.arange(H, dtype=jnp.float32) / max(H - 1, 1)
    channel_scale = jnp.exp(jax.random.uniform(channel_key, (C,), jnp.float32, math.log(0.5), math.log(2.0)))
    base = jnp.clip(jax.random.normal(base_key, shape, jnp.float32), -6.0, 6.0)
    rising = jnp.exp(math.log(3.0) * levels)
    values = base * rising[None, None, :, None, None] * channel_scale
    return values.astype(jnp.bfloat16)


def plant(result, stream_key, low, largest):
    longest = result.shape.index(max(result.shape))
    spots = []
    for shift in (0, 1):
        where = [jax.random.randint(jax.random.fold_in(stream_key, axis), (), 0, length) for axis, length in enumerate(result.shape)]
        where[longest] = (where[longest] + shift) % result.shape[longest]
        spots.append(tuple(where))
    return result.at[spots[0]].set(low).at[spots[1]].set(largest)


def shard_levels(stream_key, shape, cuts, smallest, largest):
    factor_of, own = 1.0, jax.random.fold_in(stream_key, 6)
    for position, blocks in cuts:
        draws = jnp.exp(jax.random.uniform(jax.random.fold_in(own, position), (blocks,), jnp.float32, smallest / len(cuts), largest / len(cuts)))
        factor_of = factor_of * jnp.repeat(draws, shape[position] // blocks).reshape([-1 if axis == position else 1 for axis in range(len(shape))])
    return factor_of


def shared_out(stream_key, own, number, rows, count, top, bound, skew):
    order = jax.random.permutation(stream_key, count)
    crowded, usual = shares(count, rows * top, bound, skew, True), shares(count, rows * top, bound, skew, False)
    places = jnp.arange(count)

    def named(lengths, turn):
        used = int((lengths > 0).sum())
        fixed = max(1, used // 4)
        shifted = fixed + (places - fixed + turn * (used - fixed)) % max(1, count - fixed)
        return jnp.zeros((count,), jnp.int32).at[order[jnp.where(places < fixed, places, shifted)]].set(jnp.asarray(lengths, jnp.int32))

    lengths = jnp.where(number % 4 == 0, named(crowded, number // 4), named(usual, number - number // 4 - 1))
    mixed = jax.random.permutation(jax.random.fold_in(own, 3), count)
    donor, receiver = mixed[0:count // 2 * 2:2], mixed[1:count // 2 * 2:2]
    margin = jnp.minimum(lengths[donor] - 1, bound - lengths[receiver]) // 2
    margin = jnp.where((donor == order[0]) | (receiver == order[0]) | (lengths[receiver] == 0), 0, jnp.maximum(margin, 0))
    shifted = jax.random.randint(jax.random.fold_in(own, 4), (count // 2,), 0, 1 << 20) % (margin + 1)
    lengths = lengths.at[donor].add(-shifted).at[receiver].add(shifted)
    labels = jnp.searchsorted(jnp.cumsum(lengths), jnp.arange(rows * top), side="right").astype(jnp.int32)
    listing = labels.reshape(top, rows).T
    listing = listing[jax.random.permutation(jax.random.fold_in(own, 1), rows)]
    turn = jax.random.randint(jax.random.fold_in(own, 2), (rows, 1), 0, top)
    return jnp.take_along_axis(listing, (jnp.arange(top)[None, :] + turn) % top, axis=1)


def shares(number_of, total, bound, lean, full):
    loads = [(1 << 20) // math.isqrt(standing ** lean) + 1 for standing in range(1, number_of + 1)]
    largest = bound if full else min(bound, max(-(-total // number_of), total * loads[0] // sum(loads)))
    least = 1 if total - largest >= number_of - 1 else 0
    counts, spare = [largest] + [least] * (number_of - 1), total - largest - least * (number_of - 1)
    while spare > 0:
        candidates = [i for i in range(1, number_of) if counts[i] < largest] or [i for i in range(1, number_of) if counts[i] < bound]
        whole, left = sum([loads[i] for i in candidates]), spare
        for i in candidates:
            addition = min(bound - counts[i], max(1, left * loads[i] // whole), spare)
            counts[i] = counts[i] + addition
            spare = spare - addition
    return np.array(counts)


def centred(own_key, extent, scale, most, pieces=(), kind=jnp.bfloat16):
    level = shard_levels(own_key, extent, pieces, -0.22, 0.18) if pieces else 1.0
    drawn = jax.random.normal(own_key, extent, jnp.float32) * scale * level
    return jnp.minimum(jnp.maximum(drawn, -most), most).astype(kind)


def setup_inputs(seed: int = 0) -> dict:
    key_list = jax.random.split(jax.random.key(seed), 15)
    features = draw_features(jax.random.fold_in(key_list[14], 71), 0)
    target = centred(key_list[1], (CLIPS, F, H, WCOL, CO), 1.0, 6.0, ((0, 16), (2, 8)))
    gn_gain = jnp.clip(1.0 + 0.1 * jax.random.normal(key_list[2], (C,), jnp.float32), 0.5, 1.5)
    attn_query = draw_attn_query(jax.random.fold_in(key_list[14], 71), 0)
    attn_key = draw_attn_key(jax.random.fold_in(key_list[14], 71), 0)
    attn_value = centred(key_list[5], (C, C), C ** -0.5, 0.25)
    attn_out = centred(key_list[6], (C, C), C ** -0.5, 0.25)
    conv_weight = centred(key_list[7], (3, 3, 3, C, CO), (27 * C) ** -0.5, 0.0546875)
    conv_bias = centred(key_list[8], (CO,), 0.5, 3.0, (), jnp.float32)
    percept = centred(key_list[9], (CO, CO), CO ** -0.5, 0.375)
    lpips_weight = jnp.clip(jnp.exp(jax.random.uniform(key_list[10], (CO,), jnp.float32, math.log(0.2), math.log(2.0))), 0.2, 2.0)
    crop_owner_keys = jax.random.split(jax.random.fold_in(key_list[11], 1), CLIPS * NCROP // CROP_DEV)
    crop_owner_turns = jax.random.permutation(jax.random.fold_in(key_list[11], 3), CLIPS * NCROP // CROP_DEV)
    crop_owner = jax.vmap(lambda own, number: shared_out(jax.random.fold_in(key_list[11], 2), own, number, CROP_DEV, N_TILE, 1, CAP, 2))(crop_owner_keys, crop_owner_turns).reshape((CLIPS, NCROP, 1))
    crop_frame = plant(jax.random.randint(key_list[12], (CLIPS, NCROP), 0, F), jax.random.fold_in(key_list[12], 1), 0, F - 1).astype(jnp.int32)
    crop_col = plant(jax.random.randint(key_list[13], (CLIPS, NCROP), 0, WCOL - CROPW + 1), jax.random.fold_in(key_list[13], 1), 0, WCOL - CROPW).astype(jnp.int32)
    return {"features": features, "target": target, "gn_gain": gn_gain, "attn_query": attn_query, "attn_key": attn_key, "attn_value": attn_value, "attn_out": attn_out, "conv_weight": conv_weight, "conv_bias": conv_bias, "percept": percept, "lpips_weight": lpips_weight, "crop_owner": crop_owner, "crop_frame": crop_frame, "crop_col": crop_col}


EPSILON = 1e-06

def normalize(grouped, first, second, total, gain):
    mean = first / total
    spread = second / total - mean * mean
    scaled = (grouped - mean[None, :, None]) * lax.rsqrt(spread + EPSILON)[None, :, None]
    return (scaled.reshape(grouped.shape[0], -1) * gain[None, :]).astype(jnp.bfloat16)

def prepare(field):
    first_frame = field[0:1]
    timed = jnp.concatenate([first_frame, first_frame, field], axis=0)
    return jnp.pad(timed, ((0, 0), (0, 0), (1, 1), (0, 0)))

def conv_forward(padded, conv_weight, frames, rows, cols):
    width = padded.shape[-1]
    total = jnp.zeros((frames * rows * cols, conv_weight.shape[-1]), jnp.float32)
    for offset_t in range(3):
        for offset_y in range(3):
            for offset_x in range(3):
                tap = padded[offset_t:offset_t + frames, offset_y:offset_y + rows, offset_x:offset_x + cols].reshape(-1, width)
                total = total + jnp.dot(tap, conv_weight[offset_t, offset_y, offset_x], preferred_element_type=jnp.float32)
    return total

def conv_backward(padded, grad_rows, frames, rows, cols):
    width = padded.shape[-1]
    parts = []
    for offset_t in range(3):
        for offset_y in range(3):
            for offset_x in range(3):
                tap = padded[offset_t:offset_t + frames, offset_y:offset_y + rows, offset_x:offset_x + cols].reshape(-1, width)
                parts.append(lax.dot_general(tap, grad_rows, (((0,), (0,)), ((), ())), preferred_element_type=jnp.float32))
    return jnp.stack(parts).reshape(3, 3, 3, width, grad_rows.shape[-1])

def perceive(crop, table):
    mapped = jax.nn.gelu(jnp.dot(crop, table, precision=lax.Precision.HIGHEST))
    return mapped * lax.rsqrt(lax.optimization_barrier(jnp.mean(mapped * mapped, axis=-1, keepdims=True)) + EPSILON)

def crop_distance(crop, other, percept, lpips_weight):
    table = percept.astype(jnp.float32)
    gap = perceive(crop, table) - perceive(other, table)
    return jnp.mean(lax.optimization_barrier(jnp.sum(gap * gap * lpips_weight[None, :], axis=-1)))

def crop_eval(crop, other, percept, lpips_weight):
    other_wide = other.astype(jnp.float32)
    value, pull = jax.vjp(lambda moving: crop_distance(moving, other_wide, percept, lpips_weight), crop.astype(jnp.float32))
    return (value, pull(jnp.ones((), jnp.float32))[0])

def reference(features, target, gn_gain, attn_query, attn_key, attn_value, attn_out, conv_weight, conv_bias, percept, lpips_weight, crop_owner, crop_frame, crop_col):
    rows_all = ROWS_DEV * N_TILE
    zero = jnp.zeros((), jnp.int32)

    def one_clip(carry, items):
        feats, goal, owners, frame_list, col_list = items
        inputs = feats.reshape(-1, C)
        grouped = inputs.astype(jnp.float32).reshape(inputs.shape[0], GROUPS, C // GROUPS)
        first = lax.optimization_barrier(jnp.sum(grouped, axis=(0, 2)))
        second = lax.optimization_barrier(jnp.sum(grouped * grouped, axis=(0, 2)))
        total = jnp.float32(inputs.shape[0] * (C // GROUPS))
        normed = normalize(grouped, first, second, total, gn_gain)
        queries = jnp.dot(normed, attn_query, preferred_element_type=jnp.float32).astype(jnp.bfloat16)
        keys = jnp.dot(normed, attn_key, preferred_element_type=jnp.float32).astype(jnp.bfloat16)
        values = jnp.dot(normed, attn_value, preferred_element_type=jnp.float32).astype(jnp.bfloat16)
        scores = lax.dot_general(queries, keys, (((1,), (1,)), ((), ())), preferred_element_type=jnp.float32) / jnp.sqrt(jnp.float32(C))
        peak = lax.optimization_barrier(jnp.max(scores, axis=1, keepdims=True))
        weights = jnp.exp(scores - peak)
        totals = lax.optimization_barrier(jnp.sum(weights, axis=1, keepdims=True))
        mixed = (jnp.dot(weights.astype(jnp.bfloat16), values, preferred_element_type=jnp.float32) / totals).astype(jnp.bfloat16)
        hidden = (inputs.astype(jnp.float32) + jnp.dot(mixed, attn_out, preferred_element_type=jnp.float32)).astype(jnp.bfloat16)
        field = jnp.pad(hidden.reshape(F, rows_all, WCOL, C), ((0, 0), (1, 1), (0, 0), (0, 0)))
        padded = prepare(field)
        decoded = (conv_forward(padded, conv_weight, F, rows_all, WCOL) + conv_bias[None, :]).astype(jnp.bfloat16).reshape(F, rows_all, WCOL, CO)

        def cut(source, owner, frame, col):
            start = (frame.astype(jnp.int32), (owner * ROWS_DEV).astype(jnp.int32), col.astype(jnp.int32), zero)
            return lax.dynamic_slice(source, start, (1, ROWS_DEV, CROPW, CO)).reshape(ROWS_DEV * CROPW, CO)
        made = jax.vmap(lambda owner, frame, col: cut(decoded, owner, frame, col))(owners, frame_list, col_list)
        wanted = jax.vmap(lambda owner, frame, col: cut(goal, owner, frame, col))(owners, frame_list, col_list)
        dists, grads = jax.vmap(lambda crop, other: crop_eval(crop, other, percept, lpips_weight))(made, wanted)
        grads = grads.astype(jnp.bfloat16)

        def add_crop(index, grad_map):
            start = (frame_list[index].astype(jnp.int32), (owners[index] * ROWS_DEV).astype(jnp.int32), col_list[index].astype(jnp.int32), zero)
            current = lax.dynamic_slice(grad_map, start, (1, ROWS_DEV, CROPW, CO))
            update = grads[index].astype(jnp.float32).reshape(1, ROWS_DEV, CROPW, CO)
            return lax.dynamic_update_slice(grad_map, current + update, start)
        grad_map = lax.fori_loop(0, NCROP, add_crop, jnp.zeros((F, rows_all, WCOL, CO), jnp.float32))
        grad_rows = grad_map.astype(jnp.bfloat16).reshape(-1, CO)
        carry = carry + conv_backward(padded, grad_rows, F, rows_all, WCOL)
        return (carry, (decoded, dists))
    start_grad = jnp.zeros((3, 3, 3, C, CO), jnp.float32)
    conv_grad, (decoded, distances) = lax.scan(one_clip, start_grad, (features, target, crop_owner[:, :, 0], crop_frame, crop_col))
    return (decoded, conv_grad, distances)
```

```python
import functools
import math

import jax
import jax.numpy as jnp
from jax import lax
from jax.experimental import pallas as pl
from jax.experimental.pallas import tpu as pltpu
from jax.sharding import PartitionSpec as P

GROUPS = 32
CROPW = 64
EPSILON = 1e-06
F32 = jnp.float32
BF16 = jnp.bfloat16


def dot(a, b):
    return jnp.dot(a, b, preferred_element_type=F32)


def dot_nt(a, b):
    return lax.dot_general(a, b, (((1,), (1,)), ((), ())), preferred_element_type=F32)


def dot_tn(a, b):
    return lax.dot_general(a, b, (((0,), (0,)), ((), ())), preferred_element_type=F32)


def gelu_parts(z):
    k = math.sqrt(2.0 / math.pi)
    t = jnp.tanh(k * (z + 0.044715 * (z * z * z)))
    return 0.5 * z * (1.0 + t), t


def gelu_slope(z, t):
    k = math.sqrt(2.0 / math.pi)
    return 0.5 * (1.0 + t) + 0.5 * z * (1.0 - t * t) * (k * (1.0 + 3.0 * 0.044715 * (z * z)))


def shift_rows(value, step, cols):
    count = value.shape[0]
    place = lax.broadcasted_iota(jnp.int32, (count, 1), 0) % cols
    if step > 0:
        return jnp.where(place == 0, 0.0, pltpu.roll(value, 1, 0))
    return jnp.where(place == cols - 1, 0.0, pltpu.roll(value, count - 1, 0))


def body(
    tiles, frames, cols, gsum_ref,
    mine_ref, feats_ref, gain_ref, wq_ref, wk_ref, wv_ref, wo_ref, bias_ref, percept_ref,
    lpips_ref, target_ref, owner_ref, frame_ref, col_ref, weight_hbm,
    decoded_ref, hidden_t, grad_ref, dist_ref,
    weight, normed, qs, acc, peak, total, hidden, sem,
):
    mine = mine_ref[0]
    cells = frames * cols
    width = feats_ref.shape[-1]
    outputs = bias_ref.shape[-1]
    fetch = pltpu.make_async_copy(weight_hbm, weight, sem)
    fetch.start()

    def add_tile(i, sums):
        x = feats_ref[i].astype(F32)
        return (
            sums[0] + jnp.sum(x, axis=0, keepdims=True),
            sums[1] + jnp.sum(x * x, axis=0, keepdims=True),
        )

    zero_row = jnp.zeros((1, width), F32)
    first, second = lax.fori_loop(0, tiles, add_tile, (zero_row, zero_row))
    sums = jnp.concatenate([first, second, jnp.zeros((6, width), F32)], axis=0)
    grouped = jnp.dot(sums, gsum_ref[...], precision=lax.Precision.HIGHEST, preferred_element_type=F32)
    count = F32(tiles * cells * (width // GROUPS))
    mean = grouped[0:1] / count
    spread = grouped[1:2] / count - mean * mean
    scale = lax.rsqrt(spread + EPSILON)
    gain = gain_ref[...]

    def normalize(i, _):
        x = feats_ref[i].astype(F32)
        normed[i] = (((x - mean) * scale) * gain).astype(BF16)
        return 0

    lax.fori_loop(0, tiles, normalize, 0)

    factor = 1.0 / math.sqrt(width)

    def row_of(b):
        return jnp.clip(mine + b - 1, 0, tiles - 1)

    def make_queries(b, _):
        q = dot(normed[row_of(b)], wq_ref[...]).astype(BF16)
        here = pl.ds(b * cells, cells)
        qs[here, :] = (dot_nt(q, wk_ref[...]) * factor).astype(BF16)
        acc[here, :] = jnp.zeros((cells, width), F32)
        peak[here, :] = jnp.full((cells, 128), -1e30, F32)
        total[here, :] = jnp.zeros((cells, 128), F32)
        return 0

    lax.fori_loop(0, 3, make_queries, 0)

    def attend(step, _):
        i = step // 3
        here = pl.ds((step % 3) * cells, cells)
        keys = normed[i]
        s = dot_nt(qs[here, :], keys)
        old = peak[here, :]
        new = jnp.maximum(old, jnp.max(s, axis=1, keepdims=True))
        p = jnp.exp(s - new[:, 0:1])
        fade = jnp.exp(old - new)
        part = p[:, 0:128]
        for j in range(1, cells // 128):
            part = part + p[:, j * 128 : (j + 1) * 128]
        peak[here, :] = new
        total[here, :] = total[here, :] * fade + part
        acc[here, :] = acc[here, :] * fade[:, 0:1] + dot(p.astype(BF16), keys)
        return 0

    lax.fori_loop(0, tiles * 3, attend, 0)

    def finish(b, _):
        here = pl.ds(b * cells, cells)
        whole = jnp.sum(total[here, :], axis=1, keepdims=True)
        context = (acc[here, :] / whole).astype(BF16)
        mixed = dot(context, wv_ref[...]).astype(BF16)
        row = feats_ref[row_of(b)].astype(F32) + dot(mixed, wo_ref[...])
        inside = (mine + b >= 1) & (mine + b <= tiles)
        row = jnp.where(inside, row, 0.0)
        hidden[b] = row.astype(BF16)
        hidden_t[b] = row.T.astype(BF16)
        return 0

    lax.fori_loop(0, 3, finish, 0)
    fetch.wait()

    sides = []
    for e in range(3):
        def taps(b, sums, e=e):
            h = hidden[b]
            at = lambda a: weight[(a * 3 + b) * 3 + e]
            return (
                sums[0] + dot(h, at(2)),
                sums[1] + dot(h[: 2 * cols], at(1)),
                sums[2] + dot(h[:cols], at(0)),
            )
        a2, a1, a0 = lax.fori_loop(
            0, 3, taps,
            (jnp.zeros((cells, outputs), F32), jnp.zeros((2 * cols, outputs), F32), jnp.zeros((cols, outputs), F32)),
        )
        sides.append(a2 + jnp.concatenate([a1[:cols], a1], axis=0) + jnp.concatenate([a0, a0, a0], axis=0))
    made = shift_rows(sides[0], 1, cols) + sides[1] + shift_rows(sides[2], -1, cols) + bias_ref[...]
    made = made.astype(BF16)
    decoded_ref[...] = made

    table = percept_ref[...]
    lw = lpips_ref[...]
    z = dot(made, table)
    m, t = gelu_parts(z)
    s = lax.rsqrt(jnp.mean(m * m, axis=-1, keepdims=True) + EPSILON)
    zt = dot(target_ref[...], table)
    mt, _ = gelu_parts(zt)
    st = lax.rsqrt(jnp.mean(mt * mt, axis=-1, keepdims=True) + EPSILON)
    gap = m * s - mt * st
    weighted = gap * lw
    apart = jnp.sum(weighted * gap, axis=-1, keepdims=True)
    up = weighted * (2.0 / CROPW)
    dm = up * s - m * (s * s * s) * (jnp.sum(up * m, axis=-1, keepdims=True) / outputs)
    dz = dm * gelu_slope(z, t)
    high = dz.astype(BF16)
    low = (dz - high.astype(F32)).astype(BF16)
    pull = (dot_nt(high, table) + dot_nt(low, table)).astype(BF16).astype(F32)

    place = lax.broadcasted_iota(jnp.int32, (cols, 1), 0)
    col = col_ref[...]
    covers = (place >= col) & (place < col + CROPW) & (owner_ref[...] == mine)
    distance = jnp.zeros((1, col.shape[1]), F32)
    for f in range(frames):
        cover = (covers & (frame_ref[...] == f)).astype(F32)
        rows = slice(f * cols, (f + 1) * cols)
        distance = distance + jnp.sum(cover * apart[rows], axis=0, keepdims=True)
        grad_ref[rows, :] = (pull[rows] * jnp.sum(cover, axis=1, keepdims=True)).astype(BF16)
    dist_ref[...] = jnp.broadcast_to(distance / CROPW, dist_ref.shape)


def chip_place():
    clip = lax.axis_index("clip")
    tile = lax.axis_index("tile")
    return (tile // 2, clip // 4, (tile % 2) * 2 + (clip // 2) % 2), clip % 2


def device_at(place, core):
    x, y, z = place
    return (y * 4 + (z % 2) * 2 + core, x * 2 + z // 2)


def on_axis(place, axis, position):
    moved = list(place)
    moved[axis] = lax.rem(position + 4, 4)
    return tuple(moved)


def grad_sum(
    frames, cols, hidden_t, grad_hbm, dist_ref, out_ref, dist_out,
    own_h, other_h, own_g, other_g, rhs, part, left1, right1, comb, got, red1, got2, got3, quarter,
    dist_row, dist_pair, send, recv, local, swap_send, swap_recv, dist_send, dist_recv,
):
    place, core = chip_place()
    cells = frames * cols
    outputs = grad_hbm.shape[1]
    half = own_h.shape[1]
    quarter_rows = red1.shape[1]
    half_rows = quarter_rows // 2
    piece = quarter_rows // 4
    partner = device_at(place, 1 - core)

    def peer(axis, step):
        return device_at(on_axis(place, axis, place[axis] + step), core)

    barrier = pltpu.get_barrier_semaphore()
    peers = [peer(axis, step) for axis in range(3) for step in (1, 2, 3)] + [partner]
    for other in peers:
        pl.semaphore_signal(barrier, inc=1, device_id=other, device_id_type=pl.DeviceIdType.MESH)
    own1 = pltpu.make_async_copy(hidden_t.at[:, pl.ds(core * half, half)], own_h, local.at[0])
    own2 = pltpu.make_async_copy(grad_hbm, own_g, local.at[1])
    own1.start()
    own2.start()
    pl.semaphore_wait(barrier, len(peers))

    def remote(src, dst, sems, rsems, index, target):
        return pltpu.make_async_remote_copy(
            src_ref=src, dst_ref=dst, send_sem=sems.at[index], recv_sem=rsems.at[index],
            device_id=target, device_id_type=pl.DeviceIdType.MESH,
        )

    swap_h = remote(hidden_t.at[:, pl.ds((1 - core) * half, half)], other_h, swap_send, swap_recv, 0, partner)
    swap_g = remote(grad_hbm, other_g, swap_send, swap_recv, 1, partner)
    swap_g.start()
    swap_h.start()
    row_copies = []
    for step in (1, 2, 3):
        copy = remote(dist_ref, dist_row.at[step - 1], dist_send, dist_recv, step - 1, peer(0, step))
        copy.start()
        row_copies.append(copy)

    own1.wait()
    own2.wait()
    swap_g.wait()
    swap_h.wait()

    def ring_copy(p, kind):
        m = place[p]
        rows = lambda q, h: pl.ds(pl.multiple_of(lax.rem(q + 4, 4) * quarter_rows + h * half_rows, 16), half_rows)
        source, target, step = {
            0: (part.at[p, rows(m + 2, 0)], left1.at[p], 1),
            1: (part.at[p, rows(m + 2, 1)], right1.at[p], 3),
            2: (part.at[p, rows(m + 1, 1)], got.at[p, 0, pl.ds(half_rows, half_rows)], 1),
            3: (part.at[p, rows(m - 1, 0)], got.at[p, 1, pl.ds(0, half_rows)], 3),
            4: (comb.at[p, 0], got.at[p, 0, pl.ds(0, half_rows)], 1),
            5: (comb.at[p, 1], got.at[p, 1, pl.ds(half_rows, half_rows)], 3),
        }[kind]
        return remote(source, target, send, recv, p * 27 + kind, peer(p, step))

    g_own = [own_g[f * cols : (f + 1) * cols].astype(F32) for f in range(frames)]
    g_other = [other_g[f * cols : (f + 1) * cols].astype(F32) for f in range(frames)]
    mixes = (
        lambda g: [g[0] + g[1] + g[2]],
        lambda g: [g[0] + g[1], g[2]],
        lambda g: g,
    )
    ring = [[ring_copy(p, kind) for kind in range(6)] for p in range(3)]
    for p in range(3):
        depth = (p + 1) * cols
        both = jnp.concatenate(mixes[p](g_own) + mixes[p](g_other), axis=0)
        rhs[: 2 * depth] = jnp.concatenate(
            [shift_rows(both, -1, cols), both, shift_rows(both, 1, cols)], axis=1
        ).astype(BF16)

        def write(b, _, p=p, depth=depth):
            lhs = jnp.concatenate([own_h[b, :, :depth], other_h[b, :, :depth]], axis=1)
            for e in range(3):
                base = pl.multiple_of((b * 3 + e) * half, half)
                part[p, pl.ds(base, half), :] = dot(
                    lhs, rhs[: 2 * depth, e * outputs : (e + 1) * outputs]
                ).astype(BF16)
            return 0

        lax.fori_loop(0, 3, write, 0)
        for kind in range(4):
            ring[p][kind].start()

    total = dist_ref[...]
    for copy in row_copies:
        copy.wait()
    by_step = [dist_ref[...]] + [dist_row[i] for i in range(3)]
    total = by_step[0] + by_step[1] + by_step[2] + by_step[3]
    dist_pair[0] = total
    pair = remote(dist_pair.at[0], dist_pair.at[1], dist_send, dist_recv, 3, peer(2, 2))
    pair.start()

    for p in range(3):
        m = place[p]
        for side, kind, arrived, q, h in ((0, 0, left1, m + 1, 0), (1, 1, right1, m - 1, 1)):
            ring[p][kind].wait_recv()
            rows = pl.ds(pl.multiple_of(lax.rem(q + 4, 4) * quarter_rows + h * half_rows, 16), half_rows)
            comb[p, side] = (part[p, rows, :].astype(F32) + arrived[p].astype(F32)).astype(BF16)
            ring[p][4 + side].start()
    pair.wait()
    mine = lax.axis_index("tile")
    count = dist_out.shape[1]
    pick = lax.broadcasted_iota(jnp.int32, (dist_ref.shape[1], count), 0) == (
        mine * count + lax.broadcasted_iota(jnp.int32, (dist_ref.shape[1], count), 1)
    )
    dist_out[...] = jnp.dot(
        dist_pair[0] + dist_pair[1], pick.astype(F32), precision=lax.Precision.HIGHEST, preferred_element_type=F32
    )[0:1]

    second = []
    for p in range(3):
        axis = (p + 1) % 3
        for kind in (2, 3, 4, 5):
            ring[p][kind].wait_recv()
        own = part[p, pl.ds(pl.multiple_of(place[p] * quarter_rows, 16), quarter_rows), :].astype(F32)
        red1[p] = (own + got[p, 0].astype(F32) + got[p, 1].astype(F32)).astype(BF16)
        copies = []
        for step in (1, 2, 3):
            to = lax.rem(place[axis] + step, 4)
            copy = remote(
                red1.at[p, pl.ds(pl.multiple_of(to * piece, 16), piece)], got2.at[p, step - 1],
                send, recv, p * 27 + 5 + step, peer(axis, step),
            )
            copy.start()
            copies.append(copy)
        second.append(copies)

    third = []
    for p in range(3):
        axis = (p + 2) % 3
        here = place[(p + 1) % 3]
        for copy in second[p]:
            copy.wait_recv()
        piece_sum = red1[p, pl.ds(pl.multiple_of(here * piece, 16), piece), :].astype(F32)
        for i in range(3):
            piece_sum = piece_sum + got2[p, i].astype(F32)
        got3[p, place[axis]] = piece_sum.astype(BF16)
        copies = []
        for step in (1, 2, 3):
            slot = got3.at[p, place[axis]]
            copy = remote(slot, slot, send, recv, p * 27 + 8 + step, peer(axis, step))
            copy.start()
            copies.append(copy)
        third.append(copies)

    fourth = []
    for p in range(3):
        axis = (p + 1) % 3
        for copy in third[p]:
            copy.wait_recv()
        whole = got3[p, 0].astype(F32)
        for i in range(1, 4):
            whole = whole + got3[p, i].astype(F32)
        rows = pl.ds(pl.multiple_of(place[axis] * piece, 16), piece)
        quarter[p, rows, :] = whole.astype(BF16)
        copies = []
        for step in (1, 2, 3):
            slot = quarter.at[p, rows]
            copy = remote(slot, slot, send, recv, p * 27 + 11 + step, peer(axis, step))
            copy.start()
            copies.append(copy)
        fourth.append(copies)

    def out_rows(p, q, h, count=1):
        start = pl.multiple_of(lax.rem(q + 4, 4) * quarter_rows + h * half_rows, 16)
        return out_ref.at[core, p, pl.ds(start, half_rows * count)]

    fifth, to_core, stored = [], [], []
    for p in range(3):
        m = place[p]
        for copy in fourth[p]:
            copy.wait_recv()
        copies = {}
        for kind, h, step in ((0, 0, 1), (1, 1, 3), (2, 1, 1), (3, 0, 3)):
            copies[kind] = remote(
                quarter.at[p, pl.ds(h * half_rows, half_rows)], out_rows(p, m, h), send, recv, p * 27 + 15 + kind,
                peer(p, step),
            )
            copies[kind].start()
        fifth.append(copies)
        across = remote(quarter.at[p], out_rows(p, m, 0, 2), send, recv, p * 27 + 21, partner)
        across.start()
        to_core.append(across)
        store = pltpu.make_async_copy(quarter.at[p], out_rows(p, m, 0, 2), local.at[2 + p])
        store.start()
        stored.append(store)
    forward = []
    for p in range(3):
        m = place[p]
        for kind, q, h, step in ((0, m - 1, 0, 1), (1, m + 1, 1, 3)):
            fifth[p][kind].wait_recv()
            rows = out_rows(p, q, h)
            copy = remote(rows, rows, send, recv, p * 27 + 19 + kind, peer(p, step))
            copy.start()
            forward.append(copy)
    for p in range(3):
        m = place[p]
        for kind, q, index in ((2, m - 1, 22), (3, m + 1, 23)):
            fifth[p][kind].wait_recv()
            rows = out_rows(p, q, 0, 2)
            copy = remote(rows, rows, send, recv, p * 27 + index, partner)
            copy.start()
            to_core.append(copy)
    for p in range(3):
        m = place[p]
        for side in range(2):
            forward[p * 2 + side].wait_recv()
            rows = out_rows(p, m + 2, side)
            copy = remote(rows, rows, send, recv, p * 27 + 24 + side, partner)
            copy.start()
            to_core.append(copy)
    for copy in to_core:
        copy.wait()
    for copy in stored:
        copy.wait()
    for p in range(3):
        for kind in range(6):
            ring[p][kind].wait_send()
        for copy in second[p] + third[p] + fourth[p] + [fifth[p][kind] for kind in range(4)]:
            copy.wait_send()
    for copy in forward:
        copy.wait_send()


def on_device(
    features, target, gn_gain, attn_query, attn_key, attn_value, attn_out, conv_weight, conv_bias,
    percept, lpips_weight, crop_owner, crop_frame, crop_col,
):
    tiles = lax.axis_size("tile")
    mine = lax.axis_index("tile").astype(jnp.int32)
    frames, rows_dev, cols, width = features.shape[1:]
    outputs = conv_weight.shape[-1]
    cells = frames * rows_dev * cols
    taps = 27
    group = width // GROUPS
    lane = jnp.arange(width) // group
    gsum = (lane[:, None] == lane[None, :]).astype(F32)
    gathered = lax.all_gather(features.reshape(cells, width), "tile", axis=0)
    vmem = pl.BlockSpec(memory_space=pltpu.VMEM)
    half = width // 2
    part_rows = taps // 3 * half
    quarter_rows = part_rows // 4
    crops = crop_col.shape[1]
    decoded, hidden_t, grad, dist = pl.pallas_call(
        functools.partial(body, tiles, frames, cols),
        in_specs=[vmem, pl.BlockSpec(memory_space=pltpu.SMEM)] + [vmem] * 13 + [pl.BlockSpec(memory_space=pl.ANY)],
        out_specs=[vmem] * 4,
        out_shape=[
            jax.ShapeDtypeStruct((cells, outputs), BF16),
            jax.ShapeDtypeStruct((3, width, cells), BF16),
            jax.ShapeDtypeStruct((cells, outputs), BF16),
            jax.ShapeDtypeStruct((8, crops), F32),
        ],
        scratch_shapes=[
            pltpu.VMEM((taps, width, outputs), BF16),
            pltpu.VMEM((tiles, cells, width), BF16),
            pltpu.VMEM((3 * cells, width), BF16),
            pltpu.VMEM((3 * cells, width), F32),
            pltpu.VMEM((3 * cells, 128), F32),
            pltpu.VMEM((3 * cells, 128), F32),
            pltpu.VMEM((3, cells, width), BF16),
            pltpu.SemaphoreType.DMA,
        ],
        compiler_params=pltpu.CompilerParams(vmem_limit_bytes=60 * 1024 * 1024),
        cost_estimate=pl.CostEstimate(flops=12_000_000_000, bytes_accessed=14_000_000, transcendentals=4_000_000),
        name="decoder_window",
    )(
        gsum, mine.reshape(1), gathered, gn_gain[None, :], attn_query, attn_key, attn_value, attn_out,
        conv_bias[None, :], percept, lpips_weight[None, :], target.reshape(cells, outputs),
        crop_owner.reshape(1, -1), crop_frame, crop_col, conv_weight.reshape(taps, width, outputs),
    )
    hbm = pl.BlockSpec(memory_space=pl.ANY)
    summed, distances = pl.pallas_call(
        functools.partial(grad_sum, frames, cols),
        in_specs=[hbm, hbm, vmem],
        out_specs=[hbm, vmem],
        out_shape=[
            jax.ShapeDtypeStruct((2, 3, part_rows, outputs), BF16),
            jax.ShapeDtypeStruct((1, crops // tiles), F32),
        ],
        scratch_shapes=[
            pltpu.VMEM((3, half, cells), BF16),
            pltpu.VMEM((3, half, cells), BF16),
            pltpu.VMEM((cells, outputs), BF16),
            pltpu.VMEM((cells, outputs), BF16),
            pltpu.VMEM((2 * cells, 3 * outputs), BF16),
            pltpu.VMEM((3, part_rows, outputs), BF16),
            pltpu.VMEM((3, quarter_rows // 2, outputs), BF16),
            pltpu.VMEM((3, quarter_rows // 2, outputs), BF16),
            pltpu.VMEM((3, 2, quarter_rows // 2, outputs), BF16),
            pltpu.VMEM((3, 2, quarter_rows, outputs), BF16),
            pltpu.VMEM((3, quarter_rows, outputs), BF16),
            pltpu.VMEM((3, 3, quarter_rows // 4, outputs), BF16),
            pltpu.VMEM((3, 4, quarter_rows // 4, outputs), BF16),
            pltpu.VMEM((3, quarter_rows, outputs), BF16),
            pltpu.VMEM((3, 8, crops), F32),
            pltpu.VMEM((2, 8, crops), F32),
            pltpu.SemaphoreType.DMA((81,)),
            pltpu.SemaphoreType.DMA((81,)),
            pltpu.SemaphoreType.DMA((5,)),
            pltpu.SemaphoreType.DMA((2,)),
            pltpu.SemaphoreType.DMA((2,)),
            pltpu.SemaphoreType.DMA((4,)),
            pltpu.SemaphoreType.DMA((4,)),
        ],
        compiler_params=pltpu.CompilerParams(
            collective_id=1, has_side_effects=True, vmem_limit_bytes=50 * 1024 * 1024
        ),
        cost_estimate=pl.CostEstimate(flops=3_000_000_000, bytes_accessed=14_000_000, transcendentals=0),
        name="grad_sum",
    )(hidden_t, grad, dist)
    conv_total = summed.reshape(2, taps, half, outputs).transpose(1, 0, 2, 3).astype(F32).reshape(conv_weight.shape)
    return (decoded.reshape(1, frames, rows_dev, cols, outputs), conv_total, distances)


def solution(mesh):
    return jax.shard_map(
        on_device,
        mesh=mesh,
        in_specs=(
            P("clip", None, "tile", None, None),
            P("clip", None, "tile", None, None),
            P(), P(), P(), P(), P(), P(), P(), P(), P(),
            P("clip", None, None),
            P("clip", None),
            P("clip", None),
        ),
        out_specs=(P("clip", None, "tile", None, None), P(), P("clip", "tile")),
        check_vma=False,
    )
```

```python
import functools
import math

import jax
import jax.numpy as jnp
from jax import lax
from jax.experimental import pallas as pl
from jax.experimental.pallas import tpu as pltpu
from jax.sharding import PartitionSpec as P

GROUPS = 32
CROPW = 64
EPSILON = 1e-06
F32 = jnp.float32
BF16 = jnp.bfloat16


def dot(a, b):
    return jnp.dot(a, b, preferred_element_type=F32)


def dot_nt(a, b):
    return lax.dot_general(a, b, (((1,), (1,)), ((), ())), preferred_element_type=F32)


def dot_tn(a, b):
    return lax.dot_general(a, b, (((0,), (0,)), ((), ())), preferred_element_type=F32)


def gelu_parts(z):
    k = math.sqrt(2.0 / math.pi)
    t = jnp.tanh(k * (z + 0.044715 * (z * z * z)))
    return 0.5 * z * (1.0 + t), t


def gelu_slope(z, t):
    k = math.sqrt(2.0 / math.pi)
    return 0.5 * (1.0 + t) + 0.5 * z * (1.0 - t * t) * (k * (1.0 + 3.0 * 0.044715 * (z * z)))


def shift_rows(value, step, cols):
    count = value.shape[0]
    place = lax.broadcasted_iota(jnp.int32, (count, 1), 0) % cols
    if step > 0:
        return jnp.where(place == 0, 0.0, pltpu.roll(value, 1, 0))
    return jnp.where(place == cols - 1, 0.0, pltpu.roll(value, count - 1, 0))


def chip_place():
    clip = lax.axis_index("clip")
    tile = lax.axis_index("tile")
    return (tile // 2, clip // 4, (tile % 2) * 2 + (clip // 2) % 2), clip % 2


def device_at(place, core):
    x, y, z = place
    return (y * 4 + (z % 2) * 2 + core, x * 2 + z // 2)


def on_axis(place, axis, position):
    moved = list(place)
    moved[axis] = lax.rem(position + 4, 4)
    return tuple(moved)


def decoder_window(
    tiles, frames, cols,
    features, target_ref, gain_ref, wq_ref, wk_ref, wv_ref, wo_ref, bias_ref, percept_ref, lpips_ref,
    owner_ref, frame_ref, col_ref, weight_hbm,
    decoded_ref, out_ref, dist_out,
    weight, feats, normed, stats, qs, acc, peak, total, hidden, hidden_t, other_h, own_g, other_g, rhs,
    part, left1, right1, comb, got, red1, got2, got3, quarter, dist_row, dist_pair,
    gather_send, gather_recv, stat_send, stat_recv, swap_send, swap_recv, dist_send, dist_recv, send, recv, local,
):
    place, core = chip_place()
    clip = lax.axis_index("clip")
    mine = lax.axis_index("tile")
    x, side = mine // 2, mine % 2
    cells = frames * cols
    width = feats.shape[-1]
    outputs = bias_ref.shape[-1]
    half = width // 2
    cut = cells // 2

    def tile_at(step, other):
        return lax.rem(x + step + 4, 4) * 2 + (side + other) % 2

    def peer(axis, step):
        return device_at(on_axis(place, axis, place[axis] + step), core)

    def remote(src, dst, sems, rsems, index, target):
        copy = pltpu.make_async_remote_copy(
            src_ref=src, dst_ref=dst, send_sem=sems.at[index], recv_sem=rsems.at[index],
            device_id=target, device_id_type=pl.DeviceIdType.MESH,
        )
        copy.start()
        return copy

    own, left, right, opposite = (tile_at(step, 0) for step in (0, -1, 1, 2))
    partner, left2, right2, opposite2 = (tile_at(step, 1) for step in (0, -1, 1, 2))
    far = jnp.where(side == 0, left2, right2)
    near = jnp.where(side == 0, right2, left2)
    sibling = device_at(place, 1 - core)

    barrier = pltpu.get_barrier_semaphore()
    peers = [(clip, lax.rem(mine + step, tiles)) for step in range(1, tiles)]
    peers += [peer(1, 1), peer(1, 2), peer(1, 3), peer(2, 1), peer(2, 3), sibling]
    for other in peers:
        pl.semaphore_signal(barrier, inc=1, device_id=other, device_id_type=pl.DeviceIdType.MESH)
    load = pltpu.make_async_copy(features, feats.at[own], local.at[0])
    load.start()
    fetch = pltpu.make_async_copy(weight_hbm, weight, local.at[1])
    fetch.start()

    load.wait()
    wide = feats[own].astype(F32)
    stats[own] = jnp.concatenate(
        [jnp.sum(wide, axis=0, keepdims=True), jnp.sum(wide * wide, axis=0, keepdims=True), jnp.zeros((6, width), F32)],
        axis=0,
    )
    pl.semaphore_wait(barrier, len(peers))
    told = [
        remote(stats.at[own], stats.at[own], stat_send, stat_recv, step, peers[step]) for step in range(tiles - 1)
    ]

    def pass_on(index, unit, h, to):
        rows = feats.at[unit, pl.ds(h * cut, cut)]
        return remote(rows, rows, gather_send, gather_recv, index, (clip, to))

    links = {}
    links["z0"] = pass_on(0, own, 0, partner)
    links["l0"] = pass_on(1, own, 0, right)
    links["r1"] = pass_on(2, own, 1, left)
    links["z1"] = pass_on(3, own, 1, partner)
    links["l1"] = pass_on(4, own, 1, right)
    links["r0"] = pass_on(5, own, 0, left)

    lane = lax.broadcasted_iota(jnp.int32, (width, width), 0) // (width // GROUPS)
    same = (lane == lax.broadcasted_iota(jnp.int32, (width, width), 1) // (width // GROUPS)).astype(BF16)
    for copy in told:
        copy.wait_recv()
    sums = stats[0]
    for i in range(1, tiles):
        sums = sums + stats[i]
    pieces, rest = [], sums
    for _ in range(3):
        pieces.append(rest.astype(BF16))
        rest = rest - pieces[-1].astype(F32)
    grouped = dot(pieces[0], same) + dot(pieces[1], same) + dot(pieces[2], same)
    count = F32(tiles * cells * (width // GROUPS))
    mean = grouped[0:1] / count
    spread = grouped[1:2] / count - mean * mean
    scale = lax.rsqrt(spread + EPSILON)
    gain = gain_ref[...]
    factor = math.log2(math.e) / math.sqrt(width)

    def normalize(slot, unit):
        normed[slot * cells : (slot + 1) * cells, :] = (((feats[unit].astype(F32) - mean) * scale) * gain).astype(BF16)

    def make_queries(role, slot):
        q = dot(normed[slot * cells : (slot + 1) * cells, :], wq_ref[...]).astype(BF16)
        qs[role * cells : (role + 1) * cells, :] = (dot_nt(q, wk_ref[...]) * factor).astype(BF16)

    def attend(roles, slots, first):
        here = slice(roles[0] * cells, roles[1] * cells)
        keys = normed[slots[0] * cells : slots[1] * cells, :]
        s = dot_nt(qs[here, :], keys)
        groups = [s[:, j : j + 128] for j in range(0, s.shape[1], 128)]
        top = jnp.max(functools.reduce(jnp.maximum, groups), axis=1, keepdims=True)
        new = jnp.broadcast_to(top, (s.shape[0], 128)) if first else jnp.maximum(peak[here, :], top)
        raised = [jnp.exp2(group - new) for group in groups]
        lanes = functools.reduce(jnp.add, raised)
        out = dot(jnp.concatenate([group.astype(BF16) for group in raised], axis=1), keys)
        if first:
            total[here, :] = lanes
            acc[here, :] = out
        else:
            fade = jnp.exp2(peak[here, :] - new)
            total[here, :] = total[here, :] * fade + lanes
            for j in range(0, width, 128):
                acc[here, j : j + 128] = acc[here, j : j + 128] * fade + out[:, j : j + 128]
        peak[here, :] = new

    normalize(0, own)
    make_queries(0, 0)
    links["l0"].wait_recv()
    links["o0"] = pass_on(6, left, 0, right)
    links["r1"].wait_recv()
    links["o1"] = pass_on(7, right, 1, left)
    links["z0"].wait_recv()
    links["l2"] = pass_on(8, partner, 0, right)
    links["z1"].wait_recv()
    links["r3"] = pass_on(9, partner, 1, left)
    links["l3"] = pass_on(10, partner, 1, right)
    links["r2"] = pass_on(11, partner, 0, left)
    normalize(1, partner)
    make_queries(1, 1)
    links["l1"].wait_recv()
    links["r0"].wait_recv()
    normalize(2, left)
    normalize(3, right)
    attend((0, 2), (0, 4), True)
    links["o0"].wait_recv()
    links["o1"].wait_recv()
    normalize(4, opposite)
    links["l2"].wait_recv()
    links["p0"] = pass_on(12, left2, 0, right)
    links["r3"].wait_recv()
    links["p1"] = pass_on(13, right2, 1, left)
    links["l3"].wait_recv()
    links["r2"].wait_recv()
    normalize(5, far)
    normalize(6, near)
    make_queries(2, 5)
    attend((2, 3), (0, 4), True)
    attend((0, 3), (4, 6), False)
    links["p0"].wait_recv()
    links["p1"].wait_recv()
    normalize(7, opposite2)
    attend((0, 3), (6, 8), False)

    def choose(i, values):
        chosen = values[0]
        for j in range(1, len(values)):
            chosen = jnp.where(i == j, values[j], chosen)
        return chosen

    def finish(role, _):
        here = pl.ds(pl.multiple_of(role * cells, cells), cells)
        unit = choose(role, [own, partner, far])
        b = choose(role, [1, 2 - 2 * side, 2 * side])
        whole = jnp.sum(total[here, :], axis=1, keepdims=True)
        context = (acc[here, :] / whole).astype(BF16)
        mixed = dot(context, wv_ref[...]).astype(BF16)
        row = feats[unit].astype(F32) + dot(mixed, wo_ref[...])
        inside = (mine + b >= 1) & (mine + b <= tiles)
        row = jnp.where(inside, row, 0.0)
        hidden[b] = row.astype(BF16)
        hidden_t[b] = row.T.astype(BF16)
        return 0

    lax.fori_loop(0, 3, finish, 0)
    swap_h = remote(
        hidden_t.at[:, pl.ds(pl.multiple_of((1 - core) * half, half), half)], other_h, swap_send, swap_recv, 0, sibling
    )
    fetch.wait()

    sides = []
    for e in range(3):
        a2, a1, a0 = (
            sum(
                dot(hidden[b, : (a + 1) * cols, :], weight[(a * 3 + b) * 3 + e]) for b in range(3)
            )
            for a in (2, 1, 0)
        )
        sides.append(a2 + jnp.concatenate([a1[:cols], a1], axis=0) + jnp.concatenate([a0, a0, a0], axis=0))
    made = shift_rows(sides[0], 1, cols) + sides[1] + shift_rows(sides[2], -1, cols) + bias_ref[...]
    made = made.astype(BF16)
    decoded_ref[...] = made

    table = percept_ref[...]
    lw = lpips_ref[...]
    z = dot(made, table)
    m, t = gelu_parts(z)
    s = lax.rsqrt(jnp.mean(m * m, axis=-1, keepdims=True) + EPSILON)
    zt = dot(target_ref[...], table)
    mt, _ = gelu_parts(zt)
    st = lax.rsqrt(jnp.mean(mt * mt, axis=-1, keepdims=True) + EPSILON)
    gap = m * s - mt * st
    weighted = gap * lw
    apart = jnp.sum(weighted * gap, axis=-1, keepdims=True)
    up = weighted * (2.0 / CROPW)
    dm = up * s - m * (s * s * s) * (jnp.sum(up * m, axis=-1, keepdims=True) / outputs)
    dz = dm * gelu_slope(z, t)
    high = dz.astype(BF16)
    low = (dz - high.astype(F32)).astype(BF16)
    pull = (dot_nt(high, table) + dot_nt(low, table)).astype(BF16).astype(F32)

    spot = lax.broadcasted_iota(jnp.int32, (cols, 1), 0)
    col = col_ref[...]
    covers = (spot >= col) & (spot < col + CROPW) & (owner_ref[...] == mine)
    distance = jnp.zeros((1, col.shape[1]), F32)
    for f in range(frames):
        cover = (covers & (frame_ref[...] == f)).astype(F32)
        rows = slice(f * cols, (f + 1) * cols)
        distance = distance + jnp.sum(cover * apart[rows], axis=0, keepdims=True)
        own_g[rows, :] = (pull[rows] * jnp.sum(cover, axis=1, keepdims=True)).astype(BF16)
    dist_row[3] = jnp.broadcast_to(distance / CROPW, dist_row.shape[1:])
    swap_g = remote(own_g, other_g, swap_send, swap_recv, 1, sibling)
    row_copies = [
        remote(dist_row.at[3], dist_row.at[step - 1], dist_send, dist_recv, step - 1, peer(0, step)) for step in (1, 2, 3)
    ]
    swap_g.wait_recv()
    swap_h.wait_recv()

    mixes = (
        lambda g: [g[0] + g[1] + g[2]],
        lambda g: [g[0] + g[1], g[2]],
        lambda g: g,
    )
    split = [[ref[f * cols : (f + 1) * cols, :].astype(F32) for f in range(frames)] for ref in (own_g, other_g)]
    for p in range(3):
        both = jnp.concatenate(mixes[p](split[0]) + mixes[p](split[1]), axis=0)
        rhs[p, : both.shape[0], :] = jnp.concatenate(
            [shift_rows(both, -1, cols), both, shift_rows(both, 1, cols)], axis=1
        ).astype(BF16)

    quarter_rows = quarter.shape[1]
    half_rows = quarter_rows // 2
    piece = quarter_rows // 4
    chunk_rows = 4 * quarter_rows
    own_half = pl.ds(pl.multiple_of(core * half, half), half)
    sent = {}

    def chunk_at(b, q, h, count=1):
        return pl.ds(pl.multiple_of(b * chunk_rows + lax.rem(q + 4, 4) * quarter_rows + h * half_rows, 16), half_rows * count)

    def out_rows(p, b, q, h, count=1):
        return out_ref.at[core, p, chunk_at(b, q, h, count)]

    def go(c, kind, src, dst, to):
        sent[c, kind] = remote(src, dst, send, recv, c * 27 + kind, to)

    def make(b):
        for p in range(3):
            c, m, depth = p * 3 + b, place[p], (p + 1) * cols
            lhs = jnp.concatenate([hidden_t[b, own_half, :depth], other_h[b, :, :depth]], axis=1)
            for e in range(3):
                base = b * chunk_rows + e * half
                part[p, base : base + half, :] = dot(
                    lhs, rhs[p, : 2 * depth, e * outputs : (e + 1) * outputs]
                ).astype(BF16)
            go(c, 0, part.at[p, chunk_at(b, m + 2, 0)], left1.at[c], peer(p, 1))
            go(c, 1, part.at[p, chunk_at(b, m + 2, 1)], right1.at[c], peer(p, 3))
            go(c, 2, part.at[p, chunk_at(b, m + 1, 1)], got.at[c, 0, pl.ds(half_rows, half_rows)], peer(p, 1))
            go(c, 3, part.at[p, chunk_at(b, m - 1, 0)], got.at[c, 1, pl.ds(0, half_rows)], peer(p, 3))

    def ring(b):
        for p in range(3):
            c, m = p * 3 + b, place[p]
            for way, arrived, q, step in ((0, left1, m + 1, 1), (1, right1, m - 1, 3)):
                sent[c, way].wait_recv()
                comb[c, way] = (part[p, chunk_at(b, q, way), :].astype(F32) + arrived[c].astype(F32)).astype(BF16)
                go(c, 4 + way, comb.at[c, way], got.at[c, way, pl.ds(way * half_rows, half_rows)], peer(p, step))

    def direct(b):
        for p in range(3):
            c, axis = p * 3 + b, (p + 1) % 3
            for kind in (2, 3, 4, 5):
                sent[c, kind].wait_recv()
            mine_rows = part[p, chunk_at(b, place[p], 0, 2), :].astype(F32)
            red1[c] = (mine_rows + got[c, 0].astype(F32) + got[c, 1].astype(F32)).astype(BF16)
            for step in (1, 2, 3):
                to = lax.rem(place[axis] + step, 4)
                go(c, 5 + step, red1.at[c, pl.ds(pl.multiple_of(to * piece, 16), piece)], got2.at[c, step - 1], peer(axis, step))

    def to_all(b):
        for p in range(3):
            c, axis, here = p * 3 + b, (p + 2) % 3, place[(p + 1) % 3]
            for step in (1, 2, 3):
                sent[c, 5 + step].wait_recv()
            added = red1[c, pl.ds(pl.multiple_of(here * piece, 16), piece), :].astype(F32)
            for i in range(3):
                added = added + got2[c, i].astype(F32)
            got3[c, place[axis]] = added.astype(BF16)
            for step in (1, 2, 3):
                slot = got3.at[c, place[axis]]
                go(c, 8 + step, slot, slot, peer(axis, step))

    def back(b):
        for p in range(3):
            c, axis = p * 3 + b, (p + 1) % 3
            for step in (1, 2, 3):
                sent[c, 8 + step].wait_recv()
            whole = got3[c, 0].astype(F32)
            for i in range(1, 4):
                whole = whole + got3[c, i].astype(F32)
            rows = pl.ds(pl.multiple_of(place[axis] * piece, 16), piece)
            quarter[c, rows, :] = whole.astype(BF16)
            for step in (1, 2, 3):
                slot = quarter.at[c, rows]
                go(c, 11 + step, slot, slot, peer(axis, step))

    stored = []

    def spread_out(b):
        for p in range(3):
            c, m = p * 3 + b, place[p]
            for step in (1, 2, 3):
                sent[c, 11 + step].wait_recv()
            for kind, h, step in ((0, 0, 1), (1, 1, 3), (2, 1, 1), (3, 0, 3)):
                go(c, 15 + kind, quarter.at[c, pl.ds(h * half_rows, half_rows)], out_rows(p, b, m, h), peer(p, step))
            go(c, 21, quarter.at[c], out_rows(p, b, m, 0, 2), sibling)
            store = pltpu.make_async_copy(quarter.at[c], out_rows(p, b, m, 0, 2), local.at[2 + c])
            store.start()
            stored.append(store)

    def forward(b):
        for p in range(3):
            c, m = p * 3 + b, place[p]
            for kind, q, step in ((0, m - 1, 1), (1, m + 1, 3)):
                sent[c, 15 + kind].wait_recv()
                go(c, 19 + kind, out_rows(p, b, q, kind), out_rows(p, b, q, kind), peer(p, step))

    def across(b):
        for p in range(3):
            c, m = p * 3 + b, place[p]
            for kind, q in ((2, m - 1), (3, m + 1)):
                sent[c, 15 + kind].wait_recv()
                go(c, 20 + kind, out_rows(p, b, q, 0, 2), out_rows(p, b, q, 0, 2), sibling)

    def across_last(b):
        for p in range(3):
            c, m = p * 3 + b, place[p]
            for h in range(2):
                sent[c, 19 + h].wait_recv()
                go(c, 24 + h, out_rows(p, b, m + 2, h), out_rows(p, b, m + 2, h), sibling)

    make(0)
    make(1)
    ring(0)
    make(2)

    for copy in row_copies:
        copy.wait_recv()
    dist_pair[0] = dist_row[0] + dist_row[1] + dist_row[2] + dist_row[3]
    pair = remote(dist_pair.at[0], dist_pair.at[1], dist_send, dist_recv, 3, peer(2, 2))

    ring(1)
    direct(0)
    ring(2)
    direct(1)
    to_all(0)
    direct(2)
    back(0)
    to_all(1)
    spread_out(0)
    back(1)
    to_all(2)
    forward(0)
    spread_out(1)
    back(2)
    across(0)
    forward(1)
    spread_out(2)
    across_last(0)
    across(1)
    forward(2)
    across_last(1)
    across(2)
    across_last(2)

    pair.wait()
    crops, scored = dist_pair.shape[2], dist_out.shape[1]
    pick = lax.broadcasted_iota(jnp.int32, (crops, scored), 0) == (
        mine * scored + lax.broadcasted_iota(jnp.int32, (crops, scored), 1)
    )
    dist_out[...] = jnp.dot(
        dist_pair[0] + dist_pair[1], pick.astype(F32), precision=lax.Precision.HIGHEST, preferred_element_type=F32
    )[0:1]
    for (c, kind), copy in sent.items():
        if kind >= 21:
            copy.wait_recv()
        copy.wait_send()
    for copy in stored:
        copy.wait()
    for copy in told + list(links.values()) + row_copies + [swap_g, swap_h]:
        copy.wait_send()


def widen(half_ref, out_ref):
    half = half_ref.shape[2]
    for i in range(half_ref.shape[1]):
        for h in range(2):
            out_ref[i, pl.ds(h * half, half), :] = half_ref[h, i].astype(F32)


def on_device(
    features, target, gn_gain, attn_query, attn_key, attn_value, attn_out, conv_weight, conv_bias,
    percept, lpips_weight, crop_owner, crop_frame, crop_col,
):
    tiles = lax.axis_size("tile")
    frames, rows_dev, cols, width = features.shape[1:]
    outputs = conv_weight.shape[-1]
    cells = frames * rows_dev * cols
    taps = 27
    half = width // 2
    part_rows = taps // 3 * half
    quarter = part_rows // 12
    crops = crop_col.shape[1]
    vmem = pl.BlockSpec(memory_space=pltpu.VMEM)
    hbm = pl.BlockSpec(memory_space=pl.ANY)
    sems = lambda count: pltpu.SemaphoreType.DMA((count,))
    decoded, summed, distances = pl.pallas_call(
        functools.partial(decoder_window, tiles, frames, cols),
        in_specs=[hbm] + [vmem] * 12 + [hbm],
        out_specs=[vmem, hbm, vmem],
        out_shape=[
            jax.ShapeDtypeStruct((cells, outputs), BF16),
            jax.ShapeDtypeStruct((2, 3, part_rows, outputs), BF16),
            jax.ShapeDtypeStruct((1, crops // tiles), F32),
        ],
        scratch_shapes=[
            pltpu.VMEM((taps, width, outputs), BF16),
            pltpu.VMEM((tiles, cells, width), BF16),
            pltpu.VMEM((tiles * cells, width), BF16),
            pltpu.VMEM((tiles, 8, width), F32),
            pltpu.VMEM((3 * cells, width), BF16),
            pltpu.VMEM((3 * cells, width), F32),
            pltpu.VMEM((3 * cells, 128), F32),
            pltpu.VMEM((3 * cells, 128), F32),
            pltpu.VMEM((3, cells, width), BF16),
            pltpu.VMEM((3, width, cells), BF16),
            pltpu.VMEM((3, half, cells), BF16),
            pltpu.VMEM((cells, outputs), BF16),
            pltpu.VMEM((cells, outputs), BF16),
            pltpu.VMEM((3, 2 * cells, 3 * outputs), BF16),
            pltpu.VMEM((3, part_rows, outputs), BF16),
            pltpu.VMEM((9, quarter // 2, outputs), BF16),
            pltpu.VMEM((9, quarter // 2, outputs), BF16),
            pltpu.VMEM((9, 2, quarter // 2, outputs), BF16),
            pltpu.VMEM((9, 2, quarter, outputs), BF16),
            pltpu.VMEM((9, quarter, outputs), BF16),
            pltpu.VMEM((9, 3, quarter // 4, outputs), BF16),
            pltpu.VMEM((9, 4, quarter // 4, outputs), BF16),
            pltpu.VMEM((9, quarter, outputs), BF16),
            pltpu.VMEM((4, 8, crops), F32),
            pltpu.VMEM((2, 8, crops), F32),
            sems(14), sems(14), sems(tiles - 1), sems(tiles - 1), sems(2), sems(2), sems(4), sems(4),
            sems(9 * 27), sems(9 * 27), sems(11),
        ],
        compiler_params=pltpu.CompilerParams(
            collective_id=1, has_side_effects=True, vmem_limit_bytes=60 * 1024 * 1024
        ),
        cost_estimate=pl.CostEstimate(flops=14_000_000_000, bytes_accessed=24_000_000, transcendentals=4_000_000),
        name="decoder_window",
    )(
        features.reshape(cells, width), target.reshape(cells, outputs), gn_gain[None, :],
        attn_query, attn_key, attn_value, attn_out, conv_bias[None, :], percept, lpips_weight[None, :],
        crop_owner.reshape(1, -1), crop_frame, crop_col, conv_weight.reshape(taps, width, outputs),
    )
    conv_total = pl.pallas_call(
        widen,
        grid=(taps // 3,),
        in_specs=[pl.BlockSpec((2, 3, half, outputs), lambda i: (0, i, 0, 0))],
        out_specs=pl.BlockSpec((3, width, outputs), lambda i: (i, 0, 0)),
        out_shape=jax.ShapeDtypeStruct((taps, width, outputs), F32),
        name="widen",
    )(summed.reshape(2, taps, half, outputs)).reshape(conv_weight.shape)
    return (decoded.reshape(1, frames, rows_dev, cols, outputs), conv_total, distances)


def solution(mesh):
    return jax.shard_map(
        on_device,
        mesh=mesh,
        in_specs=(
            P("clip", None, "tile", None, None),
            P("clip", None, "tile", None, None),
            P(), P(), P(), P(), P(), P(), P(), P(), P(),
            P("clip", None, None),
            P("clip", None),
            P("clip", None),
        ),
        out_specs=(P("clip", None, "tile", None, None), P(), P("clip", "tile")),
        check_vma=False,
    )
```

```python
import functools
import math

import jax
import jax.numpy as jnp
from jax import lax
from jax.experimental import pallas as pl
from jax.experimental.pallas import tpu as pltpu
from jax.sharding import PartitionSpec as P

GROUPS = 32
CROPW = 64
EPSILON = 1e-06
F32 = jnp.float32
BF16 = jnp.bfloat16


def dot(a, b):
    return jnp.dot(a, b, preferred_element_type=F32)


def dot_nt(a, b):
    return lax.dot_general(a, b, (((1,), (1,)), ((), ())), preferred_element_type=F32)


def dot_tn(a, b):
    return lax.dot_general(a, b, (((0,), (0,)), ((), ())), preferred_element_type=F32)


def gelu_parts(z):
    k = math.sqrt(2.0 / math.pi)
    t = jnp.tanh(k * (z + 0.044715 * (z * z * z)))
    return 0.5 * z * (1.0 + t), t


def gelu_slope(z, t):
    k = math.sqrt(2.0 / math.pi)
    return 0.5 * (1.0 + t) + 0.5 * z * (1.0 - t * t) * (k * (1.0 + 3.0 * 0.044715 * (z * z)))


def shift_rows(value, step, cols):
    count = value.shape[0]
    place = lax.broadcasted_iota(jnp.int32, (count, 1), 0) % cols
    if step > 0:
        return jnp.where(place == 0, 0.0, pltpu.roll(value, 1, 0))
    return jnp.where(place == cols - 1, 0.0, pltpu.roll(value, count - 1, 0))


def chip_place():
    clip = lax.axis_index("clip")
    tile = lax.axis_index("tile")
    return (tile // 2, clip // 4, (tile % 2) * 2 + (clip // 2) % 2), clip % 2


def device_at(place, core):
    x, y, z = place
    return (y * 4 + (z % 2) * 2 + core, x * 2 + z // 2)


def on_axis(place, axis, position):
    moved = list(place)
    moved[axis] = lax.rem(position + 4, 4)
    return tuple(moved)


def decoder_window(
    tiles, frames, cols,
    features, target_ref, gain_ref, wq_ref, wk_ref, wv_ref, wo_ref, bias_ref, percept_ref, lpips_ref,
    owner_ref, frame_ref, col_ref, weight_hbm,
    decoded_ref, out_ref, dist_out,
    weight, feats, normed, stats, qs, acc, peak, total, hidden, hidden_t, other_h, own_g, other_g, rhs,
    part, left1, right1, comb, got, red1, got2, got3, quarter, dist_row, dist_pair,
    once, gather_recv, recv, local,
):
    place, core = chip_place()
    clip = lax.axis_index("clip")
    mine = lax.axis_index("tile")
    x, side = mine // 2, mine % 2
    cells = frames * cols
    width = feats.shape[-1]
    outputs = bias_ref.shape[-1]
    half = width // 2
    cut = cells // 2

    def tile_at(step, other):
        return lax.rem(x + step + 4, 4) * 2 + (side + other) % 2

    def peer(axis, step):
        return device_at(on_axis(place, axis, place[axis] + step), core)

    def remote(src, dst, sent_sem, got_sem, target):
        copy = pltpu.make_async_remote_copy(
            src_ref=src, dst_ref=dst, send_sem=sent_sem, recv_sem=got_sem,
            device_id=target, device_id_type=pl.DeviceIdType.MESH,
        )
        copy.start()
        return copy

    def take(rows, sem):
        pltpu.make_async_copy(rows, rows, sem).wait()

    own, left, right, opposite = (tile_at(step, 0) for step in (0, -1, 1, 2))
    partner, left2, right2, opposite2 = (tile_at(step, 1) for step in (0, -1, 1, 2))
    far = jnp.where(side == 0, left2, right2)
    near = jnp.where(side == 0, right2, left2)
    sibling = device_at(place, 1 - core)

    barrier = pltpu.get_barrier_semaphore()
    peers = [(clip, lax.rem(mine + step, tiles)) for step in range(1, tiles)]
    peers += [peer(1, 1), peer(1, 2), peer(1, 3), peer(2, 1), peer(2, 3), sibling]
    for other in peers:
        pl.semaphore_signal(barrier, inc=1, device_id=other, device_id_type=pl.DeviceIdType.MESH)
    load = pltpu.make_async_copy(features, feats.at[own], local.at[0])
    load.start()
    fetch = pltpu.make_async_copy(weight_hbm, weight, local.at[1])
    fetch.start()

    load.wait()
    wide = feats[own].astype(F32)
    stats[own] = jnp.concatenate(
        [jnp.sum(wide, axis=0, keepdims=True), jnp.sum(wide * wide, axis=0, keepdims=True), jnp.zeros((6, width), F32)],
        axis=0,
    )
    pl.semaphore_wait(barrier, len(peers))
    for step in range(tiles - 1):
        remote(stats.at[own], stats.at[own], once.at[0], once.at[1], peers[step])

    def pass_on(index, unit, h, to):
        rows = feats.at[unit, pl.ds(h * cut, cut)]
        return remote(rows, rows, once.at[2], gather_recv.at[index], (clip, to))

    links = {}
    links["z0"] = pass_on(0, own, 0, partner)
    links["l0"] = pass_on(1, own, 0, right)
    links["r1"] = pass_on(2, own, 1, left)
    links["z1"] = pass_on(3, own, 1, partner)
    links["l1"] = pass_on(4, own, 1, right)
    links["r0"] = pass_on(5, own, 0, left)

    lane = lax.broadcasted_iota(jnp.int32, (width, width), 0) // (width // GROUPS)
    same = (lane == lax.broadcasted_iota(jnp.int32, (width, width), 1) // (width // GROUPS)).astype(BF16)
    take(stats.at[pl.ds(0, tiles - 1)], once.at[1])
    sums = stats[0]
    for i in range(1, tiles):
        sums = sums + stats[i]
    pieces, rest = [], sums
    for _ in range(3):
        pieces.append(rest.astype(BF16))
        rest = rest - pieces[-1].astype(F32)
    grouped = dot(pieces[0], same) + dot(pieces[1], same) + dot(pieces[2], same)
    count = F32(tiles * cells * (width // GROUPS))
    mean = grouped[0:1] / count
    spread = grouped[1:2] / count - mean * mean
    scale = lax.rsqrt(spread + EPSILON)
    gain = gain_ref[...]
    factor = math.log2(math.e) / math.sqrt(width)

    def normalize(slot, unit):
        normed[slot * cells : (slot + 1) * cells, :] = (((feats[unit].astype(F32) - mean) * scale) * gain).astype(BF16)

    def make_queries(role, slot):
        q = dot(normed[slot * cells : (slot + 1) * cells, :], wq_ref[...]).astype(BF16)
        qs[role * cells : (role + 1) * cells, :] = (dot_nt(q, wk_ref[...]) * factor).astype(BF16)

    def attend(roles, slots, first):
        here = slice(roles[0] * cells, roles[1] * cells)
        keys = normed[slots[0] * cells : slots[1] * cells, :]
        s = dot_nt(qs[here, :], keys)
        groups = [s[:, j : j + 128] for j in range(0, s.shape[1], 128)]
        top = jnp.max(functools.reduce(jnp.maximum, groups), axis=1, keepdims=True)
        new = jnp.broadcast_to(top, (s.shape[0], 128)) if first else jnp.maximum(peak[here, :], top)
        raised = [jnp.exp2(group - new) for group in groups]
        lanes = functools.reduce(jnp.add, raised)
        out = dot(jnp.concatenate([group.astype(BF16) for group in raised], axis=1), keys)
        if first:
            total[here, :] = lanes
            acc[here, :] = out
        else:
            fade = jnp.exp2(peak[here, :] - new)
            total[here, :] = total[here, :] * fade + lanes
            for j in range(0, width, 128):
                acc[here, j : j + 128] = acc[here, j : j + 128] * fade + out[:, j : j + 128]
        peak[here, :] = new

    normalize(0, own)
    make_queries(0, 0)
    links["l0"].wait_recv()
    links["o0"] = pass_on(6, left, 0, right)
    links["r1"].wait_recv()
    links["o1"] = pass_on(7, right, 1, left)
    links["z0"].wait_recv()
    links["l2"] = pass_on(8, partner, 0, right)
    links["z1"].wait_recv()
    links["r3"] = pass_on(9, partner, 1, left)
    links["l3"] = pass_on(10, partner, 1, right)
    links["r2"] = pass_on(11, partner, 0, left)
    normalize(1, partner)
    make_queries(1, 1)
    links["l1"].wait_recv()
    links["r0"].wait_recv()
    normalize(2, left)
    normalize(3, right)
    attend((0, 2), (0, 4), True)
    links["o0"].wait_recv()
    links["o1"].wait_recv()
    normalize(4, opposite)
    attend((0, 2), (4, 5), False)
    links["l2"].wait_recv()
    links["p0"] = pass_on(12, left2, 0, right)
    links["r3"].wait_recv()
    links["p1"] = pass_on(13, right2, 1, left)
    links["l3"].wait_recv()
    links["r2"].wait_recv()
    normalize(5, far)
    normalize(6, near)
    make_queries(2, 5)
    attend((2, 3), (0, 5), True)
    attend((0, 3), (5, 7), False)
    links["p0"].wait_recv()
    links["p1"].wait_recv()
    normalize(7, opposite2)
    attend((0, 3), (7, 8), False)

    def choose(i, values):
        chosen = values[0]
        for j in range(1, len(values)):
            chosen = jnp.where(i == j, values[j], chosen)
        return chosen

    def finish(role, _):
        here = pl.ds(pl.multiple_of(role * cells, cells), cells)
        unit = choose(role, [own, partner, far])
        b = choose(role, [1, 2 - 2 * side, 2 * side])
        whole = jnp.sum(total[here, :], axis=1, keepdims=True)
        context = (acc[here, :] / whole).astype(BF16)
        mixed = dot(context, wv_ref[...]).astype(BF16)
        row = feats[unit].astype(F32) + dot(mixed, wo_ref[...])
        inside = (mine + b >= 1) & (mine + b <= tiles)
        row = jnp.where(inside, row, 0.0)
        hidden[b] = row.astype(BF16)
        hidden_t[b] = row.T.astype(BF16)
        return 0

    lax.fori_loop(0, 3, finish, 0)
    swap_h = remote(
        hidden_t.at[:, pl.ds(pl.multiple_of((1 - core) * half, half), half)], other_h, once.at[3], once.at[4], sibling
    )
    fetch.wait()

    sides = []
    for e in range(3):
        a2, a1, a0 = (
            sum(
                dot(hidden[b, : (a + 1) * cols, :], weight[(a * 3 + b) * 3 + e]) for b in range(3)
            )
            for a in (2, 1, 0)
        )
        sides.append(a2 + jnp.concatenate([a1[:cols], a1], axis=0) + jnp.concatenate([a0, a0, a0], axis=0))
    made = shift_rows(sides[0], 1, cols) + sides[1] + shift_rows(sides[2], -1, cols) + bias_ref[...]
    made = made.astype(BF16)
    decoded_ref[...] = made

    table = percept_ref[...]
    lw = lpips_ref[...]
    z = dot(made, table)
    m, t = gelu_parts(z)
    s = lax.rsqrt(jnp.mean(m * m, axis=-1, keepdims=True) + EPSILON)
    zt = dot(target_ref[...], table)
    mt, _ = gelu_parts(zt)
    st = lax.rsqrt(jnp.mean(mt * mt, axis=-1, keepdims=True) + EPSILON)
    gap = m * s - mt * st
    weighted = gap * lw
    apart = jnp.sum(weighted * gap, axis=-1, keepdims=True)
    up = weighted * (2.0 / CROPW)
    dm = up * s - m * (s * s * s) * (jnp.sum(up * m, axis=-1, keepdims=True) / outputs)
    dz = dm * gelu_slope(z, t)
    high = dz.astype(BF16)
    low = (dz - high.astype(F32)).astype(BF16)
    pull = (dot_nt(high, table) + dot_nt(low, table)).astype(BF16).astype(F32)

    spot = lax.broadcasted_iota(jnp.int32, (cols, 1), 0)
    col = col_ref[...]
    covers = (spot >= col) & (spot < col + CROPW) & (owner_ref[...] == mine)
    distance = jnp.zeros((1, col.shape[1]), F32)
    for f in range(frames):
        cover = (covers & (frame_ref[...] == f)).astype(F32)
        rows = slice(f * cols, (f + 1) * cols)
        distance = distance + jnp.sum(cover * apart[rows], axis=0, keepdims=True)
        own_g[rows, :] = (pull[rows] * jnp.sum(cover, axis=1, keepdims=True)).astype(BF16)
    dist_row[3] = jnp.broadcast_to(distance / CROPW, dist_row.shape[1:])
    swap_g = remote(own_g, other_g, once.at[5], once.at[6], sibling)
    for step in (1, 2, 3):
        remote(dist_row.at[3], dist_row.at[step - 1], once.at[7], once.at[8], peer(0, step))

    mixes = (
        lambda g: [g[0] + g[1] + g[2]],
        lambda g: [g[0] + g[1], g[2]],
        lambda g: g,
    )

    def line_up(ref, place_in):
        g = [ref[f * cols : (f + 1) * cols, :].astype(F32) for f in range(frames)]
        for p in range(3):
            mixed = jnp.concatenate(mixes[p](g), axis=0)
            depth = mixed.shape[0]
            for e, moved in enumerate((shift_rows(mixed, -1, cols), mixed, shift_rows(mixed, 1, cols))):
                rhs[p, place_in * depth : (place_in + 1) * depth, e * outputs : (e + 1) * outputs] = moved.astype(BF16)

    line_up(own_g, 0)
    swap_g.wait_recv()
    line_up(other_g, 1)
    swap_h.wait_recv()

    quarter_rows = quarter.shape[1]
    half_rows = quarter_rows // 2
    piece = quarter_rows // 4
    chunk_rows = 4 * quarter_rows
    own_half = pl.ds(pl.multiple_of(core * half, half), half)

    def chunk_at(b, q, h, count=1):
        return pl.ds(pl.multiple_of(b * chunk_rows + lax.rem(q + 4, 4) * quarter_rows + h * half_rows, 16), half_rows * count)

    def out_rows(p, b, q, h, count=1):
        return out_ref.at[core, p, chunk_at(b, q, h, count)]

    def go(c, stage, src, dst, to):
        remote(src, dst, once.at[9 if stage < 5 else 10], recv.at[c, stage], to)

    def across_to(src, dst):
        remote(src, dst, once.at[10], once.at[11], sibling)

    def make(b):
        for p in range(3):
            c, m, depth = p * 3 + b, place[p], (p + 1) * cols
            lhs = jnp.concatenate([hidden_t[b, own_half, :depth], other_h[b, :, :depth]], axis=1)
            for e in range(3):
                base = b * chunk_rows + e * half
                part[p, base : base + half, :] = dot(
                    lhs, rhs[p, : 2 * depth, e * outputs : (e + 1) * outputs]
                ).astype(BF16)
            go(c, 0, part.at[p, chunk_at(b, m + 2, 0)], left1.at[c], peer(p, 1))
            go(c, 0, part.at[p, chunk_at(b, m + 2, 1)], right1.at[c], peer(p, 3))
            go(c, 1, part.at[p, chunk_at(b, m + 1, 1)], got.at[c, 0, pl.ds(half_rows, half_rows)], peer(p, 1))
            go(c, 1, part.at[p, chunk_at(b, m - 1, 0)], got.at[c, 1, pl.ds(0, half_rows)], peer(p, 3))

    def ring(b):
        for p in range(3):
            c, m = p * 3 + b, place[p]
            take(comb.at[c], recv.at[c, 0])
            for way, arrived, q, step in ((0, left1, m + 1, 1), (1, right1, m - 1, 3)):
                comb[c, way] = (part[p, chunk_at(b, q, way), :].astype(F32) + arrived[c].astype(F32)).astype(BF16)
                go(c, 1, comb.at[c, way], got.at[c, way, pl.ds(way * half_rows, half_rows)], peer(p, step))

    def direct(b):
        for p in range(3):
            c, axis = p * 3 + b, (p + 1) % 3
            take(got.at[c], recv.at[c, 1])
            mine_rows = part[p, chunk_at(b, place[p], 0, 2), :].astype(F32)
            red1[c] = (mine_rows + got[c, 0].astype(F32) + got[c, 1].astype(F32)).astype(BF16)
            for step in (1, 2, 3):
                to = lax.rem(place[axis] + step, 4)
                go(c, 2, red1.at[c, pl.ds(pl.multiple_of(to * piece, 16), piece)], got2.at[c, step - 1], peer(axis, step))

    def to_all(b):
        for p in range(3):
            c, axis, here = p * 3 + b, (p + 2) % 3, place[(p + 1) % 3]
            take(got2.at[c], recv.at[c, 2])
            added = red1[c, pl.ds(pl.multiple_of(here * piece, 16), piece), :].astype(F32)
            for i in range(3):
                added = added + got2[c, i].astype(F32)
            got3[c, place[axis]] = added.astype(BF16)
            for step in (1, 2, 3):
                slot = got3.at[c, place[axis]]
                go(c, 3, slot, slot, peer(axis, step))

    def back(b):
        for p in range(3):
            c, axis = p * 3 + b, (p + 1) % 3
            take(got2.at[c], recv.at[c, 3])
            whole = got3[c, 0].astype(F32)
            for i in range(1, 4):
                whole = whole + got3[c, i].astype(F32)
            rows = pl.ds(pl.multiple_of(place[axis] * piece, 16), piece)
            quarter[c, rows, :] = whole.astype(BF16)
            for step in (1, 2, 3):
                slot = quarter.at[c, rows]
                go(c, 4, slot, slot, peer(axis, step))

    def spread_out(b):
        for p in range(3):
            c, m = p * 3 + b, place[p]
            take(got2.at[c], recv.at[c, 4])
            for stage, h, step in ((5, 0, 1), (5, 1, 3), (6, 1, 1), (6, 0, 3)):
                go(c, stage, quarter.at[c, pl.ds(h * half_rows, half_rows)], out_rows(p, b, m, h), peer(p, step))
            across_to(quarter.at[c], out_rows(p, b, m, 0, 2))
            pltpu.make_async_copy(quarter.at[c], out_rows(p, b, m, 0, 2), local.at[2]).start()

    def forward(b):
        for p in range(3):
            c, m = p * 3 + b, place[p]
            take(quarter.at[c], recv.at[c, 5])
            for h, q, step in ((0, m - 1, 1), (1, m + 1, 3)):
                go(c, 7, out_rows(p, b, q, h), out_rows(p, b, q, h), peer(p, step))

    def across(b):
        for p in range(3):
            c, m = p * 3 + b, place[p]
            take(quarter.at[c], recv.at[c, 6])
            for q in (m - 1, m + 1):
                across_to(out_rows(p, b, q, 0, 2), out_rows(p, b, q, 0, 2))

    def across_last(b):
        for p in range(3):
            c, m = p * 3 + b, place[p]
            take(quarter.at[c], recv.at[c, 7])
            across_to(out_rows(p, b, m + 2, 0, 2), out_rows(p, b, m + 2, 0, 2))

    make(0)
    make(1)
    ring(0)
    make(2)
    ring(1)

    take(dist_row.at[pl.ds(0, 3)], once.at[8])
    dist_pair[0] = dist_row[0] + dist_row[1] + dist_row[2] + dist_row[3]
    pair = remote(dist_pair.at[0], dist_pair.at[1], once.at[12], once.at[13], peer(2, 2))

    ring(2)
    for stage in (direct, to_all, back, spread_out, forward, across, across_last):
        for b in range(3):
            stage(b)

    pair.wait()
    crops, scored = dist_pair.shape[2], dist_out.shape[1]
    pick = lax.broadcasted_iota(jnp.int32, (crops, scored), 0) == (
        mine * scored + lax.broadcasted_iota(jnp.int32, (crops, scored), 1)
    )
    dist_out[...] = jnp.dot(
        dist_pair[0] + dist_pair[1], pick.astype(F32), precision=lax.Precision.HIGHEST, preferred_element_type=F32
    )[0:1]
    take(out_ref.at[1 - core], once.at[11])
    take(quarter, local.at[2])
    take(stats.at[pl.ds(0, tiles - 1)], once.at[0])
    take(feats.at[pl.ds(0, 7)], once.at[2])
    take(dist_row.at[pl.ds(0, 3)], once.at[7])
    take(weight.at[:, pl.ds(0, 9 * 21 * half_rows // 54)], once.at[9])
    take(weight.at[:, pl.ds(0, 9 * 14 * half_rows // 27)], once.at[10])
    swap_g.wait_send()
    swap_h.wait_send()


def widen(half_ref, out_ref):
    half = half_ref.shape[2]
    for i in range(half_ref.shape[1]):
        for h in range(2):
            out_ref[i, pl.ds(h * half, half), :] = half_ref[h, i].astype(F32)


def on_device(
    features, target, gn_gain, attn_query, attn_key, attn_value, attn_out, conv_weight, conv_bias,
    percept, lpips_weight, crop_owner, crop_frame, crop_col,
):
    tiles = lax.axis_size("tile")
    frames, rows_dev, cols, width = features.shape[1:]
    outputs = conv_weight.shape[-1]
    cells = frames * rows_dev * cols
    taps = 27
    half = width // 2
    part_rows = taps // 3 * half
    quarter = part_rows // 12
    crops = crop_col.shape[1]
    vmem = pl.BlockSpec(memory_space=pltpu.VMEM)
    hbm = pl.BlockSpec(memory_space=pl.ANY)
    sems = lambda count: pltpu.SemaphoreType.DMA((count,))
    decoded, summed, distances = pl.pallas_call(
        functools.partial(decoder_window, tiles, frames, cols),
        in_specs=[hbm] + [vmem] * 12 + [hbm],
        out_specs=[vmem, hbm, vmem],
        out_shape=[
            jax.ShapeDtypeStruct((cells, outputs), BF16),
            jax.ShapeDtypeStruct((2, 3, part_rows, outputs), BF16),
            jax.ShapeDtypeStruct((1, crops // tiles), F32),
        ],
        scratch_shapes=[
            pltpu.VMEM((taps, width, outputs), BF16),
            pltpu.VMEM((tiles, cells, width), BF16),
            pltpu.VMEM((tiles * cells, width), BF16),
            pltpu.VMEM((tiles, 8, width), F32),
            pltpu.VMEM((3 * cells, width), BF16),
            pltpu.VMEM((3 * cells, width), F32),
            pltpu.VMEM((3 * cells, 128), F32),
            pltpu.VMEM((3 * cells, 128), F32),
            pltpu.VMEM((3, cells, width), BF16),
            pltpu.VMEM((3, width, cells), BF16),
            pltpu.VMEM((3, half, cells), BF16),
            pltpu.VMEM((cells, outputs), BF16),
            pltpu.VMEM((cells, outputs), BF16),
            pltpu.VMEM((3, 2 * cells, 3 * outputs), BF16),
            pltpu.VMEM((3, part_rows, outputs), BF16),
            pltpu.VMEM((9, quarter // 2, outputs), BF16),
            pltpu.VMEM((9, quarter // 2, outputs), BF16),
            pltpu.VMEM((9, 2, quarter // 2, outputs), BF16),
            pltpu.VMEM((9, 2, quarter, outputs), BF16),
            pltpu.VMEM((9, quarter, outputs), BF16),
            pltpu.VMEM((9, 3, quarter // 4, outputs), BF16),
            pltpu.VMEM((9, 4, quarter // 4, outputs), BF16),
            pltpu.VMEM((9, quarter, outputs), BF16),
            pltpu.VMEM((4, 8, crops), F32),
            pltpu.VMEM((2, 8, crops), F32),
            sems(14), sems(14), pltpu.SemaphoreType.DMA((9, 8)), sems(3),
        ],
        compiler_params=pltpu.CompilerParams(
            collective_id=1, has_side_effects=True, vmem_limit_bytes=60 * 1024 * 1024
        ),
        cost_estimate=pl.CostEstimate(flops=14_000_000_000, bytes_accessed=24_000_000, transcendentals=4_000_000),
        name="decoder_window",
    )(
        features.reshape(cells, width), target.reshape(cells, outputs), gn_gain[None, :],
        attn_query, attn_key, attn_value, attn_out, conv_bias[None, :], percept, lpips_weight[None, :],
        crop_owner.reshape(1, -1), crop_frame, crop_col, conv_weight.reshape(taps, width, outputs),
    )
    conv_total = pl.pallas_call(
        widen,
        grid=(taps // 3,),
        in_specs=[pl.BlockSpec((2, 3, half, outputs), lambda i: (0, i, 0, 0))],
        out_specs=pl.BlockSpec((3, width, outputs), lambda i: (i, 0, 0)),
        out_shape=jax.ShapeDtypeStruct((taps, width, outputs), F32),
        name="widen",
    )(summed.reshape(2, taps, half, outputs)).reshape(conv_weight.shape)
    return (decoded.reshape(1, frames, rows_dev, cols, outputs), conv_total, distances)


def solution(mesh):
    return jax.shard_map(
        on_device,
        mesh=mesh,
        in_specs=(
            P("clip", None, "tile", None, None),
            P("clip", None, "tile", None, None),
            P(), P(), P(), P(), P(), P(), P(), P(), P(),
            P("clip", None, None),
            P("clip", None),
            P("clip", None),
        ),
        out_specs=(P("clip", None, "tile", None, None), P(), P("clip", "tile")),
        check_vma=False,
    )
```

```python
import functools
import math

import jax
import jax.numpy as jnp
from jax import lax
from jax.experimental import pallas as pl
from jax.experimental.pallas import tpu as pltpu
from jax.sharding import PartitionSpec as P

GROUPS = 32
CROPW = 64
EPSILON = 1e-06
F32 = jnp.float32
BF16 = jnp.bfloat16


def dot(a, b):
    return jnp.dot(a, b, preferred_element_type=F32)


def dot_nt(a, b):
    return lax.dot_general(a, b, (((1,), (1,)), ((), ())), preferred_element_type=F32)


def dot_tn(a, b):
    return lax.dot_general(a, b, (((0,), (0,)), ((), ())), preferred_element_type=F32)


def gelu_parts(z):
    k = math.sqrt(2.0 / math.pi)
    t = jnp.tanh(k * (z + 0.044715 * (z * z * z)))
    return 0.5 * z * (1.0 + t), t


def gelu_slope(z, t):
    k = math.sqrt(2.0 / math.pi)
    return 0.5 * (1.0 + t) + 0.5 * z * (1.0 - t * t) * (k * (1.0 + 3.0 * 0.044715 * (z * z)))


def shift_rows(value, step, cols):
    count = value.shape[0]
    place = lax.broadcasted_iota(jnp.int32, (count, 1), 0) % cols
    if step > 0:
        return jnp.where(place == 0, 0.0, pltpu.roll(value, 1, 0))
    return jnp.where(place == cols - 1, 0.0, pltpu.roll(value, count - 1, 0))


def chip_place():
    clip = lax.axis_index("clip")
    tile = lax.axis_index("tile")
    return (tile // 2, clip // 4, (tile % 2) * 2 + (clip // 2) % 2), clip % 2


def device_at(place, core):
    x, y, z = place
    return (y * 4 + (z % 2) * 2 + core, x * 2 + z // 2)


def on_axis(place, axis, position):
    moved = list(place)
    moved[axis] = lax.rem(position + 4, 4)
    return tuple(moved)


def decoder_window(
    tiles, frames, cols,
    features, target_hbm, wq_hbm, wk_hbm, wv_hbm, wo_hbm, percept_hbm, weight_hbm,
    gain_ref, bias_ref, lpips_ref, owner_ref, frame_ref, col_ref,
    decoded_ref, out_ref, dist_out,
    weight, wq_ref, wk_ref, wv_ref, wo_ref, percept_ref, target_ref, feats, normed, stats, qs, acc, peak, total, hidden, hidden_t, other_h, own_g, other_g, rhs,
    part, left1, right1, comb, got, red1, got2, got3, quarter, dist_row, dist_pair,
    once, gather_recv, recv, local,
):
    place, core = chip_place()
    clip = lax.axis_index("clip")
    mine = lax.axis_index("tile")
    x, side = mine // 2, mine % 2
    cells = frames * cols
    width = feats.shape[-1]
    outputs = bias_ref.shape[-1]
    half = width // 2
    cut = cells // 2

    def tile_at(step, other):
        return lax.rem(x + step + 4, 4) * 2 + (side + other) % 2

    def peer(axis, step):
        return device_at(on_axis(place, axis, place[axis] + step), core)

    def remote(src, dst, sent_sem, got_sem, target):
        copy = pltpu.make_async_remote_copy(
            src_ref=src, dst_ref=dst, send_sem=sent_sem, recv_sem=got_sem,
            device_id=target, device_id_type=pl.DeviceIdType.MESH,
        )
        copy.start()
        return copy

    def take(rows, sem):
        pltpu.make_async_copy(rows, rows, sem).wait()

    own, left, right, opposite = (tile_at(step, 0) for step in (0, -1, 1, 2))
    partner, left2, right2, opposite2 = (tile_at(step, 1) for step in (0, -1, 1, 2))
    far = jnp.where(side == 0, left2, right2)
    near = jnp.where(side == 0, right2, left2)
    sibling = device_at(place, 1 - core)

    barrier = pltpu.get_barrier_semaphore()
    peers = [(clip, lax.rem(mine + step, tiles)) for step in range(1, tiles)]
    peers += [peer(1, 1), peer(1, 2), peer(1, 3), peer(2, 1), peer(2, 3), sibling]
    for other in peers:
        pl.semaphore_signal(barrier, inc=1, device_id=other, device_id_type=pl.DeviceIdType.MESH)
    load = pltpu.make_async_copy(features, feats.at[own], local.at[0])
    load.start()
    early = [
        pltpu.make_async_copy(source, ref, local.at[3 + i])
        for i, (source, ref) in enumerate(
            ((wq_hbm, wq_ref), (wk_hbm, wk_ref), (wv_hbm, wv_ref), (wo_hbm, wo_ref), (percept_hbm, percept_ref), (target_hbm, target_ref))
        )
    ]
    for copy in early:
        copy.start()
    fetch = pltpu.make_async_copy(weight_hbm, weight, local.at[1])

    def pass_on(index, unit, h, to, mine_too=False):
        rows = feats.at[unit, pl.ds(h * cut, cut)]
        source = features.at[pl.ds(h * cut, cut)] if mine_too else rows
        return remote(source, rows, once.at[2], gather_recv.at[index], (clip, to))

    links = {}
    pl.semaphore_wait(barrier, len(peers))
    links["l0"] = pass_on(1, own, 0, right, True)
    links["r1"] = pass_on(2, own, 1, left, True)
    links["z0"] = pass_on(0, own, 0, partner, True)

    load.wait()
    wide = feats[own].astype(F32)
    stats[own] = jnp.concatenate(
        [jnp.sum(wide, axis=0, keepdims=True), jnp.sum(wide * wide, axis=0, keepdims=True), jnp.zeros((6, width), F32)],
        axis=0,
    )
    for step in range(tiles - 1):
        remote(stats.at[own], stats.at[own], once.at[0], once.at[1], peers[step])
    links["l1"] = pass_on(4, own, 1, right, True)
    links["r0"] = pass_on(5, own, 0, left, True)
    links["z1"] = pass_on(3, own, 1, partner, True)
    fetch.start()

    lane = lax.broadcasted_iota(jnp.int32, (width, width), 0) // (width // GROUPS)
    same = (lane == lax.broadcasted_iota(jnp.int32, (width, width), 1) // (width // GROUPS)).astype(BF16)
    links["l0"].wait_recv()
    links["o0"] = pass_on(6, left, 0, right)
    links["r1"].wait_recv()
    links["o1"] = pass_on(7, right, 1, left)
    links["z0"].wait_recv()
    links["l2"] = pass_on(8, partner, 0, right)
    links["r2"] = pass_on(11, partner, 0, left)
    take(stats.at[pl.ds(0, tiles - 1)], once.at[1])
    sums = stats[0]
    for i in range(1, tiles):
        sums = sums + stats[i]
    pieces, rest = [], sums
    for _ in range(3):
        pieces.append(rest.astype(BF16))
        rest = rest - pieces[-1].astype(F32)
    grouped = dot(pieces[0], same) + dot(pieces[1], same) + dot(pieces[2], same)
    count = F32(tiles * cells * (width // GROUPS))
    mean = grouped[0:1] / count
    spread = grouped[1:2] / count - mean * mean
    scale = lax.rsqrt(spread + EPSILON)
    gain = gain_ref[...]
    factor = math.log2(math.e) / math.sqrt(width)

    def normalize(slot, unit):
        normed[slot * cells : (slot + 1) * cells, :] = (((feats[unit].astype(F32) - mean) * scale) * gain).astype(BF16)

    def make_queries(role, slot):
        q = dot(normed[slot * cells : (slot + 1) * cells, :], wq_ref[...]).astype(BF16)
        qs[role * cells : (role + 1) * cells, :] = (dot_nt(q, wk_ref[...]) * factor).astype(BF16)

    def attend(roles, slots, first):
        here = slice(roles[0] * cells, roles[1] * cells)
        keys = normed[slots[0] * cells : slots[1] * cells, :]
        s = dot_nt(qs[here, :], keys)
        groups = [s[:, j : j + 128] for j in range(0, s.shape[1], 128)]
        top = jnp.max(functools.reduce(jnp.maximum, groups), axis=1, keepdims=True)
        new = jnp.broadcast_to(top, (s.shape[0], 128)) if first else jnp.maximum(peak[here, :], top)
        raised = [jnp.exp2(group - new) for group in groups]
        lanes = functools.reduce(jnp.add, raised)
        out = dot(jnp.concatenate([group.astype(BF16) for group in raised], axis=1), keys)
        if first:
            total[here, :] = lanes
            acc[here, :] = out
        else:
            fade = jnp.exp2(peak[here, :] - new)
            total[here, :] = total[here, :] * fade + lanes
            for j in range(0, width, 128):
                acc[here, j : j + 128] = acc[here, j : j + 128] * fade + out[:, j : j + 128]
        peak[here, :] = new

    for copy in early:
        copy.wait()
    normalize(0, own)
    make_queries(0, 0)
    links["z1"].wait_recv()
    links["r3"] = pass_on(9, partner, 1, left)
    links["l3"] = pass_on(10, partner, 1, right)
    normalize(1, partner)
    make_queries(1, 1)
    links["l1"].wait_recv()
    links["r0"].wait_recv()
    normalize(2, left)
    normalize(3, right)
    attend((0, 1), (0, 4), True)
    links["o0"].wait_recv()
    links["p0"] = pass_on(12, opposite, 0, partner)
    links["o1"].wait_recv()
    links["p1"] = pass_on(13, opposite, 1, partner)
    attend((1, 2), (0, 4), True)
    normalize(4, opposite)
    attend((0, 2), (4, 5), False)
    links["l2"].wait_recv()
    links["r3"].wait_recv()
    links["l3"].wait_recv()
    links["r2"].wait_recv()
    normalize(5, far)
    normalize(6, near)
    make_queries(2, 5)
    attend((2, 3), (0, 5), True)
    attend((0, 3), (5, 7), False)
    links["p0"].wait_recv()
    links["p1"].wait_recv()
    normalize(7, opposite2)
    attend((0, 3), (7, 8), False)

    def choose(i, values):
        chosen = values[0]
        for j in range(1, len(values)):
            chosen = jnp.where(i == j, values[j], chosen)
        return chosen

    def finish(role, _):
        here = pl.ds(pl.multiple_of(role * cells, cells), cells)
        unit = choose(role, [own, partner, far])
        b = choose(role, [1, 2 - 2 * side, 2 * side])
        whole = 1.0 / jnp.sum(total[here, :], axis=1, keepdims=True)
        context = (acc[here, :] * whole).astype(BF16)
        mixed = dot(context, wv_ref[...]).astype(BF16)
        row = feats[unit].astype(F32) + dot(mixed, wo_ref[...])
        inside = (mine + b >= 1) & (mine + b <= tiles)
        row = jnp.where(inside, row, 0.0).astype(BF16)
        hidden[b] = row
        hidden_t[b] = row.T
        return 0

    lax.fori_loop(0, 3, finish, 0)
    swap_h = remote(
        hidden_t.at[:, pl.ds(pl.multiple_of((1 - core) * half, half), half)], other_h, once.at[3], once.at[4], sibling
    )
    fetch.wait()

    sides = []
    for e in range(3):
        a2, a1, a0 = (
            sum(
                dot(hidden[b, : (a + 1) * cols, :], weight[(a * 3 + b) * 3 + e]) for b in range(3)
            )
            for a in (2, 1, 0)
        )
        sides.append(a2 + jnp.concatenate([a1[:cols], a1], axis=0) + jnp.concatenate([a0, a0, a0], axis=0))
    made = shift_rows(sides[0], 1, cols) + sides[1] + shift_rows(sides[2], -1, cols) + bias_ref[...]
    made = made.astype(BF16)
    decoded_ref[...] = made

    table = percept_ref[...]
    lw = lpips_ref[...]
    z = dot(made, table)
    m, t = gelu_parts(z)
    s = lax.rsqrt(jnp.mean(m * m, axis=-1, keepdims=True) + EPSILON)
    zt = dot(target_ref[...], table)
    mt, _ = gelu_parts(zt)
    st = lax.rsqrt(jnp.mean(mt * mt, axis=-1, keepdims=True) + EPSILON)
    gap = m * s - mt * st
    weighted = gap * lw
    apart = jnp.sum(weighted * gap, axis=-1, keepdims=True)
    up = weighted * (2.0 / CROPW)
    dm = up * s - m * (s * s * s) * (jnp.sum(up * m, axis=-1, keepdims=True) / outputs)
    dz = dm * gelu_slope(z, t)
    high = dz.astype(BF16)
    low = (dz - high.astype(F32)).astype(BF16)
    pull = (dot_nt(high, table) + dot_nt(low, table)).astype(BF16).astype(F32)

    spot = lax.broadcasted_iota(jnp.int32, (cols, 1), 0)
    col = col_ref[...]
    covers = (spot >= col) & (spot < col + CROPW) & (owner_ref[...] == mine)
    distance = jnp.zeros((1, col.shape[1]), F32)
    for f in range(frames):
        cover = (covers & (frame_ref[...] == f)).astype(F32)
        rows = slice(f * cols, (f + 1) * cols)
        distance = distance + jnp.sum(cover * apart[rows], axis=0, keepdims=True)
        own_g[rows, :] = (pull[rows] * jnp.sum(cover, axis=1, keepdims=True)).astype(BF16)
    dist_row[3] = jnp.broadcast_to(distance / CROPW, dist_row.shape[1:])
    swap_g = remote(own_g, other_g, once.at[5], once.at[6], sibling)
    for step in (1, 2, 3):
        remote(dist_row.at[3], dist_row.at[step - 1], once.at[7], once.at[8], peer(0, step))

    mixes = (
        lambda g: [g[0] + g[1] + g[2]],
        lambda g: [g[0] + g[1], g[2]],
        lambda g: g,
    )

    def line_up(ref, place_in):
        g = [ref[f * cols : (f + 1) * cols, :].astype(F32) for f in range(frames)]
        for p in range(3):
            mixed = jnp.concatenate(mixes[p](g), axis=0)
            depth = mixed.shape[0]
            for e, moved in enumerate((shift_rows(mixed, -1, cols), mixed, shift_rows(mixed, 1, cols))):
                rhs[p, place_in * depth : (place_in + 1) * depth, e * outputs : (e + 1) * outputs] = moved.astype(BF16)

    line_up(own_g, 0)
    swap_g.wait_recv()
    line_up(other_g, 1)
    swap_h.wait_recv()

    quarter_rows = quarter.shape[1]
    half_rows = quarter_rows // 2
    piece = quarter_rows // 4
    chunk_rows = 4 * quarter_rows
    own_half = pl.ds(pl.multiple_of(core * half, half), half)

    def chunk_at(b, q, h, count=1):
        return pl.ds(pl.multiple_of(b * chunk_rows + lax.rem(q + 4, 4) * quarter_rows + h * half_rows, 16), half_rows * count)

    def out_rows(p, b, q, h, count=1):
        return out_ref.at[core, p, chunk_at(b, q, h, count)]

    def go(c, stage, src, dst, to):
        remote(src, dst, once.at[9 if stage < 5 else 10], recv.at[c, stage], to)

    def across_to(src, dst):
        remote(src, dst, once.at[10], once.at[11], sibling)

    def make(b):
        for p in range(3):
            c, m, depth = p * 3 + b, place[p], (p + 1) * cols
            lhs = jnp.concatenate([hidden_t[b, own_half, :depth], other_h[b, :, :depth]], axis=1)
            for e in range(3):
                base = b * chunk_rows + e * half
                part[p, base : base + half, :] = dot(
                    lhs, rhs[p, : 2 * depth, e * outputs : (e + 1) * outputs]
                ).astype(BF16)
            go(c, 0, part.at[p, chunk_at(b, m + 2, 0)], left1.at[c], peer(p, 1))
            go(c, 0, part.at[p, chunk_at(b, m + 2, 1)], right1.at[c], peer(p, 3))
            go(c, 1, part.at[p, chunk_at(b, m + 1, 1)], got.at[c, 0, pl.ds(half_rows, half_rows)], peer(p, 1))
            go(c, 1, part.at[p, chunk_at(b, m - 1, 0)], got.at[c, 1, pl.ds(0, half_rows)], peer(p, 3))

    def ring(b):
        for p in range(3):
            c, m = p * 3 + b, place[p]
            take(comb.at[c], recv.at[c, 0])
            for way, arrived, q, step in ((0, left1, m + 1, 1), (1, right1, m - 1, 3)):
                comb[c, way] = (part[p, chunk_at(b, q, way), :].astype(F32) + arrived[c].astype(F32)).astype(BF16)
                go(c, 1, comb.at[c, way], got.at[c, way, pl.ds(way * half_rows, half_rows)], peer(p, step))

    def direct(b):
        for p in range(3):
            c, axis = p * 3 + b, (p + 1) % 3
            take(got.at[c], recv.at[c, 1])
            mine_rows = part[p, chunk_at(b, place[p], 0, 2), :].astype(F32)
            red1[c] = (mine_rows + got[c, 0].astype(F32) + got[c, 1].astype(F32)).astype(BF16)
            for step in (1, 2, 3):
                to = lax.rem(place[axis] + step, 4)
                go(c, 2, red1.at[c, pl.ds(pl.multiple_of(to * piece, 16), piece)], got2.at[c, step - 1], peer(axis, step))

    def to_all(b):
        for p in range(3):
            c, axis, here = p * 3 + b, (p + 2) % 3, place[(p + 1) % 3]
            take(got2.at[c], recv.at[c, 2])
            added = red1[c, pl.ds(pl.multiple_of(here * piece, 16), piece), :].astype(F32)
            for i in range(3):
                added = added + got2[c, i].astype(F32)
            got3[c, place[axis]] = added.astype(BF16)
            for step in (1, 2, 3):
                slot = got3.at[c, place[axis]]
                go(c, 3, slot, slot, peer(axis, step))

    def back(b):
        for p in range(3):
            c, axis = p * 3 + b, (p + 1) % 3
            take(got2.at[c], recv.at[c, 3])
            whole = got3[c, 0].astype(F32)
            for i in range(1, 4):
                whole = whole + got3[c, i].astype(F32)
            rows = pl.ds(pl.multiple_of(place[axis] * piece, 16), piece)
            quarter[c, rows, :] = whole.astype(BF16)
            for step in (1, 2, 3):
                slot = quarter.at[c, rows]
                go(c, 4, slot, slot, peer(axis, step))

    def spread_out(b):
        for p in range(3):
            c, m = p * 3 + b, place[p]
            take(got2.at[c], recv.at[c, 4])
            for stage, h, step in ((5, 0, 1), (5, 1, 3), (6, 1, 1), (6, 0, 3)):
                go(c, stage, quarter.at[c, pl.ds(h * half_rows, half_rows)], out_rows(p, b, m, h), peer(p, step))
            across_to(quarter.at[c], out_rows(p, b, m, 0, 2))
            pltpu.make_async_copy(quarter.at[c], out_rows(p, b, m, 0, 2), local.at[2]).start()

    def forward(b):
        for p in range(3):
            c, m = p * 3 + b, place[p]
            take(quarter.at[c], recv.at[c, 5])
            for h, q, step in ((0, m - 1, 1), (1, m + 1, 3)):
                go(c, 7, out_rows(p, b, q, h), out_rows(p, b, q, h), peer(p, step))

    def across(b):
        for p in range(3):
            c, m = p * 3 + b, place[p]
            take(quarter.at[c], recv.at[c, 6])
            for q in (m - 1, m + 1):
                across_to(out_rows(p, b, q, 0, 2), out_rows(p, b, q, 0, 2))

    def across_last(b):
        for p in range(3):
            c, m = p * 3 + b, place[p]
            take(quarter.at[c], recv.at[c, 7])
            across_to(out_rows(p, b, m + 2, 0, 2), out_rows(p, b, m + 2, 0, 2))

    make(0)
    make(1)
    ring(0)
    make(2)
    ring(1)

    take(dist_row.at[pl.ds(0, 3)], once.at[8])
    dist_pair[0] = dist_row[0] + dist_row[1] + dist_row[2] + dist_row[3]
    pair = remote(dist_pair.at[0], dist_pair.at[1], once.at[12], once.at[13], peer(2, 2))

    ring(2)
    for stage in (direct, to_all, back, spread_out, forward, across, across_last):
        for b in range(3):
            stage(b)

    pair.wait()
    crops, scored = dist_pair.shape[2], dist_out.shape[1]
    pick = lax.broadcasted_iota(jnp.int32, (crops, scored), 0) == (
        mine * scored + lax.broadcasted_iota(jnp.int32, (crops, scored), 1)
    )
    dist_out[...] = jnp.dot(
        dist_pair[0] + dist_pair[1], pick.astype(F32), precision=lax.Precision.HIGHEST, preferred_element_type=F32
    )[0:1]
    take(out_ref.at[1 - core], once.at[11])
    take(quarter, local.at[2])
    take(stats.at[pl.ds(0, tiles - 1)], once.at[0])
    take(feats.at[pl.ds(0, 7)], once.at[2])
    take(dist_row.at[pl.ds(0, 3)], once.at[7])
    take(weight.at[:, pl.ds(0, 9 * 21 * half_rows // 54)], once.at[9])
    take(weight.at[:, pl.ds(0, 9 * 14 * half_rows // 27)], once.at[10])
    swap_g.wait_send()
    swap_h.wait_send()


def widen(halves, out_hbm, near, wide, in_sems, out_sems):
    taps, half = halves.shape[1:3]
    steps = in_sems.shape[0]
    count = taps // steps
    pieces = [pl.ds(i * count, count) for i in range(steps)]
    loads = [pltpu.make_async_copy(halves.at[:, rows], near.at[:, rows], in_sems.at[i]) for i, rows in enumerate(pieces)]
    stores = [pltpu.make_async_copy(wide.at[rows], out_hbm.at[rows], out_sems.at[i]) for i, rows in enumerate(pieces)]
    for copy in loads:
        copy.start()
    for i in range(steps):
        loads[i].wait()
        for tap in range(i * count, (i + 1) * count):
            for h in range(2):
                wide[tap, h * half : (h + 1) * half, :] = near[h, tap].astype(F32)
        stores[i].start()
    for copy in stores:
        copy.wait()


def on_device(
    features, target, gn_gain, attn_query, attn_key, attn_value, attn_out, conv_weight, conv_bias,
    percept, lpips_weight, crop_owner, crop_frame, crop_col,
):
    tiles = lax.axis_size("tile")
    frames, rows_dev, cols, width = features.shape[1:]
    outputs = conv_weight.shape[-1]
    cells = frames * rows_dev * cols
    taps = 27
    half = width // 2
    part_rows = taps // 3 * half
    quarter = part_rows // 12
    crops = crop_col.shape[1]
    vmem = pl.BlockSpec(memory_space=pltpu.VMEM)
    hbm = pl.BlockSpec(memory_space=pl.ANY)
    sems = lambda count: pltpu.SemaphoreType.DMA((count,))
    decoded, summed, distances = pl.pallas_call(
        functools.partial(decoder_window, tiles, frames, cols),
        in_specs=[hbm] * 8 + [vmem] * 6,
        out_specs=[vmem, hbm, vmem],
        out_shape=[
            jax.ShapeDtypeStruct((cells, outputs), BF16),
            jax.ShapeDtypeStruct((2, 3, part_rows, outputs), BF16),
            jax.ShapeDtypeStruct((1, crops // tiles), F32),
        ],
        scratch_shapes=[
            pltpu.VMEM((taps, width, outputs), BF16),
            pltpu.VMEM((width, width), BF16),
            pltpu.VMEM((width, width), BF16),
            pltpu.VMEM((width, width), BF16),
            pltpu.VMEM((width, width), BF16),
            pltpu.VMEM((outputs, outputs), BF16),
            pltpu.VMEM((cells, outputs), BF16),
            pltpu.VMEM((tiles, cells, width), BF16),
            pltpu.VMEM((tiles * cells, width), BF16),
            pltpu.VMEM((tiles, 8, width), F32),
            pltpu.VMEM((3 * cells, width), BF16),
            pltpu.VMEM((3 * cells, width), F32),
            pltpu.VMEM((3 * cells, 128), F32),
            pltpu.VMEM((3 * cells, 128), F32),
            pltpu.VMEM((3, cells, width), BF16),
            pltpu.VMEM((3, width, cells), BF16),
            pltpu.VMEM((3, half, cells), BF16),
            pltpu.VMEM((cells, outputs), BF16),
            pltpu.VMEM((cells, outputs), BF16),
            pltpu.VMEM((3, 2 * cells, 3 * outputs), BF16),
            pltpu.VMEM((3, part_rows, outputs), BF16),
            pltpu.VMEM((9, quarter // 2, outputs), BF16),
            pltpu.VMEM((9, quarter // 2, outputs), BF16),
            pltpu.VMEM((9, 2, quarter // 2, outputs), BF16),
            pltpu.VMEM((9, 2, quarter, outputs), BF16),
            pltpu.VMEM((9, quarter, outputs), BF16),
            pltpu.VMEM((9, 3, quarter // 4, outputs), BF16),
            pltpu.VMEM((9, 4, quarter // 4, outputs), BF16),
            pltpu.VMEM((9, quarter, outputs), BF16),
            pltpu.VMEM((4, 8, crops), F32),
            pltpu.VMEM((2, 8, crops), F32),
            sems(14), sems(14), pltpu.SemaphoreType.DMA((9, 8)), sems(9),
        ],
        compiler_params=pltpu.CompilerParams(
            collective_id=1, has_side_effects=True, vmem_limit_bytes=60 * 1024 * 1024
        ),
        cost_estimate=pl.CostEstimate(flops=14_000_000_000, bytes_accessed=24_000_000, transcendentals=4_000_000),
        name="decoder_window",
    )(
        features.reshape(cells, width), target.reshape(cells, outputs), attn_query, attn_key, attn_value, attn_out,
        percept, conv_weight.reshape(taps, width, outputs), gn_gain[None, :], conv_bias[None, :], lpips_weight[None, :],
        crop_owner.reshape(1, -1), crop_frame, crop_col,
    )
    conv_total = pl.pallas_call(
        widen,
        in_specs=[hbm],
        out_specs=hbm,
        out_shape=jax.ShapeDtypeStruct((taps, width, outputs), F32),
        scratch_shapes=[pltpu.VMEM((2, taps, half, outputs), BF16), pltpu.VMEM((taps, width, outputs), F32), sems(9), sems(9)],
        compiler_params=pltpu.CompilerParams(vmem_limit_bytes=60 * 1024 * 1024),
        name="widen",
    )(summed.reshape(2, taps, half, outputs)).reshape(conv_weight.shape)
    return (decoded.reshape(1, frames, rows_dev, cols, outputs), conv_total, distances)


def solution(mesh):
    return jax.shard_map(
        on_device,
        mesh=mesh,
        in_specs=(
            P("clip", None, "tile", None, None),
            P("clip", None, "tile", None, None),
            P(), P(), P(), P(), P(), P(), P(), P(), P(),
            P("clip", None, None),
            P("clip", None),
            P("clip", None),
        ),
        out_specs=(P("clip", None, "tile", None, None), P(), P("clip", "tile")),
        check_vma=False,
    )
```

```python
import functools
import math

import jax
import jax.numpy as jnp
from jax import lax
from jax.experimental import pallas as pl
from jax.experimental.pallas import tpu as pltpu
from jax.sharding import PartitionSpec as P

GROUPS = 32
CROPW = 64
EPSILON = 1e-06
F32 = jnp.float32
BF16 = jnp.bfloat16


def dot(a, b):
    return jnp.dot(a, b, preferred_element_type=F32)


def dot_nt(a, b):
    return lax.dot_general(a, b, (((1,), (1,)), ((), ())), preferred_element_type=F32)


def dot_tn(a, b):
    return lax.dot_general(a, b, (((0,), (0,)), ((), ())), preferred_element_type=F32)


def gelu_parts(z):
    k = math.sqrt(2.0 / math.pi)
    t = jnp.tanh(k * (z + 0.044715 * (z * z * z)))
    return 0.5 * z * (1.0 + t), t


def gelu_slope(z, t):
    k = math.sqrt(2.0 / math.pi)
    return 0.5 * (1.0 + t) + 0.5 * z * (1.0 - t * t) * (k * (1.0 + 3.0 * 0.044715 * (z * z)))


def shift_rows(value, step, cols):
    count = value.shape[0]
    place = lax.broadcasted_iota(jnp.int32, (count, 1), 0) % cols
    if step > 0:
        return jnp.where(place == 0, 0.0, pltpu.roll(value, 1, 0))
    return jnp.where(place == cols - 1, 0.0, pltpu.roll(value, count - 1, 0))


def chip_place():
    clip = lax.axis_index("clip")
    tile = lax.axis_index("tile")
    return (tile // 2, clip // 4, (tile % 2) * 2 + (clip // 2) % 2), clip % 2


def device_at(place, core):
    x, y, z = place
    return (y * 4 + (z % 2) * 2 + core, x * 2 + z // 2)


def on_axis(place, axis, position):
    moved = list(place)
    moved[axis] = lax.rem(position + 4, 4)
    return tuple(moved)


def decoder_window(
    tiles, frames, cols,
    features, target_hbm, wq_hbm, wk_hbm, wv_hbm, wo_hbm, percept_hbm, weight_hbm,
    gain_hbm, bias_hbm, lpips_hbm, owner_hbm, frame_hbm, col_hbm,
    decoded_ref, out_ref, dist_out,
    weight, wq_ref, wk_ref, wv_ref, wo_ref, percept_ref, target_ref,
    gain_ref, bias_ref, lpips_ref, owner_ref, frame_ref, col_ref, feats, normed, stats, qs, acc, peak, total, hidden, hidden_t, other_h, own_g, other_g, rhs,
    part, left1, right1, comb, got, red1, got2, got3, quarter, dist_row, dist_pair,
    once, gather_recv, recv, local,
):
    place, core = chip_place()
    clip = lax.axis_index("clip")
    mine = lax.axis_index("tile")
    x, side = mine // 2, mine % 2
    cells = frames * cols
    width = feats.shape[-1]
    outputs = bias_ref.shape[-1]
    half = width // 2
    cut = cells // 2

    def tile_at(step, other):
        return lax.rem(x + step + 4, 4) * 2 + (side + other) % 2

    def peer(axis, step):
        return device_at(on_axis(place, axis, place[axis] + step), core)

    def remote(src, dst, sent_sem, got_sem, target):
        copy = pltpu.make_async_remote_copy(
            src_ref=src, dst_ref=dst, send_sem=sent_sem, recv_sem=got_sem,
            device_id=target, device_id_type=pl.DeviceIdType.MESH,
        )
        copy.start()
        return copy

    def take(rows, sem):
        pltpu.make_async_copy(rows, rows, sem).wait()

    own, left, right, opposite = (tile_at(step, 0) for step in (0, -1, 1, 2))
    partner, left2, right2, opposite2 = (tile_at(step, 1) for step in (0, -1, 1, 2))
    far = jnp.where(side == 0, left2, right2)
    near = jnp.where(side == 0, right2, left2)
    sibling = device_at(place, 1 - core)

    barrier = pltpu.get_barrier_semaphore()
    peers = [(clip, lax.rem(mine + step, tiles)) for step in range(1, tiles)]
    peers += [peer(1, 1), peer(1, 2), peer(1, 3), peer(2, 1), peer(2, 3), sibling]
    for other in peers:
        pl.semaphore_signal(barrier, inc=1, device_id=other, device_id_type=pl.DeviceIdType.MESH)
    load = pltpu.make_async_copy(features, feats.at[own], local.at[0])
    load.start()
    early = [
        pltpu.make_async_copy(source, ref, local.at[3 + i])
        for i, (source, ref) in enumerate(
            (
                (wq_hbm, wq_ref), (wk_hbm, wk_ref), (wv_hbm, wv_ref), (wo_hbm, wo_ref), (percept_hbm, percept_ref),
                (target_hbm, target_ref), (gain_hbm, gain_ref), (bias_hbm, bias_ref), (lpips_hbm, lpips_ref),
                (owner_hbm, owner_ref), (frame_hbm, frame_ref), (col_hbm, col_ref),
            )
        )
    ]
    for copy in early:
        copy.start()
    fetch = pltpu.make_async_copy(weight_hbm, weight, local.at[1])

    def pass_on(index, unit, h, to, mine_too=False):
        rows = feats.at[unit, pl.ds(h * cut, cut)]
        source = features.at[pl.ds(h * cut, cut)] if mine_too else rows
        return remote(source, rows, once.at[2], gather_recv.at[index], (clip, to))

    links = {}
    pl.semaphore_wait(barrier, len(peers))
    links["l0"] = pass_on(1, own, 0, right, True)
    links["r1"] = pass_on(2, own, 1, left, True)
    links["z0"] = pass_on(0, own, 0, partner, True)

    load.wait()
    wide = feats[own].astype(F32)
    stats[own] = jnp.concatenate(
        [jnp.sum(wide, axis=0, keepdims=True), jnp.sum(wide * wide, axis=0, keepdims=True), jnp.zeros((6, width), F32)],
        axis=0,
    )
    for step in range(tiles - 1):
        remote(stats.at[own], stats.at[own], once.at[0], once.at[1], peers[step])
    links["l1"] = pass_on(4, own, 1, right, True)
    links["r0"] = pass_on(5, own, 0, left, True)
    links["z1"] = pass_on(3, own, 1, partner, True)
    fetch.start()

    lane = lax.broadcasted_iota(jnp.int32, (width, width), 0) // (width // GROUPS)
    same = (lane == lax.broadcasted_iota(jnp.int32, (width, width), 1) // (width // GROUPS)).astype(BF16)
    links["l0"].wait_recv()
    links["o0"] = pass_on(6, left, 0, right)
    links["r1"].wait_recv()
    links["o1"] = pass_on(7, right, 1, left)
    links["z0"].wait_recv()
    links["l2"] = pass_on(8, partner, 0, right)
    links["r2"] = pass_on(11, partner, 0, left)
    take(stats.at[pl.ds(0, tiles - 1)], once.at[1])
    sums = stats[0]
    for i in range(1, tiles):
        sums = sums + stats[i]
    pieces, rest = [], sums
    for _ in range(3):
        pieces.append(rest.astype(BF16))
        rest = rest - pieces[-1].astype(F32)
    grouped = dot(pieces[0], same) + dot(pieces[1], same) + dot(pieces[2], same)
    count = F32(tiles * cells * (width // GROUPS))
    mean = grouped[0:1] / count
    spread = grouped[1:2] / count - mean * mean
    scale = lax.rsqrt(spread + EPSILON)
    for copy in early:
        copy.wait()
    gain = gain_ref[...]
    factor = math.log2(math.e) / math.sqrt(width)

    def normalize(slot, unit):
        normed[slot * cells : (slot + 1) * cells, :] = (((feats[unit].astype(F32) - mean) * scale) * gain).astype(BF16)

    def make_queries(role, slot):
        q = dot(normed[slot * cells : (slot + 1) * cells, :], wq_ref[...]).astype(BF16)
        qs[role * cells : (role + 1) * cells, :] = (dot_nt(q, wk_ref[...]) * factor).astype(BF16)

    def attend(roles, slots, first):
        here = slice(roles[0] * cells, roles[1] * cells)
        keys = normed[slots[0] * cells : slots[1] * cells, :]
        s = dot_nt(qs[here, :], keys)
        groups = [s[:, j : j + 128] for j in range(0, s.shape[1], 128)]
        top = jnp.max(functools.reduce(jnp.maximum, groups), axis=1, keepdims=True)
        new = jnp.broadcast_to(top, (s.shape[0], 128)) if first else jnp.maximum(peak[here, :], top)
        raised = [jnp.exp2(group - new) for group in groups]
        lanes = functools.reduce(jnp.add, raised)
        out = dot(jnp.concatenate([group.astype(BF16) for group in raised], axis=1), keys)
        if first:
            total[here, :] = lanes
            acc[here, :] = out
        else:
            fade = jnp.exp2(peak[here, :] - new)
            total[here, :] = total[here, :] * fade + lanes
            for j in range(0, width, 128):
                acc[here, j : j + 128] = acc[here, j : j + 128] * fade + out[:, j : j + 128]
        peak[here, :] = new

    normalize(0, own)
    make_queries(0, 0)
    links["z1"].wait_recv()
    links["r3"] = pass_on(9, partner, 1, left)
    links["l3"] = pass_on(10, partner, 1, right)
    normalize(1, partner)
    make_queries(1, 1)
    links["l1"].wait_recv()
    links["r0"].wait_recv()
    normalize(2, left)
    normalize(3, right)
    attend((0, 1), (0, 4), True)
    links["o0"].wait_recv()
    links["p0"] = pass_on(12, opposite, 0, partner)
    links["o1"].wait_recv()
    links["p1"] = pass_on(13, opposite, 1, partner)
    attend((1, 2), (0, 4), True)
    normalize(4, opposite)
    attend((0, 2), (4, 5), False)
    links["l2"].wait_recv()
    links["r3"].wait_recv()
    links["l3"].wait_recv()
    links["r2"].wait_recv()
    normalize(5, far)
    normalize(6, near)
    make_queries(2, 5)
    attend((2, 3), (0, 5), True)
    attend((0, 3), (5, 7), False)
    links["p0"].wait_recv()
    links["p1"].wait_recv()
    normalize(7, opposite2)
    attend((0, 3), (7, 8), False)

    for role, unit, b in ((0, own, 1), (1, partner, 2 - 2 * side), (2, far, 2 * side)):
        here = slice(role * cells, (role + 1) * cells)
        whole = 1.0 / jnp.sum(total[here, :], axis=1, keepdims=True)
        context = (acc[here, :] * whole).astype(BF16)
        mixed = dot(context, wv_ref[...]).astype(BF16)
        row = feats[unit].astype(F32) + dot(mixed, wo_ref[...])
        inside = (mine + b >= 1) & (mine + b <= tiles)
        row = jnp.where(inside, row, 0.0).astype(BF16)
        hidden[b] = row
        hidden_t[b] = row.T

    swap_h = remote(
        hidden_t.at[:, pl.ds(pl.multiple_of((1 - core) * half, half), half)], other_h, once.at[3], once.at[4], sibling
    )
    fetch.wait()

    sides = []
    for e in range(3):
        a2, a1, a0 = (
            sum(
                dot(hidden[b, : (a + 1) * cols, :], weight[(a * 3 + b) * 3 + e]) for b in range(3)
            )
            for a in (2, 1, 0)
        )
        sides.append(a2 + jnp.concatenate([a1[:cols], a1], axis=0) + jnp.concatenate([a0, a0, a0], axis=0))
    made = shift_rows(sides[0], 1, cols) + sides[1] + shift_rows(sides[2], -1, cols) + bias_ref[...]
    made = made.astype(BF16)
    decoded_ref[...] = made

    table = percept_ref[...]
    lw = lpips_ref[...]
    z = dot(made, table)
    m, t = gelu_parts(z)
    s = lax.rsqrt(jnp.mean(m * m, axis=-1, keepdims=True) + EPSILON)
    zt = dot(target_ref[...], table)
    mt, _ = gelu_parts(zt)
    st = lax.rsqrt(jnp.mean(mt * mt, axis=-1, keepdims=True) + EPSILON)
    gap = m * s - mt * st
    weighted = gap * lw
    apart = jnp.sum(weighted * gap, axis=-1, keepdims=True)
    up = weighted * (2.0 / CROPW)
    dm = up * s - m * (s * s * s) * (jnp.sum(up * m, axis=-1, keepdims=True) / outputs)
    dz = dm * gelu_slope(z, t)
    high = dz.astype(BF16)
    low = (dz - high.astype(F32)).astype(BF16)
    pull = (dot_nt(high, table) + dot_nt(low, table)).astype(BF16).astype(F32)

    spot = lax.broadcasted_iota(jnp.int32, (cols, 1), 0)
    col = col_ref[...]
    covers = (spot >= col) & (spot < col + CROPW) & (owner_ref[...] == mine)
    distance = jnp.zeros((1, col.shape[1]), F32)
    for f in range(frames):
        cover = (covers & (frame_ref[...] == f)).astype(F32)
        rows = slice(f * cols, (f + 1) * cols)
        distance = distance + jnp.sum(cover * apart[rows], axis=0, keepdims=True)
        own_g[rows, :] = (pull[rows] * jnp.sum(cover, axis=1, keepdims=True)).astype(BF16)
    dist_row[3] = jnp.broadcast_to(distance / CROPW, dist_row.shape[1:])
    swap_g = remote(own_g, other_g, once.at[5], once.at[6], sibling)
    for step in (1, 2, 3):
        remote(dist_row.at[3], dist_row.at[step - 1], once.at[7], once.at[8], peer(0, step))

    mixes = (
        lambda g: [g[0] + g[1] + g[2]],
        lambda g: [g[0] + g[1], g[2]],
        lambda g: g,
    )

    def line_up(ref, place_in):
        g = [ref[f * cols : (f + 1) * cols, :].astype(F32) for f in range(frames)]
        for p in range(3):
            mixed = jnp.concatenate(mixes[p](g), axis=0)
            depth = mixed.shape[0]
            for e, moved in enumerate((shift_rows(mixed, -1, cols), mixed, shift_rows(mixed, 1, cols))):
                rhs[p, place_in * depth : (place_in + 1) * depth, e * outputs : (e + 1) * outputs] = moved.astype(BF16)

    line_up(own_g, 0)
    swap_g.wait_recv()
    line_up(other_g, 1)
    swap_h.wait_recv()

    quarter_rows = quarter.shape[1]
    half_rows = quarter_rows // 2
    piece = quarter_rows // 4
    chunk_rows = 4 * quarter_rows
    own_half = pl.ds(pl.multiple_of(core * half, half), half)

    def chunk_at(b, q, h, count=1):
        return pl.ds(pl.multiple_of(b * chunk_rows + lax.rem(q + 4, 4) * quarter_rows + h * half_rows, 16), half_rows * count)

    def out_rows(p, b, q, h, count=1):
        return out_ref.at[core, p, chunk_at(b, q, h, count)]

    def go(c, stage, src, dst, to):
        remote(src, dst, once.at[9 if stage < 5 else 10], recv.at[c, stage], to)

    def across_to(src, dst):
        remote(src, dst, once.at[10], once.at[11], sibling)

    def make(b):
        for p in range(3):
            c, m, depth = p * 3 + b, place[p], (p + 1) * cols
            lhs = jnp.concatenate([hidden_t[b, own_half, :depth], other_h[b, :, :depth]], axis=1)
            for e in range(3):
                base = b * chunk_rows + e * half
                part[p, base : base + half, :] = dot(
                    lhs, rhs[p, : 2 * depth, e * outputs : (e + 1) * outputs]
                ).astype(BF16)
            go(c, 0, part.at[p, chunk_at(b, m + 2, 0)], left1.at[c], peer(p, 1))
            go(c, 0, part.at[p, chunk_at(b, m + 2, 1)], right1.at[c], peer(p, 3))
            go(c, 1, part.at[p, chunk_at(b, m + 1, 1)], got.at[c, 0, pl.ds(half_rows, half_rows)], peer(p, 1))
            go(c, 1, part.at[p, chunk_at(b, m - 1, 0)], got.at[c, 1, pl.ds(0, half_rows)], peer(p, 3))

    def ring(b):
        for p in range(3):
            c, m = p * 3 + b, place[p]
            take(comb.at[c], recv.at[c, 0])
            for way, arrived, q, step in ((0, left1, m + 1, 1), (1, right1, m - 1, 3)):
                comb[c, way] = (part[p, chunk_at(b, q, way), :].astype(F32) + arrived[c].astype(F32)).astype(BF16)
                go(c, 1, comb.at[c, way], got.at[c, way, pl.ds(way * half_rows, half_rows)], peer(p, step))

    def direct(b):
        for p in range(3):
            c, axis = p * 3 + b, (p + 1) % 3
            take(got.at[c], recv.at[c, 1])
            mine_rows = part[p, chunk_at(b, place[p], 0, 2), :].astype(F32)
            red1[c] = (mine_rows + got[c, 0].astype(F32) + got[c, 1].astype(F32)).astype(BF16)
            for step in (1, 2, 3):
                to = lax.rem(place[axis] + step, 4)
                go(c, 2, red1.at[c, pl.ds(pl.multiple_of(to * piece, 16), piece)], got2.at[c, step - 1], peer(axis, step))

    def to_all(b):
        for p in range(3):
            c, axis, here = p * 3 + b, (p + 2) % 3, place[(p + 1) % 3]
            take(got2.at[c], recv.at[c, 2])
            added = red1[c, pl.ds(pl.multiple_of(here * piece, 16), piece), :].astype(F32)
            for i in range(3):
                added = added + got2[c, i].astype(F32)
            got3[c, place[axis]] = added.astype(BF16)
            for step in (1, 2, 3):
                slot = got3.at[c, place[axis]]
                go(c, 3, slot, slot, peer(axis, step))

    def back(b):
        for p in range(3):
            c, axis = p * 3 + b, (p + 1) % 3
            take(got2.at[c], recv.at[c, 3])
            whole = got3[c, 0].astype(F32)
            for i in range(1, 4):
                whole = whole + got3[c, i].astype(F32)
            rows = pl.ds(pl.multiple_of(place[axis] * piece, 16), piece)
            quarter[c, rows, :] = whole.astype(BF16)
            for step in (1, 2, 3):
                slot = quarter.at[c, rows]
                go(c, 4, slot, slot, peer(axis, step))

    def spread_out(b):
        for p in range(3):
            c, m = p * 3 + b, place[p]
            take(got2.at[c], recv.at[c, 4])
            for stage, h, step in ((5, 0, 1), (5, 1, 3), (6, 1, 1), (6, 0, 3)):
                go(c, stage, quarter.at[c, pl.ds(h * half_rows, half_rows)], out_rows(p, b, m, h), peer(p, step))
            across_to(quarter.at[c], out_rows(p, b, m, 0, 2))
            pltpu.make_async_copy(quarter.at[c], out_rows(p, b, m, 0, 2), local.at[2]).start()

    def forward(b):
        for p in range(3):
            c, m = p * 3 + b, place[p]
            take(quarter.at[c], recv.at[c, 5])
            for h, q, step in ((0, m - 1, 1), (1, m + 1, 3)):
                go(c, 7, out_rows(p, b, q, h), out_rows(p, b, q, h), peer(p, step))

    def across(b):
        for p in range(3):
            c, m = p * 3 + b, place[p]
            take(quarter.at[c], recv.at[c, 6])
            for q in (m - 1, m + 1):
                across_to(out_rows(p, b, q, 0, 2), out_rows(p, b, q, 0, 2))

    def across_last(b):
        for p in range(3):
            c, m = p * 3 + b, place[p]
            take(quarter.at[c], recv.at[c, 7])
            across_to(out_rows(p, b, m + 2, 0, 2), out_rows(p, b, m + 2, 0, 2))

    make(0)
    make(1)
    ring(0)
    make(2)
    ring(1)

    take(dist_row.at[pl.ds(0, 3)], once.at[8])
    dist_pair[0] = dist_row[0] + dist_row[1] + dist_row[2] + dist_row[3]
    pair = remote(dist_pair.at[0], dist_pair.at[1], once.at[12], once.at[13], peer(2, 2))

    ring(2)
    for stage in (direct, to_all, back, spread_out, forward, across, across_last):
        for b in range(3):
            stage(b)

    pair.wait()
    crops, scored = dist_pair.shape[2], dist_out.shape[1]
    pick = lax.broadcasted_iota(jnp.int32, (crops, scored), 0) == (
        mine * scored + lax.broadcasted_iota(jnp.int32, (crops, scored), 1)
    )
    dist_out[...] = jnp.dot(
        dist_pair[0] + dist_pair[1], pick.astype(F32), precision=lax.Precision.HIGHEST, preferred_element_type=F32
    )[0:1]
    take(out_ref.at[1 - core], once.at[11])
    take(quarter, local.at[2])
    take(stats.at[pl.ds(0, tiles - 1)], once.at[0])
    take(feats.at[pl.ds(0, 7)], once.at[2])
    take(dist_row.at[pl.ds(0, 3)], once.at[7])
    take(weight.at[:, pl.ds(0, 9 * 21 * half_rows // 54)], once.at[9])
    take(weight.at[:, pl.ds(0, 9 * 14 * half_rows // 27)], once.at[10])
    swap_g.wait_send()
    swap_h.wait_send()


def widen(halves, made, scored, out_hbm, made_out, scored_out, near, wide, in_sems, out_sems, made_sem):
    hand_on = pltpu.make_async_copy(made, made_out, made_sem)
    taps, half = halves.shape[1:3]
    steps = in_sems.shape[0]
    count = taps // steps
    pieces = [pl.ds(i * count, count) for i in range(steps)]
    loads = [pltpu.make_async_copy(halves.at[:, rows], near.at[:, rows], in_sems.at[i]) for i, rows in enumerate(pieces)]
    stores = [pltpu.make_async_copy(wide.at[rows], out_hbm.at[rows], out_sems.at[i]) for i, rows in enumerate(pieces)]
    for copy in loads:
        copy.start()
    hand_on.start()
    scored_out[...] = scored[...]
    for i in range(steps):
        loads[i].wait()
        for tap in range(i * count, (i + 1) * count):
            for h in range(2):
                wide[tap, h * half : (h + 1) * half, :] = near[h, tap].astype(F32)
        stores[i].start()
    for copy in stores:
        copy.wait()
    hand_on.wait()


def on_device(
    features, target, gn_gain, attn_query, attn_key, attn_value, attn_out, conv_weight, conv_bias,
    percept, lpips_weight, crop_owner, crop_frame, crop_col,
):
    tiles = lax.axis_size("tile")
    frames, rows_dev, cols, width = features.shape[1:]
    outputs = conv_weight.shape[-1]
    cells = frames * rows_dev * cols
    taps = 27
    half = width // 2
    part_rows = taps // 3 * half
    quarter = part_rows // 12
    crops = crop_col.shape[1]
    vmem = pl.BlockSpec(memory_space=pltpu.VMEM)
    hbm = pl.BlockSpec(memory_space=pl.ANY)
    sems = lambda count: pltpu.SemaphoreType.DMA((count,))
    decoded, summed, distances = pl.pallas_call(
        functools.partial(decoder_window, tiles, frames, cols),
        in_specs=[hbm] * 14,
        out_specs=[vmem, hbm, vmem],
        out_shape=[
            jax.ShapeDtypeStruct((cells, outputs), BF16),
            jax.ShapeDtypeStruct((2, 3, part_rows, outputs), BF16),
            jax.ShapeDtypeStruct((1, crops // tiles), F32),
        ],
        scratch_shapes=[
            pltpu.VMEM((taps, width, outputs), BF16),
            pltpu.VMEM((width, width), BF16),
            pltpu.VMEM((width, width), BF16),
            pltpu.VMEM((width, width), BF16),
            pltpu.VMEM((width, width), BF16),
            pltpu.VMEM((outputs, outputs), BF16),
            pltpu.VMEM((cells, outputs), BF16),
            pltpu.VMEM((1, width), F32),
            pltpu.VMEM((1, outputs), F32),
            pltpu.VMEM((1, outputs), F32),
            pltpu.VMEM((1, crops), jnp.int32),
            pltpu.VMEM((1, crops), jnp.int32),
            pltpu.VMEM((1, crops), jnp.int32),
            pltpu.VMEM((tiles, cells, width), BF16),
            pltpu.VMEM((tiles * cells, width), BF16),
            pltpu.VMEM((tiles, 8, width), F32),
            pltpu.VMEM((3 * cells, width), BF16),
            pltpu.VMEM((3 * cells, width), F32),
            pltpu.VMEM((3 * cells, 128), F32),
            pltpu.VMEM((3 * cells, 128), F32),
            pltpu.VMEM((3, cells, width), BF16),
            pltpu.VMEM((3, width, cells), BF16),
            pltpu.VMEM((3, half, cells), BF16),
            pltpu.VMEM((cells, outputs), BF16),
            pltpu.VMEM((cells, outputs), BF16),
            pltpu.VMEM((3, 2 * cells, 3 * outputs), BF16),
            pltpu.VMEM((3, part_rows, outputs), BF16),
            pltpu.VMEM((9, quarter // 2, outputs), BF16),
            pltpu.VMEM((9, quarter // 2, outputs), BF16),
            pltpu.VMEM((9, 2, quarter // 2, outputs), BF16),
            pltpu.VMEM((9, 2, quarter, outputs), BF16),
            pltpu.VMEM((9, quarter, outputs), BF16),
            pltpu.VMEM((9, 3, quarter // 4, outputs), BF16),
            pltpu.VMEM((9, 4, quarter // 4, outputs), BF16),
            pltpu.VMEM((9, quarter, outputs), BF16),
            pltpu.VMEM((4, 8, crops), F32),
            pltpu.VMEM((2, 8, crops), F32),
            sems(14), sems(14), pltpu.SemaphoreType.DMA((9, 8)), sems(15),
        ],
        compiler_params=pltpu.CompilerParams(
            collective_id=1, has_side_effects=True, vmem_limit_bytes=60 * 1024 * 1024
        ),
        cost_estimate=pl.CostEstimate(flops=14_000_000_000, bytes_accessed=24_000_000, transcendentals=4_000_000),
        name="decoder_window",
    )(
        features.reshape(cells, width), target.reshape(cells, outputs), attn_query, attn_key, attn_value, attn_out,
        percept, conv_weight.reshape(taps, width, outputs), gn_gain[None, :], conv_bias[None, :], lpips_weight[None, :],
        crop_owner.reshape(1, -1), crop_frame, crop_col,
    )
    conv_total, decoded, distances = pl.pallas_call(
        widen,
        in_specs=[hbm, hbm, vmem],
        out_specs=[hbm, hbm, vmem],
        out_shape=[
            jax.ShapeDtypeStruct((taps, width, outputs), F32),
            jax.ShapeDtypeStruct(decoded.shape, BF16),
            jax.ShapeDtypeStruct(distances.shape, F32),
        ],
        scratch_shapes=[pltpu.VMEM((2, taps, half, outputs), BF16), pltpu.VMEM((taps, width, outputs), F32), sems(9), sems(9), pltpu.SemaphoreType.DMA],
        compiler_params=pltpu.CompilerParams(vmem_limit_bytes=60 * 1024 * 1024),
        name="widen",
    )(summed.reshape(2, taps, half, outputs), decoded, distances)
    conv_total = conv_total.reshape(conv_weight.shape)
    return (decoded.reshape(1, frames, rows_dev, cols, outputs), conv_total, distances)


def solution(mesh):
    return jax.shard_map(
        on_device,
        mesh=mesh,
        in_specs=(
            P("clip", None, "tile", None, None),
            P("clip", None, "tile", None, None),
            P(), P(), P(), P(), P(), P(), P(), P(), P(),
            P("clip", None, None),
            P("clip", None),
            P("clip", None),
        ),
        out_specs=(P("clip", None, "tile", None, None), P(), P("clip", "tile")),
        check_vma=False,
    )
```

```python
import functools
import math

import jax
import jax.numpy as jnp
from jax import lax
from jax.experimental import pallas as pl
from jax.experimental.pallas import tpu as pltpu
from jax.sharding import PartitionSpec as P

GROUPS = 32
CROPW = 64
EPSILON = 1e-06
F32 = jnp.float32
BF16 = jnp.bfloat16


def dot(a, b):
    return jnp.dot(a, b, preferred_element_type=F32)


def dot_nt(a, b):
    return lax.dot_general(a, b, (((1,), (1,)), ((), ())), preferred_element_type=F32)


def dot_tn(a, b):
    return lax.dot_general(a, b, (((0,), (0,)), ((), ())), preferred_element_type=F32)


def gelu_parts(z):
    k = math.sqrt(2.0 / math.pi)
    t = jnp.tanh(k * (z + 0.044715 * (z * z * z)))
    return 0.5 * z * (1.0 + t), t


def gelu_slope(z, t):
    k = math.sqrt(2.0 / math.pi)
    return 0.5 * (1.0 + t) + 0.5 * z * (1.0 - t * t) * (k * (1.0 + 3.0 * 0.044715 * (z * z)))


def shift_rows(value, step, cols):
    count = value.shape[0]
    place = lax.broadcasted_iota(jnp.int32, (count, 1), 0) % cols
    if step > 0:
        return jnp.where(place == 0, 0.0, pltpu.roll(value, 1, 0))
    return jnp.where(place == cols - 1, 0.0, pltpu.roll(value, count - 1, 0))


def chip_place():
    clip = lax.axis_index("clip")
    tile = lax.axis_index("tile")
    return (tile // 2, clip // 4, (tile % 2) * 2 + (clip // 2) % 2), clip % 2


def device_at(place, core):
    x, y, z = place
    return (y * 4 + (z % 2) * 2 + core, x * 2 + z // 2)


def on_axis(place, axis, position):
    moved = list(place)
    moved[axis] = lax.rem(position + 4, 4)
    return tuple(moved)


def decoder_window(
    tiles, frames, cols,
    features, target_hbm, wq_hbm, wk_hbm, wv_hbm, wo_hbm, percept_hbm, weight_hbm,
    gain_hbm, bias_hbm, lpips_hbm, owner_hbm, frame_hbm, col_hbm,
    decoded_ref, out_ref, dist_out,
    weight, wq_ref, wk_ref, wv_ref, wo_ref, percept_ref, target_ref,
    gain_ref, bias_ref, lpips_ref, owner_ref, frame_ref, col_ref, feats, normed, stats, qs, acc, peak, total, hidden, hidden_t, other_h, own_g, other_g, rhs,
    part, left1, right1, comb, got, red1, got2, got3, quarter, dist_row, dist_pair,
    once, gather_recv, recv, local,
):
    place, core = chip_place()
    clip = lax.axis_index("clip")
    mine = lax.axis_index("tile")
    x, side = mine // 2, mine % 2
    cells = frames * cols
    width = feats.shape[-1]
    outputs = bias_ref.shape[-1]
    half = width // 2
    cut = cells // 2

    def tile_at(step, other):
        return lax.rem(x + step + 4, 4) * 2 + (side + other) % 2

    def peer(axis, step):
        return device_at(on_axis(place, axis, place[axis] + step), core)

    def remote(src, dst, sent_sem, got_sem, target):
        copy = pltpu.make_async_remote_copy(
            src_ref=src, dst_ref=dst, send_sem=sent_sem, recv_sem=got_sem,
            device_id=target, device_id_type=pl.DeviceIdType.MESH,
        )
        copy.start()
        return copy

    def take(rows, sem):
        pltpu.make_async_copy(rows, rows, sem).wait()

    own, left, right, opposite = (tile_at(step, 0) for step in (0, -1, 1, 2))
    partner, left2, right2, opposite2 = (tile_at(step, 1) for step in (0, -1, 1, 2))
    far = jnp.where(side == 0, left2, right2)
    near = jnp.where(side == 0, right2, left2)
    sibling = device_at(place, 1 - core)

    barrier = pltpu.get_barrier_semaphore()
    peers = [(clip, lax.rem(mine + step, tiles)) for step in range(1, tiles)]
    peers += [peer(1, 1), peer(1, 2), peer(1, 3), peer(2, 1), peer(2, 3), sibling]
    for other in peers:
        pl.semaphore_signal(barrier, inc=1, device_id=other, device_id_type=pl.DeviceIdType.MESH)
    load = pltpu.make_async_copy(features, feats.at[own], local.at[0])
    load.start()
    early = [
        pltpu.make_async_copy(source, ref, local.at[3 + i])
        for i, (source, ref) in enumerate(
            (
                (wq_hbm, wq_ref), (wk_hbm, wk_ref), (wv_hbm, wv_ref), (wo_hbm, wo_ref), (percept_hbm, percept_ref),
                (target_hbm, target_ref), (gain_hbm, gain_ref), (bias_hbm, bias_ref), (lpips_hbm, lpips_ref),
                (owner_hbm, owner_ref), (frame_hbm, frame_ref), (col_hbm, col_ref),
            )
        )
    ]
    for copy in early:
        copy.start()
    fetch = pltpu.make_async_copy(weight_hbm, weight, local.at[1])

    def pass_on(index, unit, h, to, mine_too=False):
        rows = feats.at[unit, pl.ds(h * cut, cut)]
        source = features.at[pl.ds(h * cut, cut)] if mine_too else rows
        return remote(source, rows, once.at[2], gather_recv.at[index], (clip, to))

    links = {}
    pl.semaphore_wait(barrier, len(peers))
    links["l0"] = pass_on(1, own, 0, right, True)
    links["r1"] = pass_on(2, own, 1, left, True)
    links["z0"] = pass_on(0, own, 0, partner, True)

    load.wait()
    wide = feats[own].astype(F32)
    stats[own] = jnp.concatenate(
        [jnp.sum(wide, axis=0, keepdims=True), jnp.sum(wide * wide, axis=0, keepdims=True), jnp.zeros((6, width), F32)],
        axis=0,
    )
    for step in range(tiles - 1):
        remote(stats.at[own], stats.at[own], once.at[0], once.at[1], peers[step])
    links["l1"] = pass_on(4, own, 1, right, True)
    links["r0"] = pass_on(5, own, 0, left, True)
    links["z1"] = pass_on(3, own, 1, partner, True)
    fetch.start()

    lane = lax.broadcasted_iota(jnp.int32, (width, width), 0) // (width // GROUPS)
    same = (lane == lax.broadcasted_iota(jnp.int32, (width, width), 1) // (width // GROUPS)).astype(BF16)
    links["l0"].wait_recv()
    links["o0"] = pass_on(6, left, 0, right)
    links["r1"].wait_recv()
    links["o1"] = pass_on(7, right, 1, left)
    links["z0"].wait_recv()
    links["l2"] = pass_on(8, partner, 0, right)
    links["r2"] = pass_on(11, partner, 0, left)
    take(stats.at[pl.ds(0, tiles - 1)], once.at[1])
    sums = stats[0]
    for i in range(1, tiles):
        sums = sums + stats[i]
    pieces, rest = [], sums
    for _ in range(3):
        pieces.append(rest.astype(BF16))
        rest = rest - pieces[-1].astype(F32)
    grouped = dot(pieces[0], same) + dot(pieces[1], same) + dot(pieces[2], same)
    count = F32(tiles * cells * (width // GROUPS))
    mean = grouped[0:1] / count
    spread = grouped[1:2] / count - mean * mean
    scale = lax.rsqrt(spread + EPSILON)
    for copy in early:
        copy.wait()
    gain = gain_ref[...]
    factor = math.log2(math.e) / math.sqrt(width)

    def normalize(slot, unit):
        normed[slot * cells : (slot + 1) * cells, :] = (((feats[unit].astype(F32) - mean) * scale) * gain).astype(BF16)

    def make_queries(role, slot):
        q = dot(normed[slot * cells : (slot + 1) * cells, :], wq_ref[...]).astype(BF16)
        qs[role * cells : (role + 1) * cells, :] = (dot_nt(q, wk_ref[...]) * factor).astype(BF16)

    def attend(roles, slots, first):
        here = slice(roles[0] * cells, roles[1] * cells)
        keys = normed[slots[0] * cells : slots[1] * cells, :]
        s = dot_nt(qs[here, :], keys)
        groups = [s[:, j : j + 128] for j in range(0, s.shape[1], 128)]
        top = jnp.max(functools.reduce(jnp.maximum, groups), axis=1, keepdims=True)
        new = jnp.broadcast_to(top, (s.shape[0], 128)) if first else jnp.maximum(peak[here, :], top)
        raised = [jnp.exp2(group - new) for group in groups]
        lanes = functools.reduce(jnp.add, raised)
        out = dot(jnp.concatenate([group.astype(BF16) for group in raised], axis=1), keys)
        if first:
            total[here, :] = lanes
            acc[here, :] = out
        else:
            fade = jnp.exp2(peak[here, :] - new)
            total[here, :] = total[here, :] * fade + lanes
            for j in range(0, width, 128):
                acc[here, j : j + 128] = acc[here, j : j + 128] * fade + out[:, j : j + 128]
        peak[here, :] = new

    normalize(0, own)
    make_queries(0, 0)
    links["z1"].wait_recv()
    links["r3"] = pass_on(9, partner, 1, left)
    links["l3"] = pass_on(10, partner, 1, right)
    normalize(1, partner)
    make_queries(1, 1)
    links["l1"].wait_recv()
    links["r0"].wait_recv()
    normalize(2, left)
    normalize(3, right)
    attend((0, 1), (0, 4), True)
    links["o0"].wait_recv()
    links["p0"] = pass_on(12, opposite, 0, partner)
    links["o1"].wait_recv()
    links["p1"] = pass_on(13, opposite, 1, partner)
    attend((1, 2), (0, 4), True)
    normalize(4, opposite)
    attend((0, 2), (4, 5), False)
    links["l2"].wait_recv()
    links["r3"].wait_recv()
    links["l3"].wait_recv()
    links["r2"].wait_recv()
    normalize(5, far)
    normalize(6, near)
    make_queries(2, 5)
    attend((2, 3), (0, 5), True)
    attend((0, 3), (5, 7), False)
    links["p0"].wait_recv()
    links["p1"].wait_recv()
    normalize(7, opposite2)
    attend((0, 3), (7, 8), False)

    for role, unit, b in ((0, own, 1), (1, partner, 2 - 2 * side), (2, far, 2 * side)):
        here = slice(role * cells, (role + 1) * cells)
        whole = 1.0 / jnp.sum(total[here, :], axis=1, keepdims=True)
        context = (acc[here, :] * whole).astype(BF16)
        mixed = dot(context, wv_ref[...]).astype(BF16)
        row = feats[unit].astype(F32) + dot(mixed, wo_ref[...])
        inside = (mine + b >= 1) & (mine + b <= tiles)
        row = jnp.where(inside, row, 0.0).astype(BF16)
        hidden[b] = row
        hidden_t[b] = row.T

    swap_h = remote(
        hidden_t.at[:, pl.ds(pl.multiple_of((1 - core) * half, half), half)], other_h, once.at[3], once.at[4], sibling
    )
    fetch.wait()

    sides = []
    for e in range(3):
        a2, a1, a0 = (
            sum(
                dot(hidden[b, : (a + 1) * cols, :], weight[(a * 3 + b) * 3 + e]) for b in range(3)
            )
            for a in (2, 1, 0)
        )
        sides.append(a2 + jnp.concatenate([a1[:cols], a1], axis=0) + jnp.concatenate([a0, a0, a0], axis=0))
    made = shift_rows(sides[0], 1, cols) + sides[1] + shift_rows(sides[2], -1, cols) + bias_ref[...]
    made = made.astype(BF16)
    decoded_ref[...] = made

    table = percept_ref[...]
    lw = lpips_ref[...]
    z = dot(made, table)
    m, t = gelu_parts(z)
    s = lax.rsqrt(jnp.mean(m * m, axis=-1, keepdims=True) + EPSILON)
    zt = dot(target_ref[...], table)
    mt, _ = gelu_parts(zt)
    st = lax.rsqrt(jnp.mean(mt * mt, axis=-1, keepdims=True) + EPSILON)
    gap = m * s - mt * st
    weighted = gap * lw
    apart = jnp.sum(weighted * gap, axis=-1, keepdims=True)
    up = weighted * (2.0 / CROPW)
    dm = up * s - m * (s * s * s) * (jnp.sum(up * m, axis=-1, keepdims=True) / outputs)
    dz = dm * gelu_slope(z, t)
    high = dz.astype(BF16)
    low = (dz - high.astype(F32)).astype(BF16)
    pull = (dot_nt(high, table) + dot_nt(low, table)).astype(BF16).astype(F32)

    spot = lax.broadcasted_iota(jnp.int32, (cols, 1), 0)
    col = col_ref[...]
    covers = (spot >= col) & (spot < col + CROPW) & (owner_ref[...] == mine)
    distance = jnp.zeros((1, col.shape[1]), F32)
    for f in range(frames):
        cover = (covers & (frame_ref[...] == f)).astype(F32)
        rows = slice(f * cols, (f + 1) * cols)
        distance = distance + jnp.sum(cover * apart[rows], axis=0, keepdims=True)
        own_g[rows, :] = (pull[rows] * jnp.sum(cover, axis=1, keepdims=True)).astype(BF16)
    dist_row[3] = jnp.broadcast_to(distance / CROPW, dist_row.shape[1:])
    swap_g = remote(own_g, other_g, once.at[5], once.at[6], sibling)
    for step in (1, 2, 3):
        remote(dist_row.at[3], dist_row.at[step - 1], once.at[7], once.at[8], peer(0, step))

    mixes = (
        lambda g: [g[0] + g[1] + g[2]],
        lambda g: [g[0] + g[1], g[2]],
        lambda g: g,
    )

    def line_up(ref, place_in):
        g = [ref[f * cols : (f + 1) * cols, :].astype(F32) for f in range(frames)]
        for p in range(3):
            mixed = jnp.concatenate(mixes[p](g), axis=0)
            depth = mixed.shape[0]
            for e, moved in enumerate((shift_rows(mixed, -1, cols), mixed, shift_rows(mixed, 1, cols))):
                rhs[p, place_in * depth : (place_in + 1) * depth, e * outputs : (e + 1) * outputs] = moved.astype(BF16)

    line_up(own_g, 0)
    swap_g.wait_recv()
    line_up(other_g, 1)
    swap_h.wait_recv()

    quarter_rows = quarter.shape[1]
    half_rows = quarter_rows // 2
    piece = quarter_rows // 4
    chunk_rows = 4 * quarter_rows
    own_half = pl.ds(pl.multiple_of(core * half, half), half)

    def chunk_at(b, q, h, count=1):
        return pl.ds(pl.multiple_of(b * chunk_rows + lax.rem(q + 4, 4) * quarter_rows + h * half_rows, 16), half_rows * count)

    def out_rows(p, b, q, h, count=1):
        return out_ref.at[core, p, chunk_at(b, q, h, count)]

    def go(c, stage, src, dst, to):
        remote(src, dst, once.at[9 if stage < 5 else 10], recv.at[c, stage], to)

    def across_to(src, dst):
        remote(src, dst, once.at[10], once.at[11], sibling)

    def make(b):
        for p in range(3):
            c, m, depth = p * 3 + b, place[p], (p + 1) * cols
            lhs = jnp.concatenate([hidden_t[b, own_half, :depth], other_h[b, :, :depth]], axis=1)
            for e in range(3):
                base = b * chunk_rows + e * half
                part[p, base : base + half, :] = dot(
                    lhs, rhs[p, : 2 * depth, e * outputs : (e + 1) * outputs]
                ).astype(BF16)
            go(c, 0, part.at[p, chunk_at(b, m + 2, 0)], left1.at[c], peer(p, 1))
            go(c, 0, part.at[p, chunk_at(b, m + 2, 1)], right1.at[c], peer(p, 3))
            go(c, 1, part.at[p, chunk_at(b, m + 1, 1)], got.at[c, 0, pl.ds(half_rows, half_rows)], peer(p, 1))
            go(c, 1, part.at[p, chunk_at(b, m - 1, 0)], got.at[c, 1, pl.ds(0, half_rows)], peer(p, 3))

    def ring(b):
        for p in range(3):
            c, m = p * 3 + b, place[p]
            take(comb.at[c], recv.at[c, 0])
            for way, arrived, q, step in ((0, left1, m + 1, 1), (1, right1, m - 1, 3)):
                comb[c, way] = (part[p, chunk_at(b, q, way), :].astype(F32) + arrived[c].astype(F32)).astype(BF16)
                go(c, 1, comb.at[c, way], got.at[c, way, pl.ds(way * half_rows, half_rows)], peer(p, step))

    def direct(b):
        for p in range(3):
            c, axis = p * 3 + b, (p + 1) % 3
            take(got.at[c], recv.at[c, 1])
            mine_rows = part[p, chunk_at(b, place[p], 0, 2), :].astype(F32)
            red1[c] = (mine_rows + got[c, 0].astype(F32) + got[c, 1].astype(F32)).astype(BF16)
            for step in (1, 2, 3):
                to = lax.rem(place[axis] + step, 4)
                go(c, 2, red1.at[c, pl.ds(pl.multiple_of(to * piece, 16), piece)], got2.at[c, step - 1], peer(axis, step))

    def to_all(b):
        for p in range(3):
            c, axis, here = p * 3 + b, (p + 2) % 3, place[(p + 1) % 3]
            take(got2.at[c], recv.at[c, 2])
            added = red1[c, pl.ds(pl.multiple_of(here * piece, 16), piece), :].astype(F32)
            for i in range(3):
                added = added + got2[c, i].astype(F32)
            got3[c, place[axis]] = added.astype(BF16)
            for step in (1, 2, 3):
                slot = got3.at[c, place[axis]]
                go(c, 3, slot, slot, peer(axis, step))

    def back(b):
        for p in range(3):
            c, axis = p * 3 + b, (p + 1) % 3
            take(got2.at[c], recv.at[c, 3])
            whole = got3[c, 0].astype(F32)
            for i in range(1, 4):
                whole = whole + got3[c, i].astype(F32)
            rows = pl.ds(pl.multiple_of(place[axis] * piece, 16), piece)
            quarter[c, rows, :] = whole.astype(BF16)
            for step in (1, 2, 3):
                slot = quarter.at[c, rows]
                go(c, 4, slot, slot, peer(axis, step))

    def spread_out(b):
        for p in range(3):
            c, m = p * 3 + b, place[p]
            take(got2.at[c], recv.at[c, 4])
            for stage, h, step in ((5, 0, 1), (5, 1, 3), (6, 1, 1), (6, 0, 3)):
                go(c, stage, quarter.at[c, pl.ds(h * half_rows, half_rows)], out_rows(p, b, m, h), peer(p, step))
            across_to(quarter.at[c], out_rows(p, b, m, 0, 2))
            pltpu.make_async_copy(quarter.at[c], out_rows(p, b, m, 0, 2), local.at[2]).start()

    def forward(b):
        for p in range(3):
            c, m = p * 3 + b, place[p]
            take(quarter.at[c], recv.at[c, 5])
            for h, q, step in ((0, m - 1, 1), (1, m + 1, 3)):
                go(c, 7, out_rows(p, b, q, h), out_rows(p, b, q, h), peer(p, step))

    def across(b):
        for p in range(3):
            c, m = p * 3 + b, place[p]
            take(quarter.at[c], recv.at[c, 6])
            for q in (m - 1, m + 1):
                across_to(out_rows(p, b, q, 0, 2), out_rows(p, b, q, 0, 2))

    def across_last(b):
        for p in range(3):
            c, m = p * 3 + b, place[p]
            take(quarter.at[c], recv.at[c, 7])
            across_to(out_rows(p, b, m + 2, 0, 2), out_rows(p, b, m + 2, 0, 2))

    make(0)
    make(1)
    ring(0)
    make(2)
    ring(1)

    take(dist_row.at[pl.ds(0, 3)], once.at[8])
    dist_pair[0] = dist_row[0] + dist_row[1] + dist_row[2] + dist_row[3]
    pair = remote(dist_pair.at[0], dist_pair.at[1], once.at[12], once.at[13], peer(2, 2))

    ring(2)
    for stage in (direct, to_all, back, spread_out, forward, across, across_last):
        for b in range(3):
            stage(b)

    pair.wait()
    crops, scored = dist_pair.shape[2], dist_out.shape[1]
    pick = lax.broadcasted_iota(jnp.int32, (crops, scored), 0) == (
        mine * scored + lax.broadcasted_iota(jnp.int32, (crops, scored), 1)
    )
    dist_out[...] = jnp.dot(
        dist_pair[0] + dist_pair[1], pick.astype(F32), precision=lax.Precision.HIGHEST, preferred_element_type=F32
    )[0:1]
    take(out_ref.at[1 - core], once.at[11])
    take(quarter, local.at[2])
    take(stats.at[pl.ds(0, tiles - 1)], once.at[0])
    take(feats.at[pl.ds(0, 7)], once.at[2])
    take(dist_row.at[pl.ds(0, 3)], once.at[7])
    take(weight.at[:, pl.ds(0, 9 * 21 * half_rows // 54)], once.at[9])
    take(weight.at[:, pl.ds(0, 9 * 14 * half_rows // 27)], once.at[10])
    swap_g.wait_send()
    swap_h.wait_send()


def widen(halves, made, scored, out_hbm, made_out, scored_out, near, wide, in_sems, out_sems, hand_sems):
    hand_on = [
        pltpu.make_async_copy(made, made_out, hand_sems.at[0]),
        pltpu.make_async_copy(scored, scored_out, hand_sems.at[1]),
    ]
    taps, half = halves.shape[1:3]
    steps = in_sems.shape[0]
    count = taps // steps
    pieces = [pl.ds(i * count, count) for i in range(steps)]
    loads = [pltpu.make_async_copy(halves.at[:, rows], near.at[:, rows], in_sems.at[i]) for i, rows in enumerate(pieces)]
    stores = [pltpu.make_async_copy(wide.at[rows], out_hbm.at[rows], out_sems.at[i]) for i, rows in enumerate(pieces)]
    for copy in loads + hand_on:
        copy.start()
    for i in range(steps):
        loads[i].wait()
        for tap in range(i * count, (i + 1) * count):
            for h in range(2):
                wide[tap, h * half : (h + 1) * half, :] = near[h, tap].astype(F32)
        stores[i].start()
    for copy in stores + hand_on:
        copy.wait()


def on_device(
    features, target, gn_gain, attn_query, attn_key, attn_value, attn_out, conv_weight, conv_bias,
    percept, lpips_weight, crop_owner, crop_frame, crop_col,
):
    tiles = lax.axis_size("tile")
    frames, rows_dev, cols, width = features.shape[1:]
    outputs = conv_weight.shape[-1]
    cells = frames * rows_dev * cols
    taps = 27
    half = width // 2
    part_rows = taps // 3 * half
    quarter = part_rows // 12
    crops = crop_col.shape[1]
    vmem = pl.BlockSpec(memory_space=pltpu.VMEM)
    hbm = pl.BlockSpec(memory_space=pl.ANY)
    sems = lambda count: pltpu.SemaphoreType.DMA((count,))
    decoded, summed, distances = pl.pallas_call(
        functools.partial(decoder_window, tiles, frames, cols),
        in_specs=[hbm] * 14,
        out_specs=[vmem, hbm, vmem],
        out_shape=[
            jax.ShapeDtypeStruct((cells, outputs), BF16),
            jax.ShapeDtypeStruct((2, 3, part_rows, outputs), BF16),
            jax.ShapeDtypeStruct((1, crops // tiles), F32),
        ],
        scratch_shapes=[
            pltpu.VMEM((taps, width, outputs), BF16),
            pltpu.VMEM((width, width), BF16),
            pltpu.VMEM((width, width), BF16),
            pltpu.VMEM((width, width), BF16),
            pltpu.VMEM((width, width), BF16),
            pltpu.VMEM((outputs, outputs), BF16),
            pltpu.VMEM((cells, outputs), BF16),
            pltpu.VMEM((1, width), F32),
            pltpu.VMEM((1, outputs), F32),
            pltpu.VMEM((1, outputs), F32),
            pltpu.VMEM((1, crops), jnp.int32),
            pltpu.VMEM((1, crops), jnp.int32),
            pltpu.VMEM((1, crops), jnp.int32),
            pltpu.VMEM((tiles, cells, width), BF16),
            pltpu.VMEM((tiles * cells, width), BF16),
            pltpu.VMEM((tiles, 8, width), F32),
            pltpu.VMEM((3 * cells, width), BF16),
            pltpu.VMEM((3 * cells, width), F32),
            pltpu.VMEM((3 * cells, 128), F32),
            pltpu.VMEM((3 * cells, 128), F32),
            pltpu.VMEM((3, cells, width), BF16),
            pltpu.VMEM((3, width, cells), BF16),
            pltpu.VMEM((3, half, cells), BF16),
            pltpu.VMEM((cells, outputs), BF16),
            pltpu.VMEM((cells, outputs), BF16),
            pltpu.VMEM((3, 2 * cells, 3 * outputs), BF16),
            pltpu.VMEM((3, part_rows, outputs), BF16),
            pltpu.VMEM((9, quarter // 2, outputs), BF16),
            pltpu.VMEM((9, quarter // 2, outputs), BF16),
            pltpu.VMEM((9, 2, quarter // 2, outputs), BF16),
            pltpu.VMEM((9, 2, quarter, outputs), BF16),
            pltpu.VMEM((9, quarter, outputs), BF16),
            pltpu.VMEM((9, 3, quarter // 4, outputs), BF16),
            pltpu.VMEM((9, 4, quarter // 4, outputs), BF16),
            pltpu.VMEM((9, quarter, outputs), BF16),
            pltpu.VMEM((4, 8, crops), F32),
            pltpu.VMEM((2, 8, crops), F32),
            sems(14), sems(14), pltpu.SemaphoreType.DMA((9, 8)), sems(15),
        ],
        compiler_params=pltpu.CompilerParams(
            collective_id=1, has_side_effects=True, vmem_limit_bytes=60 * 1024 * 1024
        ),
        cost_estimate=pl.CostEstimate(flops=14_000_000_000, bytes_accessed=24_000_000, transcendentals=4_000_000),
        name="decoder_window",
    )(
        features.reshape(cells, width), target.reshape(cells, outputs), attn_query, attn_key, attn_value, attn_out,
        percept, conv_weight.reshape(taps, width, outputs), gn_gain[None, :], conv_bias[None, :], lpips_weight[None, :],
        crop_owner.reshape(1, -1), crop_frame, crop_col,
    )
    conv_total, decoded, distances = pl.pallas_call(
        widen,
        in_specs=[hbm] * 3,
        out_specs=[hbm] * 3,
        out_shape=[
            jax.ShapeDtypeStruct((taps, width, outputs), F32),
            jax.ShapeDtypeStruct(decoded.shape, BF16),
            jax.ShapeDtypeStruct(distances.shape, F32),
        ],
        scratch_shapes=[pltpu.VMEM((2, taps, half, outputs), BF16), pltpu.VMEM((taps, width, outputs), F32), sems(9), sems(9), sems(2)],
        compiler_params=pltpu.CompilerParams(vmem_limit_bytes=60 * 1024 * 1024),
        name="widen",
    )(summed.reshape(2, taps, half, outputs), decoded, distances)
    conv_total = conv_total.reshape(conv_weight.shape)
    return (decoded.reshape(1, frames, rows_dev, cols, outputs), conv_total, distances)


def solution(mesh):
    return jax.shard_map(
        on_device,
        mesh=mesh,
        in_specs=(
            P("clip", None, "tile", None, None),
            P("clip", None, "tile", None, None),
            P(), P(), P(), P(), P(), P(), P(), P(), P(),
            P("clip", None, None),
            P("clip", None),
            P("clip", None),
        ),
        out_specs=(P("clip", None, "tile", None, None), P(), P("clip", "tile")),
        check_vma=False,
    )
```

```python
import functools
import math

import jax
import jax.numpy as jnp
from jax import lax
from jax.experimental import pallas as pl
from jax.experimental.pallas import tpu as pltpu
from jax.sharding import PartitionSpec as P

GROUPS = 32
CROPW = 64
EPSILON = 1e-06
F32 = jnp.float32
BF16 = jnp.bfloat16


def dot(a, b):
    return jnp.dot(a, b, preferred_element_type=F32)


def dot_nt(a, b):
    return lax.dot_general(a, b, (((1,), (1,)), ((), ())), preferred_element_type=F32)


def dot_tn(a, b):
    return lax.dot_general(a, b, (((0,), (0,)), ((), ())), preferred_element_type=F32)


def gelu_parts(z):
    k = math.sqrt(2.0 / math.pi)
    t = jnp.tanh(k * (z + 0.044715 * (z * z * z)))
    return 0.5 * z * (1.0 + t), t


def gelu_slope(z, t):
    k = math.sqrt(2.0 / math.pi)
    return 0.5 * (1.0 + t) + 0.5 * z * (1.0 - t * t) * (k * (1.0 + 3.0 * 0.044715 * (z * z)))


def shift_rows(value, step, cols):
    count = value.shape[0]
    place = lax.broadcasted_iota(jnp.int32, (count, 1), 0) % cols
    if step > 0:
        return jnp.where(place == 0, 0.0, pltpu.roll(value, 1, 0))
    return jnp.where(place == cols - 1, 0.0, pltpu.roll(value, count - 1, 0))


def chip_place():
    clip = lax.axis_index("clip")
    tile = lax.axis_index("tile")
    return (tile // 2, clip // 4, (tile % 2) * 2 + (clip // 2) % 2), clip % 2


def device_at(place, core):
    x, y, z = place
    return (y * 4 + (z % 2) * 2 + core, x * 2 + z // 2)


def on_axis(place, axis, position):
    moved = list(place)
    moved[axis] = lax.rem(position + 4, 4)
    return tuple(moved)


def decoder_window(
    tiles, frames, cols,
    features, target_hbm, wq_hbm, wk_hbm, wv_hbm, wo_hbm, percept_hbm, weight_hbm,
    gain_hbm, bias_hbm, lpips_hbm, owner_hbm, frame_hbm, col_hbm,
    decoded_ref, out_ref, dist_out,
    weight, wq_ref, wk_ref, wv_ref, wo_ref, percept_ref, target_ref,
    gain_ref, bias_ref, lpips_ref, owner_ref, frame_ref, col_ref, feats, normed, stats, qs, acc, peak, total, hidden, hidden_t, other_h, own_g, other_g, rhs,
    part, left1, right1, comb, got, red1, got2, got3, quarter, dist_row, dist_pair,
    once, gather_recv, recv, local,
):
    place, core = chip_place()
    clip = lax.axis_index("clip")
    mine = lax.axis_index("tile")
    x, side = mine // 2, mine % 2
    cells = frames * cols
    width = feats.shape[-1]
    outputs = bias_ref.shape[-1]
    half = width // 2
    cut = cells // 2

    def tile_at(step, other):
        return lax.rem(x + step + 4, 4) * 2 + (side + other) % 2

    def peer(axis, step):
        return device_at(on_axis(place, axis, place[axis] + step), core)

    def remote(src, dst, sent_sem, got_sem, target):
        copy = pltpu.make_async_remote_copy(
            src_ref=src, dst_ref=dst, send_sem=sent_sem, recv_sem=got_sem,
            device_id=target, device_id_type=pl.DeviceIdType.MESH,
        )
        copy.start()
        return copy

    def take(rows, sem):
        pltpu.make_async_copy(rows, rows, sem).wait()

    own, left, right, opposite = (tile_at(step, 0) for step in (0, -1, 1, 2))
    partner, left2, right2, opposite2 = (tile_at(step, 1) for step in (0, -1, 1, 2))
    far = jnp.where(side == 0, left2, right2)
    near = jnp.where(side == 0, right2, left2)
    sibling = device_at(place, 1 - core)

    barrier = pltpu.get_barrier_semaphore()
    peers = [(clip, lax.rem(mine + step, tiles)) for step in range(1, tiles)]
    peers += [peer(1, 1), peer(1, 2), peer(1, 3), peer(2, 1), peer(2, 3), sibling]
    for other in peers:
        pl.semaphore_signal(barrier, inc=1, device_id=other, device_id_type=pl.DeviceIdType.MESH)
    load = pltpu.make_async_copy(features, feats.at[own], local.at[0])
    load.start()
    early = [
        pltpu.make_async_copy(source, ref, local.at[3 + i])
        for i, (source, ref) in enumerate(
            (
                (wq_hbm, wq_ref), (wk_hbm, wk_ref), (wv_hbm, wv_ref), (wo_hbm, wo_ref), (percept_hbm, percept_ref),
                (target_hbm, target_ref), (gain_hbm, gain_ref), (bias_hbm, bias_ref), (lpips_hbm, lpips_ref),
                (owner_hbm, owner_ref), (frame_hbm, frame_ref), (col_hbm, col_ref),
            )
        )
    ]
    for copy in early:
        copy.start()
    fetches = [
        pltpu.make_async_copy(weight_hbm.at[:, e], weight.at[:, :, pl.ds(e * outputs, outputs)], local.at[(1, 15, 16)[e]])
        for e in range(3)
    ]

    def pass_on(index, unit, h, to, mine_too=False):
        rows = feats.at[unit, pl.ds(h * cut, cut)]
        source = features.at[pl.ds(h * cut, cut)] if mine_too else rows
        return remote(source, rows, once.at[2], gather_recv.at[index], (clip, to))

    links = {}
    pl.semaphore_wait(barrier, len(peers))
    links["l0"] = pass_on(1, own, 0, right, True)
    links["r1"] = pass_on(2, own, 1, left, True)
    links["z0"] = pass_on(0, own, 0, partner, True)

    load.wait()
    wide = feats[own].astype(F32)
    stats[own] = jnp.concatenate(
        [jnp.sum(wide, axis=0, keepdims=True), jnp.sum(wide * wide, axis=0, keepdims=True), jnp.zeros((6, width), F32)],
        axis=0,
    )
    for step in range(tiles - 1):
        remote(stats.at[own], stats.at[own], once.at[0], once.at[1], peers[step])
    links["l1"] = pass_on(4, own, 1, right, True)
    links["r0"] = pass_on(5, own, 0, left, True)
    links["z1"] = pass_on(3, own, 1, partner, True)
    for copy in fetches:
        copy.start()

    lane = lax.broadcasted_iota(jnp.int32, (width, width), 0) // (width // GROUPS)
    same = (lane == lax.broadcasted_iota(jnp.int32, (width, width), 1) // (width // GROUPS)).astype(BF16)
    links["l0"].wait_recv()
    links["o0"] = pass_on(6, left, 0, right)
    links["r1"].wait_recv()
    links["o1"] = pass_on(7, right, 1, left)
    links["z0"].wait_recv()
    links["l2"] = pass_on(8, partner, 0, right)
    links["r2"] = pass_on(11, partner, 0, left)
    take(stats.at[pl.ds(0, tiles - 1)], once.at[1])
    sums = stats[0]
    for i in range(1, tiles):
        sums = sums + stats[i]
    pieces, rest = [], sums
    for _ in range(3):
        pieces.append(rest.astype(BF16))
        rest = rest - pieces[-1].astype(F32)
    grouped = dot(pieces[0], same) + dot(pieces[1], same) + dot(pieces[2], same)
    count = F32(tiles * cells * (width // GROUPS))
    mean = grouped[0:1] / count
    spread = grouped[1:2] / count - mean * mean
    scale = lax.rsqrt(spread + EPSILON)
    for copy in early:
        copy.wait()
    gain = gain_ref[...]
    factor = math.log2(math.e) / math.sqrt(width)

    def normalize(slot, unit):
        normed[slot * cells : (slot + 1) * cells, :] = (((feats[unit].astype(F32) - mean) * scale) * gain).astype(BF16)

    def make_queries(role, slot):
        q = dot(normed[slot * cells : (slot + 1) * cells, :], wq_ref[...]).astype(BF16)
        qs[role * cells : (role + 1) * cells, :] = (dot_nt(q, wk_ref[...]) * factor).astype(BF16)

    def attend(roles, slots, first):
        here = slice(roles[0] * cells, roles[1] * cells)
        keys = normed[slots[0] * cells : slots[1] * cells, :]
        s = dot_nt(qs[here, :], keys)
        groups = [s[:, j : j + 128] for j in range(0, s.shape[1], 128)]
        top = jnp.max(functools.reduce(jnp.maximum, groups), axis=1, keepdims=True)
        new = jnp.broadcast_to(top, (s.shape[0], 128)) if first else jnp.maximum(peak[here, :], top)
        raised = [jnp.exp2(group - new) for group in groups]
        lanes = functools.reduce(jnp.add, raised)
        out = dot(jnp.concatenate([group.astype(BF16) for group in raised], axis=1), keys)
        if first:
            total[here, :] = lanes
            acc[here, :] = out
        else:
            fade = jnp.exp2(peak[here, :] - new)
            total[here, :] = total[here, :] * fade + lanes
            for j in range(0, width, 128):
                acc[here, j : j + 128] = acc[here, j : j + 128] * fade + out[:, j : j + 128]
        peak[here, :] = new

    normalize(0, own)
    make_queries(0, 0)
    links["z1"].wait_recv()
    links["r3"] = pass_on(9, partner, 1, left)
    links["l3"] = pass_on(10, partner, 1, right)
    normalize(1, partner)
    make_queries(1, 1)
    links["l1"].wait_recv()
    links["r0"].wait_recv()
    normalize(2, left)
    normalize(3, right)
    attend((0, 1), (0, 4), True)
    links["o0"].wait_recv()
    links["p0"] = pass_on(12, opposite, 0, partner)
    links["o1"].wait_recv()
    links["p1"] = pass_on(13, opposite, 1, partner)
    attend((1, 2), (0, 4), True)
    normalize(4, opposite)
    attend((0, 2), (4, 5), False)
    table = percept_ref[...]
    zt = dot(target_ref[...], table)
    mt, _ = gelu_parts(zt)
    st = lax.rsqrt(jnp.mean(mt * mt, axis=-1, keepdims=True) + EPSILON)
    seen = mt * st
    spot = lax.broadcasted_iota(jnp.int32, (cols, 1), 0)
    col = col_ref[...]
    inside = (spot >= col) & (spot < col + CROPW) & (owner_ref[...] == mine)
    covers = [(inside & (frame_ref[...] == f)).astype(F32) for f in range(frames)]
    links["l2"].wait_recv()
    links["r3"].wait_recv()
    links["l3"].wait_recv()
    links["r2"].wait_recv()
    normalize(5, far)
    normalize(6, near)
    make_queries(2, 5)
    attend((2, 3), (0, 5), True)
    attend((0, 3), (5, 7), False)
    links["p0"].wait_recv()
    links["p1"].wait_recv()
    normalize(7, opposite2)
    attend((0, 3), (7, 8), False)

    for role, unit, b in ((0, own, 1), (1, partner, 2 - 2 * side), (2, far, 2 * side)):
        here = slice(role * cells, (role + 1) * cells)
        whole = 1.0 / jnp.sum(total[here, :], axis=1, keepdims=True)
        context = (acc[here, :] * whole).astype(BF16)
        mixed = dot(context, wv_ref[...]).astype(BF16)
        row = feats[unit].astype(F32) + dot(mixed, wo_ref[...])
        inside = (mine + b >= 1) & (mine + b <= tiles)
        row = jnp.where(inside, row, 0.0).astype(BF16)
        hidden[b] = row
        hidden_t[b] = row.T

    swap_h = remote(
        hidden_t.at[:, pl.ds(pl.multiple_of((1 - core) * half, half), half)], other_h, once.at[3], once.at[4], sibling
    )
    for copy in fetches:
        copy.wait()

    a2, a1, a0 = (
        sum(dot(hidden[b, : (a + 1) * cols, :], weight[a * 3 + b]) for b in range(3)) for a in (2, 1, 0)
    )
    wide_sum = a2 + jnp.concatenate([a1[:cols], a1], axis=0) + jnp.concatenate([a0, a0, a0], axis=0)
    sides = [wide_sum[:, e * outputs : (e + 1) * outputs] for e in range(3)]
    made = shift_rows(sides[0], 1, cols) + sides[1] + shift_rows(sides[2], -1, cols) + bias_ref[...]
    made = made.astype(BF16)
    decoded_ref[...] = made

    lw = lpips_ref[...]
    z = dot(made, table)
    m, t = gelu_parts(z)
    s = lax.rsqrt(jnp.mean(m * m, axis=-1, keepdims=True) + EPSILON)
    gap = m * s - seen
    weighted = gap * lw
    apart = jnp.sum(weighted * gap, axis=-1, keepdims=True)
    up = weighted * (2.0 / CROPW)
    dm = up * s - m * (s * s * s) * (jnp.sum(up * m, axis=-1, keepdims=True) / outputs)
    dz = dm * gelu_slope(z, t)
    high = dz.astype(BF16)
    low = (dz - high.astype(F32)).astype(BF16)
    pull = (dot_nt(high, table) + dot_nt(low, table)).astype(BF16).astype(F32)

    distance = jnp.zeros((1, col.shape[1]), F32)
    for f in range(frames):
        cover = covers[f]
        rows = slice(f * cols, (f + 1) * cols)
        distance = distance + jnp.sum(cover * apart[rows], axis=0, keepdims=True)
        own_g[rows, :] = (pull[rows] * jnp.sum(cover, axis=1, keepdims=True)).astype(BF16)
    dist_row[3] = jnp.broadcast_to(distance / CROPW, dist_row.shape[1:])
    swap_g = remote(own_g, other_g, once.at[5], once.at[6], sibling)
    for step in (1, 2, 3):
        remote(dist_row.at[3], dist_row.at[step - 1], once.at[7], once.at[8], peer(0, step))

    mixes = (
        lambda g: [g[0] + g[1] + g[2]],
        lambda g: [g[0] + g[1], g[2]],
        lambda g: g,
    )

    def line_up(ref, place_in):
        g = [ref[f * cols : (f + 1) * cols, :].astype(F32) for f in range(frames)]
        for p in range(3):
            mixed = jnp.concatenate(mixes[p](g), axis=0)
            depth = mixed.shape[0]
            for e, moved in enumerate((shift_rows(mixed, -1, cols), mixed, shift_rows(mixed, 1, cols))):
                rhs[p, place_in * depth : (place_in + 1) * depth, e * outputs : (e + 1) * outputs] = moved.astype(BF16)

    line_up(own_g, 0)
    swap_g.wait_recv()
    line_up(other_g, 1)
    swap_h.wait_recv()

    quarter_rows = quarter.shape[1]
    half_rows = quarter_rows // 2
    piece = quarter_rows // 4
    chunk_rows = 4 * quarter_rows
    own_half = pl.ds(pl.multiple_of(core * half, half), half)

    def chunk_at(b, q, h, count=1):
        return pl.ds(pl.multiple_of(b * chunk_rows + lax.rem(q + 4, 4) * quarter_rows + h * half_rows, 16), half_rows * count)

    def out_rows(p, b, q, h, count=1):
        return out_ref.at[core, p, chunk_at(b, q, h, count)]

    def go(c, stage, src, dst, to):
        remote(src, dst, once.at[9 if stage < 5 else 10], recv.at[c, stage], to)

    def across_to(src, dst):
        remote(src, dst, once.at[10], once.at[11], sibling)

    def make(b):
        for p in range(3):
            c, m, depth = p * 3 + b, place[p], (p + 1) * cols
            lhs = jnp.concatenate([hidden_t[b, own_half, :depth], other_h[b, :, :depth]], axis=1)
            made_wide = dot(lhs, rhs[p, : 2 * depth, :])
            for e in range(3):
                base = b * chunk_rows + e * half
                part[p, base : base + half, :] = made_wide[:, e * outputs : (e + 1) * outputs].astype(BF16)
            go(c, 0, part.at[p, chunk_at(b, m + 2, 0)], left1.at[c], peer(p, 1))
            go(c, 0, part.at[p, chunk_at(b, m + 2, 1)], right1.at[c], peer(p, 3))
            go(c, 1, part.at[p, chunk_at(b, m + 1, 1)], got.at[c, 0, pl.ds(half_rows, half_rows)], peer(p, 1))
            go(c, 1, part.at[p, chunk_at(b, m - 1, 0)], got.at[c, 1, pl.ds(0, half_rows)], peer(p, 3))

    def ring(b):
        for p in range(3):
            c, m = p * 3 + b, place[p]
            take(comb.at[c], recv.at[c, 0])
            for way, arrived, q, step in ((0, left1, m + 1, 1), (1, right1, m - 1, 3)):
                comb[c, way] = (part[p, chunk_at(b, q, way), :].astype(F32) + arrived[c].astype(F32)).astype(BF16)
                go(c, 1, comb.at[c, way], got.at[c, way, pl.ds(way * half_rows, half_rows)], peer(p, step))

    def direct(b):
        for p in range(3):
            c, axis = p * 3 + b, (p + 1) % 3
            take(got.at[c], recv.at[c, 1])
            mine_rows = part[p, chunk_at(b, place[p], 0, 2), :].astype(F32)
            red1[c] = (mine_rows + got[c, 0].astype(F32) + got[c, 1].astype(F32)).astype(BF16)
            for step in (1, 2, 3):
                to = lax.rem(place[axis] + step, 4)
                go(c, 2, red1.at[c, pl.ds(pl.multiple_of(to * piece, 16), piece)], got2.at[c, step - 1], peer(axis, step))

    def to_all(b):
        for p in range(3):
            c, axis, here = p * 3 + b, (p + 2) % 3, place[(p + 1) % 3]
            take(got2.at[c], recv.at[c, 2])
            added = red1[c, pl.ds(pl.multiple_of(here * piece, 16), piece), :].astype(F32)
            for i in range(3):
                added = added + got2[c, i].astype(F32)
            got3[c, place[axis]] = added.astype(BF16)
            for step in (1, 2, 3):
                slot = got3.at[c, place[axis]]
                go(c, 3, slot, slot, peer(axis, step))

    def back(b):
        for p in range(3):
            c, axis = p * 3 + b, (p + 1) % 3
            take(got2.at[c], recv.at[c, 3])
            whole = got3[c, 0].astype(F32)
            for i in range(1, 4):
                whole = whole + got3[c, i].astype(F32)
            rows = pl.ds(pl.multiple_of(place[axis] * piece, 16), piece)
            quarter[c, rows, :] = whole.astype(BF16)
            for step in (1, 2, 3):
                slot = quarter.at[c, rows]
                go(c, 4, slot, slot, peer(axis, step))

    def spread_out(b):
        for p in range(3):
            c, m = p * 3 + b, place[p]
            take(got2.at[c], recv.at[c, 4])
            for stage, h, step in ((5, 0, 1), (5, 1, 3), (6, 1, 1), (6, 0, 3)):
                go(c, stage, quarter.at[c, pl.ds(h * half_rows, half_rows)], out_rows(p, b, m, h), peer(p, step))
            across_to(quarter.at[c], out_rows(p, b, m, 0, 2))
            pltpu.make_async_copy(quarter.at[c], out_rows(p, b, m, 0, 2), local.at[2]).start()

    def forward(b):
        for p in range(3):
            c, m = p * 3 + b, place[p]
            take(quarter.at[c], recv.at[c, 5])
            for h, q, step in ((0, m - 1, 1), (1, m + 1, 3)):
                go(c, 7, out_rows(p, b, q, h), out_rows(p, b, q, h), peer(p, step))

    def across(b):
        for p in range(3):
            c, m = p * 3 + b, place[p]
            take(quarter.at[c], recv.at[c, 6])
            for q in (m - 1, m + 1):
                across_to(out_rows(p, b, q, 0, 2), out_rows(p, b, q, 0, 2))

    def across_last(b):
        for p in range(3):
            c, m = p * 3 + b, place[p]
            take(quarter.at[c], recv.at[c, 7])
            across_to(out_rows(p, b, m + 2, 0, 2), out_rows(p, b, m + 2, 0, 2))

    make(0)
    make(1)
    ring(0)
    make(2)
    ring(1)

    take(dist_row.at[pl.ds(0, 3)], once.at[8])
    dist_pair[0] = dist_row[0] + dist_row[1] + dist_row[2] + dist_row[3]
    pair = remote(dist_pair.at[0], dist_pair.at[1], once.at[12], once.at[13], peer(2, 2))

    ring(2)
    for stage in (direct, to_all, back, spread_out, forward, across, across_last):
        for b in range(3):
            stage(b)

    pair.wait()
    crops, scored = dist_pair.shape[2], dist_out.shape[1]
    pick = lax.broadcasted_iota(jnp.int32, (crops, scored), 0) == (
        mine * scored + lax.broadcasted_iota(jnp.int32, (crops, scored), 1)
    )
    dist_out[...] = jnp.dot(
        dist_pair[0] + dist_pair[1], pick.astype(F32), precision=lax.Precision.HIGHEST, preferred_element_type=F32
    )[0:1]
    take(out_ref.at[1 - core], once.at[11])
    take(quarter, local.at[2])
    take(stats.at[pl.ds(0, tiles - 1)], once.at[0])
    take(feats.at[pl.ds(0, 7)], once.at[2])
    take(dist_row.at[pl.ds(0, 3)], once.at[7])
    take(weight.at[:, pl.ds(0, 9 * 21 * half_rows // 54)], once.at[9])
    take(weight.at[:, pl.ds(0, 9 * 14 * half_rows // 27)], once.at[10])
    swap_g.wait_send()
    swap_h.wait_send()


def widen(halves, made, scored, out_hbm, made_out, scored_out, near, wide, in_sems, out_sems, hand_sems):
    hand_on = [
        pltpu.make_async_copy(made, made_out, hand_sems.at[0]),
        pltpu.make_async_copy(scored, scored_out, hand_sems.at[1]),
    ]
    taps, half = halves.shape[1:3]
    steps = in_sems.shape[0]
    count = taps // steps
    pieces = [pl.ds(i * count, count) for i in range(steps)]
    loads = [pltpu.make_async_copy(halves.at[:, rows], near.at[:, rows], in_sems.at[i]) for i, rows in enumerate(pieces)]
    stores = [pltpu.make_async_copy(wide.at[rows], out_hbm.at[rows], out_sems.at[i]) for i, rows in enumerate(pieces)]
    for copy in loads + hand_on:
        copy.start()
    for i in range(steps):
        loads[i].wait()
        for tap in range(i * count, (i + 1) * count):
            for h in range(2):
                wide[tap, h * half : (h + 1) * half, :] = near[h, tap].astype(F32)
        stores[i].start()
    for copy in stores + hand_on:
        copy.wait()


def on_device(
    features, target, gn_gain, attn_query, attn_key, attn_value, attn_out, conv_weight, conv_bias,
    percept, lpips_weight, crop_owner, crop_frame, crop_col,
):
    tiles = lax.axis_size("tile")
    frames, rows_dev, cols, width = features.shape[1:]
    outputs = conv_weight.shape[-1]
    cells = frames * rows_dev * cols
    taps = 27
    half = width // 2
    part_rows = taps // 3 * half
    quarter = part_rows // 12
    crops = crop_col.shape[1]
    vmem = pl.BlockSpec(memory_space=pltpu.VMEM)
    hbm = pl.BlockSpec(memory_space=pl.ANY)
    sems = lambda count: pltpu.SemaphoreType.DMA((count,))
    decoded, summed, distances = pl.pallas_call(
        functools.partial(decoder_window, tiles, frames, cols),
        in_specs=[hbm] * 14,
        out_specs=[vmem, hbm, vmem],
        out_shape=[
            jax.ShapeDtypeStruct((cells, outputs), BF16),
            jax.ShapeDtypeStruct((2, 3, part_rows, outputs), BF16),
            jax.ShapeDtypeStruct((1, crops // tiles), F32),
        ],
        scratch_shapes=[
            pltpu.VMEM((9, width, 3 * outputs), BF16),
            pltpu.VMEM((width, width), BF16),
            pltpu.VMEM((width, width), BF16),
            pltpu.VMEM((width, width), BF16),
            pltpu.VMEM((width, width), BF16),
            pltpu.VMEM((outputs, outputs), BF16),
            pltpu.VMEM((cells, outputs), BF16),
            pltpu.VMEM((1, width), F32),
            pltpu.VMEM((1, outputs), F32),
            pltpu.VMEM((1, outputs), F32),
            pltpu.VMEM((1, crops), jnp.int32),
            pltpu.VMEM((1, crops), jnp.int32),
            pltpu.VMEM((1, crops), jnp.int32),
            pltpu.VMEM((tiles, cells, width), BF16),
            pltpu.VMEM((tiles * cells, width), BF16),
            pltpu.VMEM((tiles, 8, width), F32),
            pltpu.VMEM((3 * cells, width), BF16),
            pltpu.VMEM((3 * cells, width), F32),
            pltpu.VMEM((3 * cells, 128), F32),
            pltpu.VMEM((3 * cells, 128), F32),
            pltpu.VMEM((3, cells, width), BF16),
            pltpu.VMEM((3, width, cells), BF16),
            pltpu.VMEM((3, half, cells), BF16),
            pltpu.VMEM((cells, outputs), BF16),
            pltpu.VMEM((cells, outputs), BF16),
            pltpu.VMEM((3, 2 * cells, 3 * outputs), BF16),
            pltpu.VMEM((3, part_rows, outputs), BF16),
            pltpu.VMEM((9, quarter // 2, outputs), BF16),
            pltpu.VMEM((9, quarter // 2, outputs), BF16),
            pltpu.VMEM((9, 2, quarter // 2, outputs), BF16),
            pltpu.VMEM((9, 2, quarter, outputs), BF16),
            pltpu.VMEM((9, quarter, outputs), BF16),
            pltpu.VMEM((9, 3, quarter // 4, outputs), BF16),
            pltpu.VMEM((9, 4, quarter // 4, outputs), BF16),
            pltpu.VMEM((9, quarter, outputs), BF16),
            pltpu.VMEM((4, 8, crops), F32),
            pltpu.VMEM((2, 8, crops), F32),
            sems(14), sems(14), pltpu.SemaphoreType.DMA((9, 8)), sems(17),
        ],
        compiler_params=pltpu.CompilerParams(
            collective_id=1, has_side_effects=True, vmem_limit_bytes=60 * 1024 * 1024
        ),
        cost_estimate=pl.CostEstimate(flops=14_000_000_000, bytes_accessed=24_000_000, transcendentals=4_000_000),
        name="decoder_window",
    )(
        features.reshape(cells, width), target.reshape(cells, outputs), attn_query, attn_key, attn_value, attn_out,
        percept, conv_weight.reshape(9, 3, width, outputs), gn_gain[None, :], conv_bias[None, :], lpips_weight[None, :],
        crop_owner.reshape(1, -1), crop_frame, crop_col,
    )
    conv_total, decoded, distances = pl.pallas_call(
        widen,
        in_specs=[hbm] * 3,
        out_specs=[hbm] * 3,
        out_shape=[
            jax.ShapeDtypeStruct((taps, width, outputs), F32),
            jax.ShapeDtypeStruct(decoded.shape, BF16),
            jax.ShapeDtypeStruct(distances.shape, F32),
        ],
        scratch_shapes=[pltpu.VMEM((2, taps, half, outputs), BF16), pltpu.VMEM((taps, width, outputs), F32), sems(9), sems(9), sems(2)],
        compiler_params=pltpu.CompilerParams(vmem_limit_bytes=60 * 1024 * 1024),
        name="widen",
    )(summed.reshape(2, taps, half, outputs), decoded, distances)
    conv_total = conv_total.reshape(conv_weight.shape)
    return (decoded.reshape(1, frames, rows_dev, cols, outputs), conv_total, distances)


def solution(mesh):
    return jax.shard_map(
        on_device,
        mesh=mesh,
        in_specs=(
            P("clip", None, "tile", None, None),
            P("clip", None, "tile", None, None),
            P(), P(), P(), P(), P(), P(), P(), P(), P(),
            P("clip", None, None),
            P("clip", None),
            P("clip", None),
        ),
        out_specs=(P("clip", None, "tile", None, None), P(), P("clip", "tile")),
        check_vma=False,
    )
```

```python
import functools
import math

import jax
import jax.numpy as jnp
from jax import lax
from jax.experimental import pallas as pl
from jax.experimental.pallas import tpu as pltpu
from jax.sharding import PartitionSpec as P

GROUPS = 32
CROPW = 64
EPSILON = 1e-06
F32 = jnp.float32
BF16 = jnp.bfloat16


def dot(a, b):
    return jnp.dot(a, b, preferred_element_type=F32)


def dot_nt(a, b):
    return lax.dot_general(a, b, (((1,), (1,)), ((), ())), preferred_element_type=F32)


def dot_tn(a, b):
    return lax.dot_general(a, b, (((0,), (0,)), ((), ())), preferred_element_type=F32)


def gelu_parts(z):
    k = math.sqrt(2.0 / math.pi)
    t = jnp.tanh(k * (z + 0.044715 * (z * z * z)))
    return 0.5 * z * (1.0 + t), t


def gelu_slope(z, t):
    k = math.sqrt(2.0 / math.pi)
    return 0.5 * (1.0 + t) + 0.5 * z * (1.0 - t * t) * (k * (1.0 + 3.0 * 0.044715 * (z * z)))


def shift_rows(value, step, cols):
    count = value.shape[0]
    place = lax.broadcasted_iota(jnp.int32, (count, 1), 0) % cols
    if step > 0:
        return jnp.where(place == 0, 0.0, pltpu.roll(value, 1, 0))
    return jnp.where(place == cols - 1, 0.0, pltpu.roll(value, count - 1, 0))


def chip_place():
    clip = lax.axis_index("clip")
    tile = lax.axis_index("tile")
    return (tile // 2, clip // 4, (tile % 2) * 2 + (clip // 2) % 2), clip % 2


def device_at(place, core):
    x, y, z = place
    return (y * 4 + (z % 2) * 2 + core, x * 2 + z // 2)


def on_axis(place, axis, position):
    moved = list(place)
    moved[axis] = lax.rem(position + 4, 4)
    return tuple(moved)


def decoder_window(
    tiles, frames, cols,
    features, target_hbm, wq_hbm, wk_hbm, wv_hbm, wo_hbm, percept_hbm, weight_hbm,
    gain_hbm, bias_hbm, lpips_hbm, owner_hbm, frame_hbm, col_hbm,
    decoded_ref, out_ref, dist_out,
    weight, wq_ref, wk_ref, wv_ref, wo_ref, percept_ref, target_ref,
    gain_ref, bias_ref, lpips_ref, owner_ref, frame_ref, col_ref, feats, normed, stats, qs, acc, peak, total, hidden, hidden_t, other_h, own_g, other_g, rhs,
    part, left1, right1, comb, got, red1, got2, got3, quarter, dist_row, dist_pair,
    once, gather_recv, recv, local,
):
    place, core = chip_place()
    clip = lax.axis_index("clip")
    mine = lax.axis_index("tile")
    x, side = mine // 2, mine % 2
    cells = frames * cols
    width = feats.shape[-1]
    outputs = bias_ref.shape[-1]
    half = width // 2
    cut = cells // 2

    def tile_at(step, other):
        return lax.rem(x + step + 4, 4) * 2 + (side + other) % 2

    def peer(axis, step):
        return device_at(on_axis(place, axis, place[axis] + step), core)

    def remote(src, dst, sent_sem, got_sem, target):
        copy = pltpu.make_async_remote_copy(
            src_ref=src, dst_ref=dst, send_sem=sent_sem, recv_sem=got_sem,
            device_id=target, device_id_type=pl.DeviceIdType.MESH,
        )
        copy.start()
        return copy

    def take(rows, sem):
        pltpu.make_async_copy(rows, rows, sem).wait()

    own, left, right, opposite = (tile_at(step, 0) for step in (0, -1, 1, 2))
    partner, left2, right2, opposite2 = (tile_at(step, 1) for step in (0, -1, 1, 2))
    far = jnp.where(side == 0, left2, right2)
    near = jnp.where(side == 0, right2, left2)
    sibling = device_at(place, 1 - core)

    barrier = pltpu.get_barrier_semaphore()
    peers = [(clip, lax.rem(mine + step, tiles)) for step in range(1, tiles)]
    peers += [peer(1, 1), peer(1, 2), peer(1, 3), peer(2, 1), peer(2, 3), sibling]
    for other in peers:
        pl.semaphore_signal(barrier, inc=1, device_id=other, device_id_type=pl.DeviceIdType.MESH)
    load = pltpu.make_async_copy(features, feats.at[own], local.at[0])
    load.start()
    early = [
        pltpu.make_async_copy(source, ref, local.at[3 + i])
        for i, (source, ref) in enumerate(
            (
                (wq_hbm, wq_ref), (wk_hbm, wk_ref), (wv_hbm, wv_ref), (wo_hbm, wo_ref), (percept_hbm, percept_ref),
                (target_hbm, target_ref), (gain_hbm, gain_ref), (bias_hbm, bias_ref), (lpips_hbm, lpips_ref),
                (owner_hbm, owner_ref), (frame_hbm, frame_ref), (col_hbm, col_ref),
            )
        )
    ]
    for copy in early:
        copy.start()
    fetches = [
        pltpu.make_async_copy(weight_hbm.at[:, e], weight.at[:, :, pl.ds(e * outputs, outputs)], local.at[(1, 15, 16)[e]])
        for e in range(3)
    ]

    def pass_on(index, unit, h, to, mine_too=False):
        rows = feats.at[unit, pl.ds(h * cut, cut)]
        source = features.at[pl.ds(h * cut, cut)] if mine_too else rows
        return remote(source, rows, once.at[2], gather_recv.at[index], (clip, to))

    links = {}
    pl.semaphore_wait(barrier, len(peers))
    links["l0"] = pass_on(1, own, 0, right, True)
    links["r1"] = pass_on(2, own, 1, left, True)
    links["z0"] = pass_on(0, own, 0, partner, True)

    load.wait()
    wide = feats[own].astype(F32)
    stats[own] = jnp.concatenate(
        [jnp.sum(wide, axis=0, keepdims=True), jnp.sum(wide * wide, axis=0, keepdims=True), jnp.zeros((6, width), F32)],
        axis=0,
    )
    for step in range(tiles - 1):
        remote(stats.at[own], stats.at[own], once.at[0], once.at[1], peers[step])
    links["l1"] = pass_on(4, own, 1, right, True)
    links["r0"] = pass_on(5, own, 0, left, True)
    links["z1"] = pass_on(3, own, 1, partner, True)
    for copy in fetches:
        copy.start()

    lane = lax.broadcasted_iota(jnp.int32, (width, width), 0) // (width // GROUPS)
    same = (lane == lax.broadcasted_iota(jnp.int32, (width, width), 1) // (width // GROUPS)).astype(BF16)
    links["l0"].wait_recv()
    links["o0"] = pass_on(6, left, 0, right)
    links["r1"].wait_recv()
    links["o1"] = pass_on(7, right, 1, left)
    links["z0"].wait_recv()
    links["l2"] = pass_on(8, partner, 0, right)
    links["r2"] = pass_on(11, partner, 0, left)
    take(stats.at[pl.ds(0, tiles - 1)], once.at[1])
    sums = stats[0]
    for i in range(1, tiles):
        sums = sums + stats[i]
    pieces, rest = [], sums
    for _ in range(3):
        pieces.append(rest.astype(BF16))
        rest = rest - pieces[-1].astype(F32)
    grouped = dot(pieces[0], same) + dot(pieces[1], same) + dot(pieces[2], same)
    count = F32(tiles * cells * (width // GROUPS))
    mean = grouped[0:1] / count
    spread = grouped[1:2] / count - mean * mean
    scale = lax.rsqrt(spread + EPSILON)
    for copy in early:
        copy.wait()
    gain = gain_ref[...]
    factor = math.log2(math.e) / math.sqrt(width)

    def normalize(slot, unit):
        normed[slot * cells : (slot + 1) * cells, :] = (((feats[unit].astype(F32) - mean) * scale) * gain).astype(BF16)

    def make_queries(role, slot):
        q = dot(normed[slot * cells : (slot + 1) * cells, :], wq_ref[...]).astype(BF16)
        qs[role * cells : (role + 1) * cells, :] = (dot_nt(q, wk_ref[...]) * factor).astype(BF16)

    def attend(roles, slots, first):
        here = slice(roles[0] * cells, roles[1] * cells)
        keys = normed[slots[0] * cells : slots[1] * cells, :]
        s = dot_nt(qs[here, :], keys)
        groups = [s[:, j : j + 128] for j in range(0, s.shape[1], 128)]
        top = jnp.max(functools.reduce(jnp.maximum, groups), axis=1, keepdims=True)
        new = jnp.broadcast_to(top, (s.shape[0], 128)) if first else jnp.maximum(peak[here, :], top)
        raised = [jnp.exp2(group - new) for group in groups]
        lanes = functools.reduce(jnp.add, raised)
        out = dot(jnp.concatenate([group.astype(BF16) for group in raised], axis=1), keys)
        if first:
            total[here, :] = lanes
            acc[here, :] = out
        else:
            fade = jnp.exp2(peak[here, :] - new)
            total[here, :] = total[here, :] * fade + lanes
            for j in range(0, width, 128):
                acc[here, j : j + 128] = acc[here, j : j + 128] * fade + out[:, j : j + 128]
        peak[here, :] = new

    normalize(0, own)
    make_queries(0, 0)
    links["z1"].wait_recv()
    links["r3"] = pass_on(9, partner, 1, left)
    links["l3"] = pass_on(10, partner, 1, right)
    normalize(1, partner)
    make_queries(1, 1)
    links["l1"].wait_recv()
    links["r0"].wait_recv()
    normalize(2, left)
    normalize(3, right)
    attend((0, 1), (0, 4), True)
    links["o0"].wait_recv()
    links["p0"] = pass_on(12, opposite, 0, partner)
    links["o1"].wait_recv()
    links["p1"] = pass_on(13, opposite, 1, partner)
    attend((1, 2), (0, 4), True)
    normalize(4, opposite)
    attend((0, 2), (4, 5), False)
    table = percept_ref[...]
    zt = dot(target_ref[...], table)
    mt, _ = gelu_parts(zt)
    st = lax.rsqrt(jnp.mean(mt * mt, axis=-1, keepdims=True) + EPSILON)
    seen = mt * st
    spot = lax.broadcasted_iota(jnp.int32, (cols, 1), 0)
    col = col_ref[...]
    inside = (spot >= col) & (spot < col + CROPW) & (owner_ref[...] == mine)
    covers = [(inside & (frame_ref[...] == f)).astype(F32) for f in range(frames)]
    links["l2"].wait_recv()
    links["r3"].wait_recv()
    links["l3"].wait_recv()
    links["r2"].wait_recv()
    normalize(5, far)
    normalize(6, near)
    make_queries(2, 5)
    attend((2, 3), (0, 5), True)
    attend((0, 3), (5, 7), False)
    links["p0"].wait_recv()
    links["p1"].wait_recv()
    normalize(7, opposite2)
    attend((0, 3), (7, 8), False)

    for role, unit, b in ((0, own, 1), (1, partner, 2 - 2 * side), (2, far, 2 * side)):
        here = slice(role * cells, (role + 1) * cells)
        whole = 1.0 / jnp.sum(total[here, :], axis=1, keepdims=True)
        context = (acc[here, :] * whole).astype(BF16)
        mixed = dot(context, wv_ref[...]).astype(BF16)
        row = feats[unit].astype(F32) + dot(mixed, wo_ref[...])
        inside = (mine + b >= 1) & (mine + b <= tiles)
        row = jnp.where(inside, row, 0.0).astype(BF16)
        hidden[b] = row
        hidden_t[b] = row.T

    swap_h = remote(
        hidden_t.at[:, pl.ds(pl.multiple_of((1 - core) * half, half), half)], other_h, once.at[3], once.at[4], sibling
    )
    for copy in fetches:
        copy.wait()

    a2, a1, a0 = (
        sum(dot(hidden[b, : (a + 1) * cols, :], weight[a * 3 + b]) for b in range(3)) for a in (2, 1, 0)
    )
    wide_sum = a2 + jnp.concatenate([a1[:cols], a1], axis=0) + jnp.concatenate([a0, a0, a0], axis=0)
    sides = [wide_sum[:, e * outputs : (e + 1) * outputs] for e in range(3)]
    made = shift_rows(sides[0], 1, cols) + sides[1] + shift_rows(sides[2], -1, cols) + bias_ref[...]
    made = made.astype(BF16)
    decoded_ref[...] = made

    lw = lpips_ref[...]
    z = dot(made, table)
    m, t = gelu_parts(z)
    s = lax.rsqrt(jnp.mean(m * m, axis=-1, keepdims=True) + EPSILON)
    gap = m * s - seen
    weighted = gap * lw
    apart = jnp.sum(weighted * gap, axis=-1, keepdims=True)
    up = weighted * (2.0 / CROPW)
    dm = up * s - m * (s * s * s) * (jnp.sum(up * m, axis=-1, keepdims=True) / outputs)
    dz = dm * gelu_slope(z, t)
    high = dz.astype(BF16)
    low = (dz - high.astype(F32)).astype(BF16)
    pull = (dot_nt(high, table) + dot_nt(low, table)).astype(BF16).astype(F32)

    distance = jnp.zeros((1, col.shape[1]), F32)
    for f in range(frames):
        cover = covers[f]
        rows = slice(f * cols, (f + 1) * cols)
        distance = distance + jnp.sum(cover * apart[rows], axis=0, keepdims=True)
        own_g[rows, :] = (pull[rows] * jnp.sum(cover, axis=1, keepdims=True)).astype(BF16)
    dist_row[3] = jnp.broadcast_to(distance / CROPW, dist_row.shape[1:])
    swap_g = remote(own_g, other_g, once.at[5], once.at[6], sibling)
    for step in (1, 2, 3):
        remote(dist_row.at[3], dist_row.at[step - 1], once.at[7], once.at[8], peer(0, step))

    mixes = (
        lambda g: [g[0] + g[1] + g[2]],
        lambda g: [g[0] + g[1], g[2]],
        lambda g: g,
    )

    def line_up(ref, place_in):
        g = [ref[f * cols : (f + 1) * cols, :].astype(F32) for f in range(frames)]
        for p in range(3):
            mixed = jnp.concatenate(mixes[p](g), axis=0)
            depth = mixed.shape[0]
            for e, moved in enumerate((shift_rows(mixed, -1, cols), mixed, shift_rows(mixed, 1, cols))):
                rhs[p, place_in * depth : (place_in + 1) * depth, e * outputs : (e + 1) * outputs] = moved.astype(BF16)

    line_up(own_g, 0)
    swap_g.wait_recv()
    line_up(other_g, 1)
    swap_h.wait_recv()

    quarter_rows = quarter.shape[1]
    half_rows = quarter_rows // 2
    piece = quarter_rows // 4
    chunk_rows = 4 * quarter_rows
    own_half = pl.ds(pl.multiple_of(core * half, half), half)

    def chunk_at(b, q, h, count=1):
        return pl.ds(pl.multiple_of(b * chunk_rows + lax.rem(q + 4, 4) * quarter_rows + h * half_rows, 16), half_rows * count)

    def out_rows(p, b, q, h, count=1):
        return out_ref.at[core, p, chunk_at(b, q, h, count)]

    def go(c, stage, src, dst, to):
        remote(src, dst, once.at[9 if stage < 5 else 10], recv.at[c, stage], to)

    def across_to(src, dst):
        remote(src, dst, once.at[10], once.at[11], sibling)

    def make(b):
        for p in range(3):
            c, m, depth = p * 3 + b, place[p], (p + 1) * cols
            lhs = jnp.concatenate([hidden_t[b, own_half, :depth], other_h[b, :, :depth]], axis=1)
            made_wide = dot(lhs, rhs[p, : 2 * depth, :])
            for e in range(3):
                base = b * chunk_rows + e * half
                part[p, base : base + half, :] = made_wide[:, e * outputs : (e + 1) * outputs].astype(BF16)
            go(c, 0, part.at[p, chunk_at(b, m + 2, 0)], left1.at[c], peer(p, 1))
            go(c, 0, part.at[p, chunk_at(b, m + 2, 1)], right1.at[c], peer(p, 3))
            go(c, 1, part.at[p, chunk_at(b, m + 1, 1)], got.at[c, 0, pl.ds(half_rows, half_rows)], peer(p, 1))
            go(c, 1, part.at[p, chunk_at(b, m - 1, 0)], got.at[c, 1, pl.ds(0, half_rows)], peer(p, 3))

    def ring(b):
        for p in range(3):
            c, m = p * 3 + b, place[p]
            take(comb.at[c], recv.at[c, 0])
            for way, arrived, q, step in ((0, left1, m + 1, 1), (1, right1, m - 1, 3)):
                comb[c, way] = (part[p, chunk_at(b, q, way), :].astype(F32) + arrived[c].astype(F32)).astype(BF16)
                go(c, 1, comb.at[c, way], got.at[c, way, pl.ds(way * half_rows, half_rows)], peer(p, step))

    def direct(b):
        for p in range(3):
            c, axis = p * 3 + b, (p + 1) % 3
            take(got.at[c], recv.at[c, 1])
            mine_rows = part[p, chunk_at(b, place[p], 0, 2), :].astype(F32)
            red1[c] = (mine_rows + got[c, 0].astype(F32) + got[c, 1].astype(F32)).astype(BF16)
            for step in (2, 1, 3):
                to = lax.rem(place[axis] + step, 4)
                go(c, 2, red1.at[c, pl.ds(pl.multiple_of(to * piece, 16), piece)], got2.at[c, step - 1], peer(axis, step))

    def to_all(b):
        for p in range(3):
            c, axis, here = p * 3 + b, (p + 2) % 3, place[(p + 1) % 3]
            take(got2.at[c], recv.at[c, 2])
            added = red1[c, pl.ds(pl.multiple_of(here * piece, 16), piece), :].astype(F32)
            for i in range(3):
                added = added + got2[c, i].astype(F32)
            got3[c, place[axis]] = added.astype(BF16)
            for step in (2, 1, 3):
                slot = got3.at[c, place[axis]]
                go(c, 3, slot, slot, peer(axis, step))

    def back(b):
        for p in range(3):
            c, axis = p * 3 + b, (p + 1) % 3
            take(got2.at[c], recv.at[c, 3])
            whole = got3[c, 0].astype(F32)
            for i in range(1, 4):
                whole = whole + got3[c, i].astype(F32)
            rows = pl.ds(pl.multiple_of(place[axis] * piece, 16), piece)
            quarter[c, rows, :] = whole.astype(BF16)
            for step in (2, 1, 3):
                slot = quarter.at[c, rows]
                go(c, 4, slot, slot, peer(axis, step))

    def spread_out(b):
        for p in range(3):
            c, m = p * 3 + b, place[p]
            take(got2.at[c], recv.at[c, 4])
            for h, step in ((0, 1), (1, 3)):
                go(c, 5, quarter.at[c, pl.ds(h * half_rows, half_rows)], out_rows(p, b, m, h), peer(p, step))
        for p in range(3):
            c, m = p * 3 + b, place[p]
            for h, step in ((1, 1), (0, 3)):
                go(c, 6, quarter.at[c, pl.ds(h * half_rows, half_rows)], out_rows(p, b, m, h), peer(p, step))
        for p in range(3):
            c, m = p * 3 + b, place[p]
            across_to(quarter.at[c], out_rows(p, b, m, 0, 2))
            pltpu.make_async_copy(quarter.at[c], out_rows(p, b, m, 0, 2), local.at[2]).start()

    def forward(b):
        for p in range(3):
            c, m = p * 3 + b, place[p]
            take(quarter.at[c], recv.at[c, 5])
            for h, q, step in ((0, m - 1, 1), (1, m + 1, 3)):
                go(c, 7, out_rows(p, b, q, h), out_rows(p, b, q, h), peer(p, step))

    def across(b):
        for p in range(3):
            c, m = p * 3 + b, place[p]
            take(quarter.at[c], recv.at[c, 6])
            for q in (m - 1, m + 1):
                across_to(out_rows(p, b, q, 0, 2), out_rows(p, b, q, 0, 2))

    def across_last(b):
        for p in range(3):
            c, m = p * 3 + b, place[p]
            take(quarter.at[c], recv.at[c, 7])
            across_to(out_rows(p, b, m + 2, 0, 2), out_rows(p, b, m + 2, 0, 2))

    make(0)
    make(1)
    ring(0)
    make(2)
    ring(1)

    take(dist_row.at[pl.ds(0, 3)], once.at[8])
    dist_pair[0] = dist_row[0] + dist_row[1] + dist_row[2] + dist_row[3]
    pair = remote(dist_pair.at[0], dist_pair.at[1], once.at[12], once.at[13], peer(2, 2))

    ring(2)
    for stage in (direct, to_all, back, spread_out, forward, across, across_last):
        for b in range(3):
            stage(b)

    pair.wait()
    crops, scored = dist_pair.shape[2], dist_out.shape[1]
    pick = lax.broadcasted_iota(jnp.int32, (crops, scored), 0) == (
        mine * scored + lax.broadcasted_iota(jnp.int32, (crops, scored), 1)
    )
    dist_out[...] = jnp.dot(
        dist_pair[0] + dist_pair[1], pick.astype(F32), precision=lax.Precision.HIGHEST, preferred_element_type=F32
    )[0:1]
    take(out_ref.at[1 - core], once.at[11])
    take(quarter, local.at[2])
    take(stats.at[pl.ds(0, tiles - 1)], once.at[0])
    take(feats.at[pl.ds(0, 7)], once.at[2])
    take(dist_row.at[pl.ds(0, 3)], once.at[7])
    take(weight.at[:, pl.ds(0, 9 * 21 * half_rows // 54)], once.at[9])
    take(weight.at[:, pl.ds(0, 9 * 14 * half_rows // 27)], once.at[10])
    swap_g.wait_send()
    swap_h.wait_send()


def widen(halves, made, scored, out_hbm, made_out, scored_out, near, wide, in_sems, out_sems, hand_sems):
    hand_on = [
        pltpu.make_async_copy(made, made_out, hand_sems.at[0]),
        pltpu.make_async_copy(scored, scored_out, hand_sems.at[1]),
    ]
    taps, half = halves.shape[1:3]
    steps = in_sems.shape[0]
    count = taps // steps
    pieces = [pl.ds(i * count, count) for i in range(steps)]
    loads = [pltpu.make_async_copy(halves.at[:, rows], near.at[:, rows], in_sems.at[i]) for i, rows in enumerate(pieces)]
    stores = [pltpu.make_async_copy(wide.at[rows], out_hbm.at[rows], out_sems.at[i]) for i, rows in enumerate(pieces)]
    for copy in loads + hand_on:
        copy.start()
    for i in range(steps):
        loads[i].wait()
        for tap in range(i * count, (i + 1) * count):
            for h in range(2):
                wide[tap, h * half : (h + 1) * half, :] = near[h, tap].astype(F32)
        stores[i].start()
    for copy in stores + hand_on:
        copy.wait()


def on_device(
    features, target, gn_gain, attn_query, attn_key, attn_value, attn_out, conv_weight, conv_bias,
    percept, lpips_weight, crop_owner, crop_frame, crop_col,
):
    tiles = lax.axis_size("tile")
    frames, rows_dev, cols, width = features.shape[1:]
    outputs = conv_weight.shape[-1]
    cells = frames * rows_dev * cols
    taps = 27
    half = width // 2
    part_rows = taps // 3 * half
    quarter = part_rows // 12
    crops = crop_col.shape[1]
    vmem = pl.BlockSpec(memory_space=pltpu.VMEM)
    hbm = pl.BlockSpec(memory_space=pl.ANY)
    sems = lambda count: pltpu.SemaphoreType.DMA((count,))
    decoded, summed, distances = pl.pallas_call(
        functools.partial(decoder_window, tiles, frames, cols),
        in_specs=[hbm] * 14,
        out_specs=[vmem, hbm, vmem],
        out_shape=[
            jax.ShapeDtypeStruct((cells, outputs), BF16),
            jax.ShapeDtypeStruct((2, 3, part_rows, outputs), BF16),
            jax.ShapeDtypeStruct((1, crops // tiles), F32),
        ],
        scratch_shapes=[
            pltpu.VMEM((9, width, 3 * outputs), BF16),
            pltpu.VMEM((width, width), BF16),
            pltpu.VMEM((width, width), BF16),
            pltpu.VMEM((width, width), BF16),
            pltpu.VMEM((width, width), BF16),
            pltpu.VMEM((outputs, outputs), BF16),
            pltpu.VMEM((cells, outputs), BF16),
            pltpu.VMEM((1, width), F32),
            pltpu.VMEM((1, outputs), F32),
            pltpu.VMEM((1, outputs), F32),
            pltpu.VMEM((1, crops), jnp.int32),
            pltpu.VMEM((1, crops), jnp.int32),
            pltpu.VMEM((1, crops), jnp.int32),
            pltpu.VMEM((tiles, cells, width), BF16),
            pltpu.VMEM((tiles * cells, width), BF16),
            pltpu.VMEM((tiles, 8, width), F32),
            pltpu.VMEM((3 * cells, width), BF16),
            pltpu.VMEM((3 * cells, width), F32),
            pltpu.VMEM((3 * cells, 128), F32),
            pltpu.VMEM((3 * cells, 128), F32),
            pltpu.VMEM((3, cells, width), BF16),
            pltpu.VMEM((3, width, cells), BF16),
            pltpu.VMEM((3, half, cells), BF16),
            pltpu.VMEM((cells, outputs), BF16),
            pltpu.VMEM((cells, outputs), BF16),
            pltpu.VMEM((3, 2 * cells, 3 * outputs), BF16),
            pltpu.VMEM((3, part_rows, outputs), BF16),
            pltpu.VMEM((9, quarter // 2, outputs), BF16),
            pltpu.VMEM((9, quarter // 2, outputs), BF16),
            pltpu.VMEM((9, 2, quarter // 2, outputs), BF16),
            pltpu.VMEM((9, 2, quarter, outputs), BF16),
            pltpu.VMEM((9, quarter, outputs), BF16),
            pltpu.VMEM((9, 3, quarter // 4, outputs), BF16),
            pltpu.VMEM((9, 4, quarter // 4, outputs), BF16),
            pltpu.VMEM((9, quarter, outputs), BF16),
            pltpu.VMEM((4, 8, crops), F32),
            pltpu.VMEM((2, 8, crops), F32),
            sems(14), sems(14), pltpu.SemaphoreType.DMA((9, 8)), sems(17),
        ],
        compiler_params=pltpu.CompilerParams(
            collective_id=1, has_side_effects=True, vmem_limit_bytes=60 * 1024 * 1024
        ),
        cost_estimate=pl.CostEstimate(flops=14_000_000_000, bytes_accessed=24_000_000, transcendentals=4_000_000),
        name="decoder_window",
    )(
        features.reshape(cells, width), target.reshape(cells, outputs), attn_query, attn_key, attn_value, attn_out,
        percept, conv_weight.reshape(9, 3, width, outputs), gn_gain[None, :], conv_bias[None, :], lpips_weight[None, :],
        crop_owner.reshape(1, -1), crop_frame, crop_col,
    )
    conv_total, decoded, distances = pl.pallas_call(
        widen,
        in_specs=[hbm] * 3,
        out_specs=[hbm] * 3,
        out_shape=[
            jax.ShapeDtypeStruct((taps, width, outputs), F32),
            jax.ShapeDtypeStruct(decoded.shape, BF16),
            jax.ShapeDtypeStruct(distances.shape, F32),
        ],
        scratch_shapes=[pltpu.VMEM((2, taps, half, outputs), BF16), pltpu.VMEM((taps, width, outputs), F32), sems(9), sems(9), sems(2)],
        compiler_params=pltpu.CompilerParams(vmem_limit_bytes=60 * 1024 * 1024),
        name="widen",
    )(summed.reshape(2, taps, half, outputs), decoded, distances)
    conv_total = conv_total.reshape(conv_weight.shape)
    return (decoded.reshape(1, frames, rows_dev, cols, outputs), conv_total, distances)


def solution(mesh):
    return jax.shard_map(
        on_device,
        mesh=mesh,
        in_specs=(
            P("clip", None, "tile", None, None),
            P("clip", None, "tile", None, None),
            P(), P(), P(), P(), P(), P(), P(), P(), P(),
            P("clip", None, None),
            P("clip", None),
            P("clip", None),
        ),
        out_specs=(P("clip", None, "tile", None, None), P(), P("clip", "tile")),
        check_vma=False,
    )
```
